256 devices in a mesh: grp: 32 (over z_lo, x, core), dp: 8 (over z_hi, y).
Axes of the slice: x: 4, y: 4, z: 8 (z_hi: 2, z_lo: 4; z = z_hi * 4 + z_lo), core: 2. Of those that a mesh axis runs over, the one named last changes fastest.
Arguments:
- projection_rows: bfloat16 [8, 4096, 6144], P('dp', 'grp'), may hold values from -7 to 7
- normed_input_rows: bfloat16 [8, 4096, 4096], P('dp', 'grp'), may hold values from -6 to 6
- adapter_down: bfloat16 [4096, 16], replicated, may hold values from -0.09375 to 0.09375
- adapter_up: bfloat16 [16, 4096], replicated, may hold values from -1.5 to 1.5
- lengths: int32 [8, 5], P('dp'), may hold values from 128 to 2048, as said below
- groups: int32 [8, 5], P('dp'), may hold values from 2 to 16, as said below
- output_gradient: bfloat16 [8, 4096, 4096], P('dp', 'grp'), may hold values from -6 to 6
Outputs:
- attn_out: bfloat16 [8, 4096, 4096], P('dp', 'grp')
- grad_qkv: bfloat16 [8, 4096, 6144], P('dp', 'grp')
- grad_lora_a: float32 [4096, 16], replicated
- grad_lora_b: float32 [16, 4096], replicated
The draws below stay inside these ranges and needn't reach their ends.
Inputs may be any that keep to these rules, and one draw needn't show every extreme that they name: `groups`: each replica's 5 group widths are powers of two that add up to 32; each group starts at a multiple of its own width, and exactly one group of each replica has 16 devices. `lengths`: sequence j has at most 128 * groups[j] rows and at least half as many; the sequence in a replica's widest group has exactly 2048 rows.
All inputs are finite; a program needn't handle non-finite values.
Results may differ from the reference program's by a relative error of at most 0.012.
The reference program's roundings to bfloat16 on the way count: a program that leaves them out, or rounds other values in their place, can miss the bound.
Values may be sent and summed in bfloat16 or wider, within the bound.
No kernel may reach another device: no remote copies, remote signals or barrier semaphores. Data moves between devices by JAX's collectives and lax.ppermute only.
A program may use at most 192 MiB of HBM per device.

```python
import math
import jax
import jax.numpy as jnp
from jax import lax

MODEL_WIDTH = 4096
HEADS = 32
KV_HEADS = 8
HEAD_DIM = 128
ADAPTER_RANK = 16
NSEQ = 5
TOK_DEV = 128
TOKG = 4096
REPLICAS = 8
QUERY_COLUMNS = 4096
QKV = 6144
N_GRP = 32


def plan_rows(key):
    key = jax.random.fold_in(key, 101)
    order_key, length_key = jax.random.split(key)
    unit_width = TOKG // TOK_DEV // 16
    table = jnp.array([[8, 2, 2, 2, 2], [2, 2, 2, 2, 8], [1, 1, 2, 4, 8], [8, 4, 2, 1, 1]], jnp.int32) * unit_width
    picked = jax.random.randint(order_key, (REPLICAS,), 0, 4)
    widths = jnp.take(table, picked, axis=0)
    capacity = widths * TOK_DEV
    drawn = jax.random.randint(length_key, (REPLICAS, NSEQ), 0, 1 << 20)
    spread = capacity - capacity // 2 + 1
    chosen_lengths = capacity // 2 + drawn % spread
    chosen_lengths = jnp.where(widths == 8 * unit_width, capacity, chosen_lengths)
    return (widths.astype(jnp.int32), chosen_lengths.astype(jnp.int32))


def draw_groups(key, part):
    widths, chosen_lengths = plan_rows(key)
    return widths


def draw_lengths(key, part):
    widths, chosen_lengths = plan_rows(key)
    return chosen_lengths


def draw_projection_rows(key, part):
    key = jax.random.fold_in(key, 11)
    base_key = jax.random.fold_in(key, 0)
    full_shape = (REPLICAS, TOKG, QKV)
    result = jax.random.truncated_normal(base_key, -4.0, 4.0, full_shape, jnp.float32)
    return result.astype(jnp.bfloat16)


def levels(rng, shape, cuts, least, largest):
    loudness, own = 1.0, jax.random.fold_in(rng, 6)
    for dim, blocks in cuts:
        draws = jnp.exp(jax.random.uniform(jax.random.fold_in(own, dim), (blocks,), jnp.float32, least / len(cuts), largest / len(cuts)))
        loudness = loudness * jnp.repeat(draws, shape[dim] // blocks).reshape([-1 if axis == dim else 1 for axis in range(len(shape))])
    return loudness


def noise(stream_key, extent, deviation, reach, pieces=(), held_as=jnp.bfloat16):
    values = deviation * jax.random.normal(stream_key, extent, jnp.float32)
    if pieces:
        values = values * levels(stream_key, extent, pieces, -0.22, 0.18)
    return jnp.clip(values, -reach, reach).astype(held_as)


def setup_inputs(seed: int = 0) -> dict:
    keys = jax.random.split(jax.random.key(seed), 8)
    projection_rows = draw_projection_rows(jax.random.fold_in(keys[7], 71), 0)
    normed_input_rows = noise(keys[1], (REPLICAS, TOKG, MODEL_WIDTH), 1.0, 6.0, ((0, 8), (1, 32)))
    adapter_down = noise(keys[2], (MODEL_WIDTH, ADAPTER_RANK), MODEL_WIDTH ** -0.5, 0.09375)
    adapter_up = noise(keys[3], (ADAPTER_RANK, QUERY_COLUMNS), ADAPTER_RANK ** -0.5, 1.5)
    lengths = draw_lengths(jax.random.fold_in(keys[7], 71), 0)
    groups = draw_groups(jax.random.fold_in(keys[7], 71), 0)
    output_gradient = noise(keys[6], (REPLICAS, TOKG, QUERY_COLUMNS), 1.0, 6.0, ((0, 8), (1, 32)))
    return dict(projection_rows=projection_rows, normed_input_rows=normed_input_rows, adapter_down=adapter_down, adapter_up=adapter_up, lengths=lengths, groups=groups, output_gradient=output_gradient)


rope_base = 500000.0

def rope_tables(offsets, half_dim):
    index_float = jnp.arange(half_dim, dtype=jnp.float32)
    inverse = jnp.power(jnp.float32(rope_base), -index_float / half_dim)
    angles = offsets.astype(jnp.float32)[:, None] * inverse[None, :]
    return (jnp.cos(angles), jnp.sin(angles))

def rotate(table, cosine, sine, direction):
    count, width = table.shape
    half_dim = cosine.shape[1]
    split_view = table.reshape(count, width // (2 * half_dim), 2, half_dim)
    first_half = split_view[:, :, 0]
    second_half = split_view[:, :, 1]
    cos_view = cosine[:, None, :]
    sin_view = direction * sine[:, None, :]
    rotated = jnp.stack([first_half * cos_view - second_half * sin_view, second_half * cos_view + first_half * sin_view], axis=2)
    return rotated.reshape(count, width)

def layout(width_row, length_row, count):
    token_at = jnp.arange(count, dtype=jnp.int32)
    rows_of = (width_row * TOK_DEV).astype(jnp.int32)
    ends_at = jnp.cumsum(rows_of).astype(jnp.int32)
    passed = token_at[:, None] >= ends_at[None, :]
    start_at = lax.optimization_barrier(jnp.sum(jnp.where(passed, rows_of[None, :], 0), axis=1)).astype(jnp.int32)
    segment = lax.optimization_barrier(jnp.sum(passed.astype(jnp.int32), axis=1)).astype(jnp.int32)
    seq_index = jnp.arange(length_row.shape[0], dtype=jnp.int32)
    length_at = lax.optimization_barrier(jnp.sum(jnp.where(segment[:, None] == seq_index[None, :], length_row[None, :], 0), axis=1)).astype(jnp.int32)
    offsets = token_at - start_at
    return (offsets, segment, offsets < length_at)

def attention_head(queries, key_rows, value_rows, cotangent, segment, valid):
    count, head_width = queries.shape
    factor = 1.0 / math.sqrt(head_width)
    block_rows = count // 8
    grad_keys = jnp.zeros((count, head_width), jnp.float32)
    grad_values = jnp.zeros((count, head_width), jnp.float32)
    outputs = []
    grad_queries = []
    for block in range(8):
        start_row = block * block_rows
        stop_row = start_row + block_rows
        query_block = queries[start_row:stop_row]
        visible_keys = key_rows[:stop_row]
        visible_values = value_rows[:stop_row]
        scores = jnp.dot(query_block, visible_keys.T, preferred_element_type=jnp.float32) * factor
        query_at = jnp.arange(start_row, stop_row)
        key_at = jnp.arange(stop_row)
        same_row = key_at[None, :] == query_at[:, None]
        allowed = (key_at[None, :] <= query_at[:, None]) & (segment[start_row:stop_row, None] == segment[None, :stop_row]) & (valid[None, :stop_row] | same_row)
        scores = jnp.where(allowed, scores, -jnp.inf)
        row_max = lax.optimization_barrier(jnp.max(scores, axis=1, keepdims=True))
        numer = jnp.exp(scores - row_max)
        probs = numer / lax.optimization_barrier(jnp.sum(numer, axis=1, keepdims=True))
        probs_half = probs.astype(jnp.bfloat16)
        out_block = jnp.dot(probs_half, visible_values, preferred_element_type=jnp.float32).astype(jnp.bfloat16)
        grad_block = cotangent[start_row:stop_row]
        row_delta = lax.optimization_barrier(jnp.sum(grad_block.astype(jnp.float32) * out_block.astype(jnp.float32), axis=1, keepdims=True))
        grad_probs = jnp.dot(grad_block, visible_values.T, preferred_element_type=jnp.float32)
        grad_scores = (probs * (grad_probs - row_delta)).astype(jnp.bfloat16)
        grad_queries.append((jnp.dot(grad_scores, visible_keys, preferred_element_type=jnp.float32) * factor).astype(jnp.bfloat16))
        grad_keys = grad_keys.at[:stop_row].add(jnp.dot(grad_scores.T, query_block, preferred_element_type=jnp.float32) * factor)
        grad_values = grad_values.at[:stop_row].add(jnp.dot(probs_half.T, grad_block, preferred_element_type=jnp.float32))
        outputs.append(out_block)
    return (jnp.concatenate(outputs, axis=0), jnp.concatenate(grad_queries, axis=0), grad_keys.astype(jnp.bfloat16), grad_values.astype(jnp.bfloat16))

def relayout(arrived):
    width = arrived.shape[-1]
    split_view = arrived.reshape(REPLICAS, N_GRP, REPLICAS, TOK_DEV // REPLICAS, width)
    return split_view.transpose(2, 1, 0, 3, 4).reshape(REPLICAS, TOKG, width)

def reference(projection_rows, normed_input_rows, adapter_down, adapter_up, lengths, groups, output_gradient):
    qkv_all = relayout(projection_rows)
    x_all = relayout(normed_input_rows)
    query_column_count = HEADS * HEAD_DIM
    kv_width = KV_HEADS * HEAD_DIM
    share = HEADS // KV_HEADS

    def heads_first(table, count):
        return table.reshape(TOKG, count, HEAD_DIM).transpose(1, 0, 2)

    def tokens_first(table):
        return table.transpose(1, 0, 2).reshape(TOKG, -1)

    def group_sum(table):
        return table.astype(jnp.float32).reshape(KV_HEADS, share, TOKG, HEAD_DIM).sum(axis=1)

    def one_replica(inputs):
        replicated_projections, replicated_inputs, length_row, width_row, grad_raw = inputs
        offsets, segment, valid = layout(width_row, length_row, TOKG)
        grad_rep = jnp.where(valid[:, None], grad_raw, jnp.zeros_like(grad_raw))
        cosine, sine = rope_tables(offsets, HEAD_DIM // 2)
        reduced_input = jnp.dot(replicated_inputs, adapter_down, preferred_element_type=jnp.float32).astype(jnp.bfloat16)
        frozen_query = replicated_projections[:, :query_column_count].astype(jnp.float32) + jnp.dot(reduced_input, adapter_up, preferred_element_type=jnp.float32)
        queries = rotate(frozen_query, cosine, sine, 1.0).astype(jnp.bfloat16)
        key_rows = rotate(replicated_projections[:, query_column_count:query_column_count + kv_width].astype(jnp.float32), cosine, sine, 1.0).astype(jnp.bfloat16)
        value_rows = replicated_projections[:, query_column_count + kv_width:]
        query_heads = heads_first(queries, HEADS)
        key_heads = jnp.repeat(heads_first(key_rows, KV_HEADS), share, axis=0)
        value_heads = jnp.repeat(heads_first(value_rows, KV_HEADS), share, axis=0)
        grad_heads = heads_first(grad_rep, HEADS)

        def per_head(items):
            return attention_head(items[0], items[1], items[2], items[3], segment, valid)
        out_heads, query_grads, key_grads, value_grads = lax.map(per_head, (query_heads, key_heads, value_heads, grad_heads))
        query_gradient = rotate(tokens_first(query_grads).astype(jnp.float32), cosine, sine, -1.0).astype(jnp.bfloat16)
        grad_key = rotate(tokens_first(group_sum(key_grads)), cosine, sine, -1.0).astype(jnp.bfloat16)
        grad_value = tokens_first(group_sum(value_grads)).astype(jnp.bfloat16)
        grad_rows = jnp.concatenate([query_gradient, grad_key, grad_value], axis=1)
        term_b = jnp.dot(reduced_input.T, query_gradient, preferred_element_type=jnp.float32)
        reduced_gradient = jnp.dot(query_gradient, adapter_up.T, preferred_element_type=jnp.float32).astype(jnp.bfloat16)
        term_a = jnp.dot(replicated_inputs.T, reduced_gradient, preferred_element_type=jnp.float32)
        return (tokens_first(out_heads), grad_rows, term_a, term_b)
    attn_out, grad_qkv, terms_a, terms_b = lax.map(one_replica, (qkv_all, x_all, lengths, groups, output_gradient))
    return (attn_out, grad_qkv, lax.optimization_barrier(jnp.sum(terms_a, axis=0)), lax.optimization_barrier(jnp.sum(terms_b, axis=0)))
```

```python
import math

import jax
import jax.numpy as jnp
from jax import lax
from jax.experimental import pallas as pl
from jax.experimental.pallas import tpu as pltpu
from jax.sharding import Mesh
from jax.sharding import PartitionSpec as P

HEAD_DIM = 128
HALF_DIM = HEAD_DIM // 2
BLOCK = 256
PAIR = 2 * HEAD_DIM
PIECE = 2 * PAIR + 2 * HEAD_DIM
rope_base = 500000.0
VMEM_BYTES = 48 * 1024 * 1024
F32 = jnp.float32
BF16 = jnp.bfloat16


def rope_tables(offsets):
    index_float = jnp.arange(HALF_DIM, dtype=F32)
    inverse = jnp.power(F32(rope_base), -index_float / HALF_DIM)
    angles = offsets.astype(F32)[:, None] * inverse[None, :]
    cosine, sine = jnp.cos(angles), jnp.sin(angles)
    return jnp.concatenate([cosine, cosine], axis=1), jnp.concatenate([-sine, sine], axis=1)


def rotated(table, cosine, sine):
    return table * cosine + pltpu.roll(table, HALF_DIM, 1) * sine


def prepare_kernel(qkv_ref, low_ref, up_ref, cos_ref, sin_ref, grad_ref, valid_ref, out_ref):
    cosine = cos_ref[...]
    sine = sin_ref[...]
    low = low_ref[...]
    kept = valid_ref[...] > 0
    queries = up_ref.shape[1]
    kv_width = (qkv_ref.shape[1] - queries) // 2
    pieces = out_ref.shape[0]
    for piece in range(pieces):
        columns = slice(piece * PAIR, (piece + 1) * PAIR)
        full = qkv_ref[:, columns].astype(F32) + jnp.dot(
            low, up_ref[:, columns], preferred_element_type=F32
        )
        for head in range(2):
            at = slice(head * HEAD_DIM, (head + 1) * HEAD_DIM)
            out_ref[piece, :, at] = rotated(full[:, at], cosine, sine).astype(BF16)
        grad = grad_ref[:, columns]
        out_ref[piece, :, PAIR : 2 * PAIR] = jnp.where(kept, grad, jnp.zeros_like(grad))
    for key_head in range(kv_width // HEAD_DIM):
        at = queries + key_head * HEAD_DIM
        keys = rotated(qkv_ref[:, at : at + HEAD_DIM].astype(F32), cosine, sine).astype(BF16)
        values = qkv_ref[:, at + kv_width : at + kv_width + HEAD_DIM]
        for piece in (2 * key_head, 2 * key_head + 1):
            out_ref[piece, :, 2 * PAIR : 2 * PAIR + HEAD_DIM] = keys
            out_ref[piece, :, 2 * PAIR + HEAD_DIM :] = values


def attention_kernel(start_ref, end_ref, x_ref, out_ref, kt, vt, dkt, dvt, numer, probs):
    step = pl.program_id(0)
    blocks = pl.num_programs(0)
    factor = 1.0 / math.sqrt(HEAD_DIM)
    exponent = factor * math.log2(math.e)
    key_at = 2 * PAIR
    value_at = 2 * PAIR + HEAD_DIM

    @pl.when(step == 0)
    def _():
        for block in range(x_ref.shape[0] // BLOCK):
            rows = slice(block * BLOCK, (block + 1) * BLOCK)
            kt[block] = x_ref[rows, key_at:value_at].T
            vt[block] = x_ref[rows, value_at:].T
        dkt[...] = jnp.zeros_like(dkt)
        dvt[...] = jnp.zeros_like(dvt)

    first = start_ref[step]
    last_row = end_ref[step]
    own = pl.ds(pl.multiple_of(step * BLOCK, BLOCK), BLOCK)
    column = lax.broadcasted_iota(jnp.int32, (1, BLOCK), 1)
    row = lax.broadcasted_iota(jnp.int32, (BLOCK, 1), 0)
    queries = [x_ref[own, h * HEAD_DIM : (h + 1) * HEAD_DIM] for h in range(2)]
    grads = [x_ref[own, PAIR + h * HEAD_DIM : PAIR + (h + 1) * HEAD_DIM] for h in range(2)]

    def halves(op, table):
        return op(table[:, :HEAD_DIM], table[:, HEAD_DIM:])

    def key_rows(block):
        return pl.ds(pl.multiple_of(block * BLOCK, BLOCK), BLOCK)

    diagonal = (column == row) | ((column < row) & (step * BLOCK + column < last_row))
    tops = []
    for h in range(2):
        scores = jnp.dot(queries[h], kt[step], preferred_element_type=F32)
        scores = jnp.where(diagonal, scores, -jnp.inf)
        numer[h, step] = scores
        tops.append(halves(jnp.maximum, scores))

    def score_pass(block, carry):
        bias = jnp.where(block * BLOCK + column < last_row, F32(0.0), F32(-jnp.inf))
        result = []
        for h in range(2):
            scores = jnp.dot(queries[h], kt[block], preferred_element_type=F32) + bias
            numer[h, block] = scores
            result.append(jnp.maximum(carry[h], halves(jnp.maximum, scores)))
        return tuple(result)

    tops = lax.fori_loop(first, step, score_pass, tuple(tops))
    tops = [jnp.max(top, axis=1, keepdims=True) for top in tops]

    def exp_pass(block, carry):
        result = []
        for h in range(2):
            powers = jnp.exp2((numer[h, block] - tops[h]) * exponent)
            numer[h, block] = powers
            result.append(carry[h] + halves(jnp.add, powers))
        return tuple(result)

    empty = jnp.zeros((BLOCK, HEAD_DIM), F32)
    totals = lax.fori_loop(first, step + 1, exp_pass, (empty, empty))
    inverse = [1.0 / jnp.sum(total, axis=1, keepdims=True) for total in totals]

    def out_pass(block, carry):
        values = x_ref[key_rows(block), value_at:]
        result = []
        for h in range(2):
            held = numer[h, block] * inverse[h]
            numer[h, block] = held
            rounded = held.astype(BF16)
            probs[h, block] = rounded
            result.append(carry[h] + jnp.dot(rounded, values, preferred_element_type=F32))
        return tuple(result)

    outs = lax.fori_loop(first, step + 1, out_pass, (empty, empty))
    outs = [out.astype(BF16) for out in outs]
    deltas = [
        jnp.sum(grads[h].astype(F32) * outs[h].astype(F32), axis=1, keepdims=True) for h in range(2)
    ]
    queries_t = [table.T for table in queries]
    grads_t = [table.T for table in grads]

    def gradient_pass(block, carry):
        keys = x_ref[key_rows(block), key_at:value_at]
        result = []
        key_part = dkt[block]
        value_part = dvt[block]
        for h in range(2):
            grad_probs = jnp.dot(grads[h], vt[block], preferred_element_type=F32)
            grad_scores = (numer[h, block] * (grad_probs - deltas[h])).astype(BF16)
            result.append(carry[h] + jnp.dot(grad_scores, keys, preferred_element_type=F32))
            key_part += jnp.dot(queries_t[h], grad_scores, preferred_element_type=F32)
            value_part += jnp.dot(grads_t[h], probs[h, block], preferred_element_type=F32)
        dkt[block] = key_part
        dvt[block] = value_part
        return tuple(result)

    query_sums = lax.fori_loop(first, step + 1, gradient_pass, (empty, empty))
    for h in range(2):
        at = h * HEAD_DIM
        out_ref[own, at : at + HEAD_DIM] = outs[h]
        out_ref[own, PAIR + at : PAIR + at + HEAD_DIM] = (query_sums[h] * factor).astype(BF16)

    @pl.when(step == blocks - 1)
    def _():
        for block in range(x_ref.shape[0] // BLOCK):
            rows = slice(block * BLOCK, (block + 1) * BLOCK)
            out_ref[rows, key_at:value_at] = (dkt[block] * factor).T.astype(BF16)
            out_ref[rows, value_at:] = dvt[block].T.astype(BF16)


def attention(table, starts, ends):
    rows, width = table.shape
    blocks = rows // BLOCK
    tiles = blocks * (blocks + 1) // 2
    return pl.pallas_call(
        attention_kernel,
        out_shape=jax.ShapeDtypeStruct((rows, width), BF16),
        grid_spec=pltpu.PrefetchScalarGridSpec(
            num_scalar_prefetch=2,
            grid=(blocks,),
            in_specs=[pl.BlockSpec((rows, width), lambda i, *_: (0, 0))],
            out_specs=pl.BlockSpec((rows, width), lambda i, *_: (0, 0)),
            scratch_shapes=[
                pltpu.VMEM((blocks, HEAD_DIM, BLOCK), BF16),
                pltpu.VMEM((blocks, HEAD_DIM, BLOCK), BF16),
                pltpu.VMEM((blocks, HEAD_DIM, BLOCK), F32),
                pltpu.VMEM((blocks, HEAD_DIM, BLOCK), F32),
                pltpu.VMEM((2, blocks, BLOCK, BLOCK), F32),
                pltpu.VMEM((2, blocks, BLOCK, BLOCK), BF16),
            ],
        ),
        compiler_params=pltpu.CompilerParams(vmem_limit_bytes=VMEM_BYTES),
        cost_estimate=pl.CostEstimate(
            flops=tiles * 2 * 6 * 2 * BLOCK * BLOCK * HEAD_DIM,
            bytes_accessed=4 * rows * width,
            transcendentals=tiles * 2 * BLOCK * BLOCK,
        ),
    )(starts, ends, table)


def finish_kernel(came_ref, low_ref, up_ref, cos_ref, sin_ref, out_ref, grad_ref, dlow_ref, term_ref):
    cosine = cos_ref[...]
    sine = -sin_ref[...]
    low_t = low_ref[...].astype(F32).T.astype(BF16)
    queries = up_ref.shape[1]
    kv_width = (grad_ref.shape[1] - queries) // 2
    dlow = jnp.zeros(dlow_ref.shape, F32)
    for piece in range(came_ref.shape[0]):
        columns = slice(piece * PAIR, (piece + 1) * PAIR)
        out_ref[:, columns] = came_ref[piece, :, :PAIR]
        for head in range(2):
            at = PAIR + head * HEAD_DIM
            to = piece * PAIR + head * HEAD_DIM
            grad_ref[:, to : to + HEAD_DIM] = rotated(
                came_ref[piece, :, at : at + HEAD_DIM].astype(F32), cosine, sine
            ).astype(BF16)
        part = grad_ref[:, columns]
        dlow += lax.dot_general(
            part, up_ref[:, columns], (((1,), (1,)), ((), ())), preferred_element_type=F32
        )
        term_ref[:, columns] = jnp.dot(low_t, part, preferred_element_type=F32)
    dlow_ref[...] = dlow.astype(BF16)
    for key_head in range(kv_width // HEAD_DIM):
        pair = (2 * key_head, 2 * key_head + 1)
        keys, values = (
            sum(came_ref[piece, :, at : at + HEAD_DIM].astype(F32) for piece in pair)
            for at in (2 * PAIR, 2 * PAIR + HEAD_DIM)
        )
        at = queries + key_head * HEAD_DIM
        grad_ref[:, at : at + HEAD_DIM] = rotated(keys, cosine, sine).astype(BF16)
        grad_ref[:, at + kv_width : at + kv_width + HEAD_DIM] = values.astype(BF16)


def exchange(table, axis):
    return lax.all_to_all(table, axis, split_axis=0, concat_axis=0, tiled=True)


def local(
    projection_rows, normed_input_rows, adapter_down, adapter_up, lengths, groups, output_gradient
):
    qkv_local = projection_rows[0]
    x_local = normed_input_rows[0]
    grad_raw = output_gradient[0]
    length_row = lengths[0]
    width_row = groups[0]
    token_count, model_width = x_local.shape
    qkv_width = qkv_local.shape[1]
    rank, query_columns = adapter_up.shape
    members = lax.axis_size("sub")
    half_index = lax.axis_index("half")
    group_index = half_index * members + lax.axis_index("sub")
    low_local = jnp.dot(x_local, adapter_down, preferred_element_type=F32).astype(BF16)
    packed_low = exchange(low_local, "dp")
    packed_qkv = exchange(qkv_local, "dp")

    ends_dev = jnp.cumsum(width_row)
    starts_dev = ends_dev - width_row

    def owner_of(device):
        picked = (device[:, None] >= starts_dev[None, :]) & (device[:, None] < ends_dev[None, :])
        start = jnp.sum(jnp.where(picked, starts_dev[None, :], 0), axis=1)
        length = jnp.sum(jnp.where(picked, length_row[None, :], 0), axis=1)
        return start, length

    start_me, length_me = owner_of(group_index[None])
    row_at = jnp.arange(token_count, dtype=jnp.int32)
    local_offsets = (group_index - start_me) * token_count + row_at
    row_valid = (local_offsets < length_me).astype(jnp.int32)[:, None]
    cosine, sine = rope_tables(local_offsets)
    per_block = BLOCK // token_count
    block_device = half_index * members + per_block * jnp.arange(
        members // per_block, dtype=jnp.int32
    )
    block_start, block_length = owner_of(block_device)
    first_rows = (block_start - half_index * members) * token_count
    starts = first_rows // BLOCK
    ends = first_rows + block_length

    params = pltpu.CompilerParams(vmem_limit_bytes=VMEM_BYTES)
    pieces = pl.pallas_call(
        prepare_kernel,
        out_shape=jax.ShapeDtypeStruct((members, token_count, PIECE), BF16),
        compiler_params=params,
    )(packed_qkv, packed_low, adapter_up, cosine, sine, grad_raw, row_valid)
    table = exchange(pieces, "sub").reshape(members * token_count, PIECE)
    results = attention(table, starts, ends)
    came = exchange(results.reshape(members, token_count, PIECE), "sub")
    attn_rows, grad_rows, reduced_gradient, term_b = pl.pallas_call(
        finish_kernel,
        out_shape=(
            jax.ShapeDtypeStruct((token_count, query_columns), BF16),
            jax.ShapeDtypeStruct((token_count, qkv_width), BF16),
            jax.ShapeDtypeStruct((token_count, rank), BF16),
            jax.ShapeDtypeStruct((rank, query_columns), F32),
        ),
        compiler_params=params,
    )(came, packed_low, adapter_up, cosine, sine)
    gradient_local = exchange(reduced_gradient, "dp")
    term_a = lax.dot_general(
        gradient_local, x_local, (((0,), (0,)), ((), ())), preferred_element_type=F32
    )
    terms = jnp.concatenate([term_a, term_b], axis=0)
    parts = exchange(terms, ("half", "sub"))
    total = jnp.sum(parts, axis=0).reshape(-1, 128)
    replicas = lax.axis_size("dp")
    apart = 1
    while apart < replicas:
        total = total + lax.ppermute(total, "dp", [(i, i ^ apart) for i in range(replicas)])
        apart *= 2
    whole = exchange(jnp.broadcast_to(total.reshape(1, -1), terms.shape), ("half", "sub"))
    return (attn_rows[None], grad_rows[None], whole[:rank].T, whole[rank:])


def solution(mesh):
    members, replicas = mesh.devices.shape
    split = Mesh(mesh.devices.reshape(2, members // 2, replicas), ("half", "sub", "dp"))
    rows = P("dp", ("half", "sub"), None)
    placed = (rows, rows, P(), P(), P("dp", None), P("dp", None), rows)
    return jax.shard_map(
        local,
        mesh=split,
        in_specs=placed,
        out_specs=(rows, rows, P(), P()),
        check_vma=False,
    )
```

```python
import math

import jax
import jax.numpy as jnp
from jax import lax
from jax.experimental import pallas as pl
from jax.experimental.pallas import tpu as pltpu
from jax.sharding import Mesh
from jax.sharding import PartitionSpec as P

HEAD_DIM = 128
HALF_DIM = HEAD_DIM // 2
PART = 256
BLOCK = 512
PAIR = 2 * HEAD_DIM
PIECE = 2 * PAIR + 2 * HEAD_DIM
rope_base = 500000.0
VMEM_BYTES = 48 * 1024 * 1024
HIDDEN = -1e30
F32 = jnp.float32
BF16 = jnp.bfloat16


def rope_tables(offsets):
    index_float = jnp.arange(HALF_DIM, dtype=F32)
    inverse = jnp.power(F32(rope_base), -index_float / HALF_DIM)
    angles = offsets.astype(F32)[:, None] * inverse[None, :]
    cosine, sine = jnp.cos(angles), jnp.sin(angles)
    return jnp.concatenate([cosine, cosine], axis=1), jnp.concatenate([-sine, sine], axis=1)


def rotated(table, cosine, sine):
    return table * cosine + pltpu.roll(table, HALF_DIM, 1) * sine


def prepare_kernel(qkv_ref, up_ref, cos_ref, sin_ref, grad_ref, valid_ref, out_ref):
    cosine = cos_ref[...]
    sine = sin_ref[...]
    kept = valid_ref[...] > 0
    rank, queries = up_ref.shape
    kv_width = (qkv_ref.shape[1] - HEAD_DIM - queries) // 2
    low_at = queries + 2 * kv_width
    low = qkv_ref[:, low_at : low_at + rank]
    pieces = out_ref.shape[0]
    for piece in range(pieces):
        columns = slice(piece * PAIR, (piece + 1) * PAIR)
        full = qkv_ref[:, columns].astype(F32) + jnp.dot(
            low, up_ref[:, columns], preferred_element_type=F32
        )
        for head in range(2):
            at = slice(head * HEAD_DIM, (head + 1) * HEAD_DIM)
            out_ref[piece, :, at] = rotated(full[:, at], cosine, sine).astype(BF16)
        grad = grad_ref[:, columns]
        out_ref[piece, :, PAIR : 2 * PAIR] = jnp.where(kept, grad, jnp.zeros_like(grad))
    for key_head in range(kv_width // HEAD_DIM):
        at = queries + key_head * HEAD_DIM
        keys = rotated(qkv_ref[:, at : at + HEAD_DIM].astype(F32), cosine, sine).astype(BF16)
        values = qkv_ref[:, at + kv_width : at + kv_width + HEAD_DIM]
        for piece in (2 * key_head, 2 * key_head + 1):
            out_ref[piece, :, 2 * PAIR : 2 * PAIR + HEAD_DIM] = keys
            out_ref[piece, :, 2 * PAIR + HEAD_DIM :] = values


def attention_kernel(start_ref, end_ref, x_ref, out_ref, kt, vt, dkt, dvt, store0, store1):
    store = (store0, store1)
    step = pl.program_id(0)
    blocks = pl.num_programs(0)
    factor = 1.0 / math.sqrt(HEAD_DIM)
    exponent = factor * math.log2(math.e)
    key_at = 2 * PAIR
    value_at = 2 * PAIR + HEAD_DIM
    tiles = x_ref.shape[0] // BLOCK
    per = BLOCK // PART

    @pl.when(step == 0)
    def _():
        for tile in range(tiles):
            rows = slice(tile * BLOCK, (tile + 1) * BLOCK)
            kt[tile] = x_ref[rows, key_at:value_at].T
            vt[tile] = x_ref[rows, value_at:].T
        dkt[...] = jnp.zeros_like(dkt)
        dvt[...] = jnp.zeros_like(dvt)

    own = pl.ds(pl.multiple_of(step * BLOCK, BLOCK), BLOCK)
    first = start_ref[step * per] // BLOCK
    last = step
    end_row = end_ref[step * per]
    column = lax.broadcasted_iota(jnp.int32, (1, BLOCK), 1)
    row = lax.broadcasted_iota(jnp.int32, (BLOCK, 1), 0)
    low_row = jnp.full((BLOCK, 1), start_ref[step * per] - last * BLOCK, jnp.int32)
    high_row = jnp.full((BLOCK, 1), end_row - last * BLOCK, jnp.int32)
    for part in range(1, per):
        inside = row >= part * PART
        low_row = jnp.where(inside, start_ref[step * per + part] - last * BLOCK, low_row)
        high_row = jnp.where(inside, end_ref[step * per + part] - last * BLOCK, high_row)
    queries = [x_ref[own, h * HEAD_DIM : (h + 1) * HEAD_DIM] for h in range(2)]
    grads = [x_ref[own, PAIR + h * HEAD_DIM : PAIR + (h + 1) * HEAD_DIM] for h in range(2)]

    def folded(op, table):
        parts = [table[:, c : c + HEAD_DIM] for c in range(0, BLOCK, HEAD_DIM)]
        while len(parts) > 1:
            parts = [op(a, b) for a, b in zip(parts[::2], parts[1::2])]
        return parts[0]

    def spread(table):
        return jnp.concatenate([table] * (BLOCK // HEAD_DIM), axis=1)

    def key_rows(tile):
        return pl.ds(pl.multiple_of(tile * BLOCK, BLOCK), BLOCK)

    diagonal = (column == row) | ((column < row) & (column >= low_row) & (column < high_row))
    carry = []
    for h in range(2):
        scores = jnp.dot(queries[h], kt[last], preferred_element_type=F32) * exponent
        scores = jnp.where(diagonal, scores, HIDDEN)
        store[h][last] = scores
        top = folded(jnp.maximum, scores)
        carry += [top, folded(jnp.add, jnp.exp2(scores - spread(top)))]

    def score_pass(tile, carry):
        bias = jnp.where(tile * BLOCK + column < end_row, F32(0.0), F32(HIDDEN))
        result = []
        for h in range(2):
            top, total = carry[2 * h], carry[2 * h + 1]
            scores = jnp.dot(queries[h], kt[tile], preferred_element_type=F32) * exponent + bias
            store[h][tile] = scores
            higher = jnp.maximum(top, folded(jnp.maximum, scores))
            total = total * jnp.exp2(top - higher) + folded(
                jnp.add, jnp.exp2(scores - spread(higher))
            )
            result += [higher, total]
        return tuple(result)

    carry = lax.fori_loop(first, last, score_pass, tuple(carry))
    tops, inverse = [], []
    for h in range(2):
        lane_top, lane_total = carry[2 * h], carry[2 * h + 1]
        top = jnp.max(lane_top, axis=1, keepdims=True)
        total = jnp.sum(lane_total * jnp.exp2(lane_top - top), axis=1, keepdims=True)
        tops.append(top)
        inverse.append(1.0 / total)

    empty = jnp.zeros((BLOCK, HEAD_DIM), F32)

    def probs_of(h, tile):
        return jnp.exp2(store[h][tile] - tops[h]) * inverse[h]

    def out_part(h, tile, total):
        values = x_ref[key_rows(tile), value_at:]
        return total + jnp.dot(
            probs_of(h, tile).astype(BF16), values, preferred_element_type=F32
        )

    outs = [None, None]
    deltas = [None, None]
    queries_t = [table.T for table in queries]
    grads_t = [table.T for table in grads]

    def settle(h, total):
        outs[h] = total.astype(BF16)
        deltas[h] = jnp.sum(
            grads[h].astype(F32) * outs[h].astype(F32), axis=1, keepdims=True
        )

    def grad_part(h, tile, total):
        keys = x_ref[key_rows(tile), key_at:value_at]
        grad_probs = jnp.dot(grads[h], vt[tile], preferred_element_type=F32)
        probs = probs_of(h, tile)
        grad_scores = (probs * (grad_probs - deltas[h])).astype(BF16)
        total = total + jnp.dot(grad_scores, keys, preferred_element_type=F32)
        dkt[tile] += jnp.dot(queries_t[h], grad_scores, preferred_element_type=F32)
        dvt[tile] += jnp.dot(grads_t[h], probs.astype(BF16), preferred_element_type=F32)
        return total

    def out_pass(tile, carry):
        return tuple(out_part(h, tile, carry[h]) for h in range(2))

    def gradient_pass(tile, carry):
        return tuple(grad_part(h, tile, carry[h]) for h in range(2))

    sums = lax.fori_loop(first, last + 1, out_pass, (empty, empty))
    for h in range(2):
        settle(h, sums[h])
    query_sums = lax.fori_loop(first, last + 1, gradient_pass, (empty, empty))
    for h in range(2):
        at = h * HEAD_DIM
        out_ref[own, at : at + HEAD_DIM] = outs[h]
        out_ref[own, PAIR + at : PAIR + at + HEAD_DIM] = (query_sums[h] * factor).astype(BF16)

    @pl.when(step == blocks - 1)
    def _():
        for tile in range(tiles):
            rows = slice(tile * BLOCK, (tile + 1) * BLOCK)
            out_ref[rows, key_at:value_at] = (dkt[tile] * factor).T.astype(BF16)
            out_ref[rows, value_at:] = dvt[tile].T.astype(BF16)


def attention(table, starts, ends):
    rows, width = table.shape
    blocks = rows // BLOCK
    tiles = blocks * (blocks + 1) // 2
    return pl.pallas_call(
        attention_kernel,
        out_shape=jax.ShapeDtypeStruct((rows, width), BF16),
        grid_spec=pltpu.PrefetchScalarGridSpec(
            num_scalar_prefetch=2,
            grid=(blocks,),
            in_specs=[pl.BlockSpec((rows, width), lambda i, *_: (0, 0))],
            out_specs=pl.BlockSpec((rows, width), lambda i, *_: (0, 0)),
            scratch_shapes=[
                pltpu.VMEM((blocks, HEAD_DIM, BLOCK), BF16),
                pltpu.VMEM((blocks, HEAD_DIM, BLOCK), BF16),
                pltpu.VMEM((blocks, HEAD_DIM, BLOCK), F32),
                pltpu.VMEM((blocks, HEAD_DIM, BLOCK), F32),
                pltpu.VMEM((blocks, BLOCK, BLOCK), F32),
                pltpu.VMEM((blocks, BLOCK, BLOCK), F32),
            ],
        ),
        compiler_params=pltpu.CompilerParams(vmem_limit_bytes=VMEM_BYTES),
        cost_estimate=pl.CostEstimate(
            flops=tiles * 2 * 6 * 2 * BLOCK * BLOCK * HEAD_DIM,
            bytes_accessed=4 * rows * width,
            transcendentals=tiles * 2 * BLOCK * BLOCK,
        ),
    )(starts, ends, table)


def finish_kernel(
    came_ref, low_ref, up_ref, inputs_ref, cos_ref, sin_ref, out_ref, grad_ref, term_ref
):
    cosine = cos_ref[...]
    sine = -sin_ref[...]
    rank, queries = up_ref.shape
    low_t = low_ref[...].astype(F32).T.astype(BF16)
    kv_width = (grad_ref.shape[1] - queries) // 2
    dlow = jnp.zeros(low_ref.shape, F32)
    for piece in range(came_ref.shape[0]):
        columns = slice(piece * PAIR, (piece + 1) * PAIR)
        out_ref[:, columns] = came_ref[piece, :, :PAIR]
        for head in range(2):
            at = PAIR + head * HEAD_DIM
            to = piece * PAIR + head * HEAD_DIM
            grad_ref[:, to : to + HEAD_DIM] = rotated(
                came_ref[piece, :, at : at + HEAD_DIM].astype(F32), cosine, sine
            ).astype(BF16)
        part = grad_ref[:, columns]
        dlow += lax.dot_general(
            part, up_ref[:, columns], (((1,), (1,)), ((), ())), preferred_element_type=F32
        )
        term_ref[piece, rank:] = jnp.dot(low_t, part, preferred_element_type=F32)
    dlow_t = dlow.astype(BF16).astype(F32).T.astype(BF16)
    for piece in range(came_ref.shape[0]):
        columns = slice(piece * PAIR, (piece + 1) * PAIR)
        term_ref[piece, :rank] = jnp.dot(
            dlow_t, inputs_ref[:, columns], preferred_element_type=F32
        )
    for key_head in range(kv_width // HEAD_DIM):
        pair = (2 * key_head, 2 * key_head + 1)
        keys, values = (
            sum(came_ref[piece, :, at : at + HEAD_DIM].astype(F32) for piece in pair)
            for at in (2 * PAIR, 2 * PAIR + HEAD_DIM)
        )
        at = queries + key_head * HEAD_DIM
        grad_ref[:, at : at + HEAD_DIM] = rotated(keys, cosine, sine).astype(BF16)
        grad_ref[:, at + kv_width : at + kv_width + HEAD_DIM] = values.astype(BF16)


def exchange(table, axis):
    return lax.all_to_all(table, axis, split_axis=0, concat_axis=0, tiled=True)


def local(
    projection_rows, normed_input_rows, adapter_down, adapter_up, lengths, groups, output_gradient
):
    qkv_local = projection_rows[0]
    x_local = normed_input_rows[0]
    grad_raw = output_gradient[0]
    length_row = lengths[0]
    width_row = groups[0]
    token_count, model_width = x_local.shape
    qkv_width = qkv_local.shape[1]
    rank, query_columns = adapter_up.shape
    members = lax.axis_size("sub")
    half_index = lax.axis_index("half")
    group_index = half_index * members + lax.axis_index("sub")
    low_local = jnp.dot(x_local, adapter_down, preferred_element_type=F32).astype(BF16)
    low_wide = jnp.pad(low_local, ((0, 0), (0, HEAD_DIM - rank)))
    packed_qkv = exchange(jnp.concatenate([qkv_local, low_wide], axis=1), "dp")
    packed_low = packed_qkv[:, qkv_width : qkv_width + rank]

    ends_dev = jnp.cumsum(width_row)
    starts_dev = ends_dev - width_row

    def owner_of(device):
        picked = (device[:, None] >= starts_dev[None, :]) & (device[:, None] < ends_dev[None, :])
        start = jnp.sum(jnp.where(picked, starts_dev[None, :], 0), axis=1)
        length = jnp.sum(jnp.where(picked, length_row[None, :], 0), axis=1)
        return start, length

    start_me, length_me = owner_of(group_index[None])
    row_at = jnp.arange(token_count, dtype=jnp.int32)
    local_offsets = (group_index - start_me) * token_count + row_at
    row_valid = (local_offsets < length_me).astype(jnp.int32)[:, None]
    cosine, sine = rope_tables(local_offsets)
    per_block = PART // token_count
    block_device = half_index * members + per_block * jnp.arange(
        members // per_block, dtype=jnp.int32
    )
    block_start, block_length = owner_of(block_device)
    first_rows = (block_start - half_index * members) * token_count
    starts = first_rows
    ends = first_rows + block_length

    params = pltpu.CompilerParams(vmem_limit_bytes=VMEM_BYTES)
    pieces = pl.pallas_call(
        prepare_kernel,
        out_shape=jax.ShapeDtypeStruct((members, token_count, PIECE), BF16),
        compiler_params=params,
    )(packed_qkv, adapter_up, cosine, sine, grad_raw, row_valid)
    table = exchange(pieces, "sub").reshape(members * token_count, PIECE)
    table, x_held = lax.optimization_barrier((table, x_local))
    packed_inputs = exchange(x_held, "dp")
    results = attention(table, starts, ends)
    came = exchange(results.reshape(members, token_count, PIECE), "sub")
    attn_rows, grad_rows, terms = pl.pallas_call(
        finish_kernel,
        out_shape=(
            jax.ShapeDtypeStruct((token_count, query_columns), BF16),
            jax.ShapeDtypeStruct((token_count, qkv_width), BF16),
            jax.ShapeDtypeStruct((members, 2 * rank, PAIR), F32),
        ),
        compiler_params=params,
    )(came, packed_low, adapter_up, packed_inputs, cosine, sine)
    total = jnp.sum(exchange(terms, "sub"), axis=0)
    for axis, apart in (("half", 1), ("dp", 1), ("dp", 2), ("dp", 4)):
        size = lax.axis_size(axis)
        total = total + lax.ppermute(total, axis, [(i, i ^ apart) for i in range(size)])
    whole = exchange(jnp.broadcast_to(total.astype(BF16)[None], terms.shape), "sub").astype(F32)
    grad_a = whole[:, :rank].transpose(0, 2, 1).reshape(model_width, rank)
    grad_b = whole[:, rank:].transpose(1, 0, 2).reshape(rank, query_columns)
    return (attn_rows[None], grad_rows[None], grad_a, grad_b)


def solution(mesh):
    members, replicas = mesh.devices.shape
    split = Mesh(mesh.devices.reshape(2, members // 2, replicas), ("half", "sub", "dp"))
    rows = P("dp", ("half", "sub"), None)
    placed = (rows, rows, P(), P(), P("dp", None), P("dp", None), rows)
    return jax.shard_map(
        local,
        mesh=split,
        in_specs=placed,
        out_specs=(rows, rows, P(), P()),
        check_vma=False,
    )
```

```python
import math

import jax
import jax.numpy as jnp
from jax import lax
from jax.experimental import pallas as pl
from jax.experimental.pallas import tpu as pltpu
from jax.sharding import Mesh
from jax.sharding import PartitionSpec as P

HEAD_DIM = 128
HALF_DIM = HEAD_DIM // 2
PART = 256
BLOCK = 512
PAIR = 2 * HEAD_DIM
PIECE = 2 * PAIR + 2 * HEAD_DIM
rope_base = 500000.0
VMEM_BYTES = 48 * 1024 * 1024
ATTENTION_VMEM_BYTES = 60 * 1024 * 1024
HIDDEN = -1e30
F32 = jnp.float32
BF16 = jnp.bfloat16


def rope_tables(offsets):
    index_float = jnp.arange(HALF_DIM, dtype=F32)
    inverse = jnp.power(F32(rope_base), -index_float / HALF_DIM)
    angles = offsets.astype(F32)[:, None] * inverse[None, :]
    cosine, sine = jnp.cos(angles), jnp.sin(angles)
    return jnp.concatenate([cosine, cosine], axis=1), jnp.concatenate([-sine, sine], axis=1)


def rotated(table, cosine, sine):
    return table * cosine + pltpu.roll(table, HALF_DIM, 1) * sine


def widen_kernel(inputs_ref, down_ref, qkv_ref, out_ref, slab, sems):
    width = qkv_ref.shape[1]
    move = pltpu.make_async_copy(qkv_ref, out_ref.at[:, :width], sems.at[0])
    move.start()
    low = lax.dot_general(
        inputs_ref[...], down_ref[...], (((1,), (1,)), ((), ())), preferred_element_type=F32
    )
    slab[...] = jnp.zeros_like(slab)
    slab[:, : low.shape[1]] = low.astype(BF16)
    add = pltpu.make_async_copy(slab, out_ref.at[:, width:], sems.at[1])
    add.start()
    move.wait()
    add.wait()


def prepare_kernel(qkv_ref, up_ref, cos_ref, sin_ref, grad_ref, valid_ref, out_ref):
    cosine = cos_ref[...]
    sine = sin_ref[...]
    kept = valid_ref[...] > 0
    rank, queries = up_ref.shape
    kv_width = (qkv_ref.shape[1] - HEAD_DIM - queries) // 2
    low_at = queries + 2 * kv_width
    low = qkv_ref[:, low_at : low_at + rank]
    pieces = out_ref.shape[0]
    for piece in range(pieces):
        columns = slice(piece * PAIR, (piece + 1) * PAIR)
        full = qkv_ref[:, columns].astype(F32) + jnp.dot(
            low, up_ref[:, columns], preferred_element_type=F32
        )
        for head in range(2):
            at = slice(head * HEAD_DIM, (head + 1) * HEAD_DIM)
            out_ref[piece, :, at] = rotated(full[:, at], cosine, sine).astype(BF16)
        grad = grad_ref[:, columns]
        out_ref[piece, :, PAIR : 2 * PAIR] = jnp.where(kept, grad, jnp.zeros_like(grad))
    for key_head in range(kv_width // HEAD_DIM):
        at = queries + key_head * HEAD_DIM
        keys = rotated(qkv_ref[:, at : at + HEAD_DIM].astype(F32), cosine, sine).astype(BF16)
        values = qkv_ref[:, at + kv_width : at + kv_width + HEAD_DIM]
        for piece in (2 * key_head, 2 * key_head + 1):
            out_ref[piece, :, 2 * PAIR : 2 * PAIR + HEAD_DIM] = keys
            out_ref[piece, :, 2 * PAIR + HEAD_DIM :] = values


def attention_kernel(start_ref, end_ref, x_ref, out_ref, kt, vt, dkt, dvt, store0, store1):
    store = (store0, store1)
    step = pl.program_id(0)
    blocks = pl.num_programs(0)
    factor = 1.0 / math.sqrt(HEAD_DIM)
    exponent = factor * math.log2(math.e)
    key_at = 2 * PAIR
    value_at = 2 * PAIR + HEAD_DIM
    tiles = x_ref.shape[0] // BLOCK
    per = BLOCK // PART

    @pl.when(step == 0)
    def _():
        for tile in range(tiles):
            rows = slice(tile * BLOCK, (tile + 1) * BLOCK)
            kt[tile] = x_ref[rows, key_at:value_at].T
            vt[tile] = x_ref[rows, value_at:].T
        dkt[...] = jnp.zeros_like(dkt)
        dvt[...] = jnp.zeros_like(dvt)

    own = pl.ds(pl.multiple_of(step * BLOCK, BLOCK), BLOCK)
    first = start_ref[step * per] // BLOCK
    last = step
    end_row = end_ref[step * per]
    column = lax.broadcasted_iota(jnp.int32, (1, BLOCK), 1)
    row = lax.broadcasted_iota(jnp.int32, (BLOCK, 1), 0)
    low_row = jnp.full((BLOCK, 1), start_ref[step * per] - last * BLOCK, jnp.int32)
    high_row = jnp.full((BLOCK, 1), end_row - last * BLOCK, jnp.int32)
    for part in range(1, per):
        inside = row >= part * PART
        low_row = jnp.where(inside, start_ref[step * per + part] - last * BLOCK, low_row)
        high_row = jnp.where(inside, end_ref[step * per + part] - last * BLOCK, high_row)
    queries = [x_ref[own, h * HEAD_DIM : (h + 1) * HEAD_DIM] for h in range(2)]
    grads = [x_ref[own, PAIR + h * HEAD_DIM : PAIR + (h + 1) * HEAD_DIM] for h in range(2)]

    def folded(op, table):
        parts = [table[:, c : c + HEAD_DIM] for c in range(0, BLOCK, HEAD_DIM)]
        while len(parts) > 1:
            parts = [op(a, b) for a, b in zip(parts[::2], parts[1::2])]
        return parts[0]

    def spread(table):
        return jnp.concatenate([table] * (BLOCK // HEAD_DIM), axis=1)

    def key_rows(tile):
        return pl.ds(pl.multiple_of(tile * BLOCK, BLOCK), BLOCK)

    diagonal = (column == row) | ((column < row) & (column >= low_row) & (column < high_row))
    carry = []
    for h in range(2):
        scores = jnp.dot(queries[h], kt[last], preferred_element_type=F32) * exponent
        scores = jnp.where(diagonal, scores, HIDDEN)
        store[h][last] = scores
        top = folded(jnp.maximum, scores)
        carry += [top, folded(jnp.add, jnp.exp2(scores - spread(top)))]

    def score_pass(tile, carry):
        bias = jnp.where(tile * BLOCK + column < end_row, F32(0.0), F32(HIDDEN))
        result = []
        for h in range(2):
            top, total = carry[2 * h], carry[2 * h + 1]
            scores = jnp.dot(queries[h], kt[tile], preferred_element_type=F32) * exponent + bias
            store[h][tile] = scores
            higher = jnp.maximum(top, folded(jnp.maximum, scores))
            total = total * jnp.exp2(top - higher) + folded(
                jnp.add, jnp.exp2(scores - spread(higher))
            )
            result += [higher, total]
        return tuple(result)

    carry = lax.fori_loop(first, last, score_pass, tuple(carry))
    tops, inverse = [], []
    for h in range(2):
        lane_top, lane_total = carry[2 * h], carry[2 * h + 1]
        top = jnp.max(lane_top, axis=1, keepdims=True)
        total = jnp.sum(lane_total * jnp.exp2(lane_top - top), axis=1, keepdims=True)
        tops.append(top)
        inverse.append(1.0 / total)

    empty = jnp.zeros((BLOCK, HEAD_DIM), F32)

    def probs_of(h, tile):
        return jnp.exp2(store[h][tile] - tops[h]) * inverse[h]

    def out_part(h, tile, total):
        values = x_ref[key_rows(tile), value_at:]
        return total + jnp.dot(
            probs_of(h, tile).astype(BF16), values, preferred_element_type=F32
        )

    outs = [None, None]
    deltas = [None, None]
    queries_t = [table.T for table in queries]
    grads_t = [table.T for table in grads]

    def settle(h, total):
        outs[h] = total.astype(BF16)
        deltas[h] = jnp.sum(
            grads[h].astype(F32) * outs[h].astype(F32), axis=1, keepdims=True
        )

    def grad_part(h, tile, total):
        keys = x_ref[key_rows(tile), key_at:value_at]
        grad_probs = jnp.dot(grads[h], vt[tile], preferred_element_type=F32)
        probs = probs_of(h, tile)
        grad_scores = (probs * (grad_probs - deltas[h])).astype(BF16)
        total = total + jnp.dot(grad_scores, keys, preferred_element_type=F32)
        dkt[tile] += jnp.dot(queries_t[h], grad_scores, preferred_element_type=F32)
        dvt[tile] += jnp.dot(grads_t[h], probs.astype(BF16), preferred_element_type=F32)
        return total

    def out_pass(tile, carry):
        return tuple(out_part(h, tile, carry[h]) for h in range(2))

    def gradient_pass(tile, carry):
        return tuple(grad_part(h, tile, carry[h]) for h in range(2))

    sums = lax.fori_loop(first, last + 1, out_pass, (empty, empty))
    for h in range(2):
        settle(h, sums[h])
    query_sums = lax.fori_loop(first, last + 1, gradient_pass, (empty, empty))
    for h in range(2):
        at = h * HEAD_DIM
        out_ref[own, at : at + HEAD_DIM] = outs[h]
        out_ref[own, PAIR + at : PAIR + at + HEAD_DIM] = (query_sums[h] * factor).astype(BF16)

    @pl.when(step == blocks - 1)
    def _():
        for tile in range(tiles):
            rows = slice(tile * BLOCK, (tile + 1) * BLOCK)
            out_ref[rows, key_at:value_at] = (dkt[tile] * factor).T.astype(BF16)
            out_ref[rows, value_at:] = dvt[tile].T.astype(BF16)


def attention(table, starts, ends):
    rows, width = table.shape
    blocks = rows // BLOCK
    tiles = blocks * (blocks + 1) // 2
    return pl.pallas_call(
        attention_kernel,
        out_shape=jax.ShapeDtypeStruct((rows, width), BF16),
        grid_spec=pltpu.PrefetchScalarGridSpec(
            num_scalar_prefetch=2,
            grid=(blocks,),
            in_specs=[pl.BlockSpec((rows, width), lambda i, *_: (0, 0))],
            out_specs=pl.BlockSpec((rows, width), lambda i, *_: (0, 0)),
            scratch_shapes=[
                pltpu.VMEM((blocks, HEAD_DIM, BLOCK), BF16),
                pltpu.VMEM((blocks, HEAD_DIM, BLOCK), BF16),
                pltpu.VMEM((blocks, HEAD_DIM, BLOCK), F32),
                pltpu.VMEM((blocks, HEAD_DIM, BLOCK), F32),
                pltpu.VMEM((blocks, BLOCK, BLOCK), F32),
                pltpu.VMEM((blocks, BLOCK, BLOCK), F32),
            ],
        ),
        compiler_params=pltpu.CompilerParams(vmem_limit_bytes=ATTENTION_VMEM_BYTES),
        cost_estimate=pl.CostEstimate(
            flops=tiles * 2 * 6 * 2 * BLOCK * BLOCK * HEAD_DIM,
            bytes_accessed=4 * rows * width,
            transcendentals=tiles * 2 * BLOCK * BLOCK,
        ),
    )(starts, ends, table)


def finish_kernel(
    came_ref, low_ref, up_ref, inputs_ref, cos_ref, sin_ref, out_ref, grad_ref, term_ref
):
    cosine = cos_ref[...]
    sine = -sin_ref[...]
    rank, queries = up_ref.shape
    low_t = low_ref[...].astype(F32).T.astype(BF16)
    kv_width = (grad_ref.shape[1] - queries) // 2
    dlow = jnp.zeros(low_ref.shape, F32)
    for piece in range(came_ref.shape[0]):
        columns = slice(piece * PAIR, (piece + 1) * PAIR)
        out_ref[:, columns] = came_ref[piece, :, :PAIR]
        for head in range(2):
            at = PAIR + head * HEAD_DIM
            to = piece * PAIR + head * HEAD_DIM
            grad_ref[:, to : to + HEAD_DIM] = rotated(
                came_ref[piece, :, at : at + HEAD_DIM].astype(F32), cosine, sine
            ).astype(BF16)
        part = grad_ref[:, columns]
        dlow += lax.dot_general(
            part, up_ref[:, columns], (((1,), (1,)), ((), ())), preferred_element_type=F32
        )
        term_ref[piece, rank:] = jnp.dot(low_t, part, preferred_element_type=F32).astype(BF16)
    dlow_t = dlow.astype(BF16).astype(F32).T.astype(BF16)
    for piece in range(came_ref.shape[0]):
        columns = slice(piece * PAIR, (piece + 1) * PAIR)
        term_ref[piece, :rank] = jnp.dot(
            dlow_t, inputs_ref[:, columns], preferred_element_type=F32
        ).astype(BF16)
    for key_head in range(kv_width // HEAD_DIM):
        pair = (2 * key_head, 2 * key_head + 1)
        keys, values = (
            sum(came_ref[piece, :, at : at + HEAD_DIM].astype(F32) for piece in pair)
            for at in (2 * PAIR, 2 * PAIR + HEAD_DIM)
        )
        at = queries + key_head * HEAD_DIM
        grad_ref[:, at : at + HEAD_DIM] = rotated(keys, cosine, sine).astype(BF16)
        grad_ref[:, at + kv_width : at + kv_width + HEAD_DIM] = values.astype(BF16)


def unfold_kernel(whole_ref, first_ref, second_ref):
    rank = first_ref.shape[0]
    for piece in range(whole_ref.shape[0]):
        columns = slice(piece * PAIR, (piece + 1) * PAIR)
        first_ref[:, columns] = whole_ref[piece, :rank].astype(F32)
        second_ref[:, columns] = whole_ref[piece, rank:].astype(F32)


def exchange(table, axis):
    return lax.all_to_all(table, axis, split_axis=0, concat_axis=0, tiled=True)


def local(
    projection_rows, normed_input_rows, adapter_down, adapter_up, lengths, groups, output_gradient
):
    qkv_local = projection_rows[0]
    x_local = normed_input_rows[0]
    grad_raw = output_gradient[0]
    length_row = lengths[0]
    width_row = groups[0]
    token_count, model_width = x_local.shape
    qkv_width = qkv_local.shape[1]
    rank, query_columns = adapter_up.shape
    members = lax.axis_size("sub")
    half_index = lax.axis_index("half")
    group_index = half_index * members + lax.axis_index("sub")
    in_vmem = pl.BlockSpec(memory_space=pltpu.VMEM)
    in_place = pl.BlockSpec(memory_space=pl.ANY)
    wide = pl.pallas_call(
        widen_kernel,
        out_shape=jax.ShapeDtypeStruct((token_count, qkv_width + HEAD_DIM), BF16),
        in_specs=[in_vmem, in_vmem, in_place],
        out_specs=in_place,
        scratch_shapes=[
            pltpu.VMEM((token_count, HEAD_DIM), BF16),
            pltpu.SemaphoreType.DMA((2,)),
        ],
        compiler_params=pltpu.CompilerParams(vmem_limit_bytes=VMEM_BYTES),
    )(x_local, adapter_down.T, qkv_local)
    packed_qkv = exchange(wide, "dp")
    packed_low = packed_qkv[:, qkv_width : qkv_width + rank]

    ends_dev = jnp.cumsum(width_row)
    starts_dev = ends_dev - width_row

    def owner_of(device):
        picked = (device[:, None] >= starts_dev[None, :]) & (device[:, None] < ends_dev[None, :])
        start = jnp.sum(jnp.where(picked, starts_dev[None, :], 0), axis=1)
        length = jnp.sum(jnp.where(picked, length_row[None, :], 0), axis=1)
        return start, length

    start_me, length_me = owner_of(group_index[None])
    row_at = jnp.arange(token_count, dtype=jnp.int32)
    local_offsets = (group_index - start_me) * token_count + row_at
    row_valid = (local_offsets < length_me).astype(jnp.int32)[:, None]
    cosine, sine = rope_tables(local_offsets)
    per_block = PART // token_count
    block_device = half_index * members + per_block * jnp.arange(
        members // per_block, dtype=jnp.int32
    )
    block_start, block_length = owner_of(block_device)
    first_rows = (block_start - half_index * members) * token_count
    starts = first_rows
    ends = first_rows + block_length

    params = pltpu.CompilerParams(vmem_limit_bytes=VMEM_BYTES)
    pieces = pl.pallas_call(
        prepare_kernel,
        out_shape=jax.ShapeDtypeStruct((members, token_count, PIECE), BF16),
        compiler_params=params,
    )(packed_qkv, adapter_up, cosine, sine, grad_raw, row_valid)
    table = exchange(pieces, "sub").reshape(members * token_count, PIECE)
    table, x_held = lax.optimization_barrier((table, x_local))
    packed_inputs = exchange(x_held, "dp")
    results = attention(table, starts, ends)
    came = exchange(results.reshape(members, token_count, PIECE), "sub")
    attn_rows, grad_rows, terms = pl.pallas_call(
        finish_kernel,
        out_shape=(
            jax.ShapeDtypeStruct((token_count, query_columns), BF16),
            jax.ShapeDtypeStruct((token_count, qkv_width), BF16),
            jax.ShapeDtypeStruct((members, 2 * rank, PAIR), BF16),
        ),
        compiler_params=params,
    )(came, packed_low, adapter_up, packed_inputs, cosine, sine)
    total = jnp.sum(exchange(terms, "sub").astype(F32), axis=0)
    for axis, apart in (("half", 1), ("dp", 1), ("dp", 2), ("dp", 4)):
        size = lax.axis_size(axis)
        total = total + lax.ppermute(total, axis, [(i, i ^ apart) for i in range(size)])
    whole = exchange(jnp.broadcast_to(total.astype(BF16)[None], terms.shape), "sub")
    grad_a, grad_b = pl.pallas_call(
        unfold_kernel,
        out_shape=(
            jax.ShapeDtypeStruct((rank, model_width), F32),
            jax.ShapeDtypeStruct((rank, query_columns), F32),
        ),
        compiler_params=params,
    )(whole)
    return (attn_rows[None], grad_rows[None], grad_a.T, grad_b)


def solution(mesh):
    members, replicas = mesh.devices.shape
    split = Mesh(mesh.devices.reshape(2, members // 2, replicas), ("half", "sub", "dp"))
    rows = P("dp", ("half", "sub"), None)
    placed = (rows, rows, P(), P(), P("dp", None), P("dp", None), rows)
    return jax.shard_map(
        local,
        mesh=split,
        in_specs=placed,
        out_specs=(rows, rows, P(), P()),
        check_vma=False,
    )
```

```python
import math

import jax
import jax.numpy as jnp
from jax import lax
from jax.experimental import pallas as pl
from jax.experimental.pallas import tpu as pltpu
from jax.sharding import Mesh
from jax.sharding import PartitionSpec as P

HEAD_DIM = 128
HALF_DIM = HEAD_DIM // 2
PART = 256
BLOCK = 512
PAIR = 2 * HEAD_DIM
PIECE = 2 * PAIR + 2 * HEAD_DIM
rope_base = 500000.0
VMEM_BYTES = 48 * 1024 * 1024
ATTENTION_VMEM_BYTES = 60 * 1024 * 1024
HIDDEN = -1e30
CHUNKS = 4
F32 = jnp.float32
BF16 = jnp.bfloat16


def rope_tables(offsets):
    index_float = jnp.arange(HALF_DIM, dtype=F32)
    inverse = jnp.power(F32(rope_base), -index_float / HALF_DIM)
    angles = offsets.astype(F32)[:, None] * inverse[None, :]
    cosine, sine = jnp.cos(angles), jnp.sin(angles)
    return jnp.concatenate([cosine, cosine], axis=1), jnp.concatenate([-sine, sine], axis=1)


def rotated(table, cosine, sine):
    return table * cosine + pltpu.roll(table, HALF_DIM, 1) * sine


def widen_kernel(inputs_ref, down_ref, qkv_ref, out_ref, inputs, down, slab, sems):
    width = qkv_ref.shape[1]
    chunk = inputs.shape[1] // CHUNKS
    parts = [slice(part * chunk, (part + 1) * chunk) for part in range(CHUNKS)]
    loads = [
        pltpu.make_async_copy(inputs_ref.at[:, part], inputs.at[:, part], sems.at[index])
        for index, part in enumerate(parts)
    ]
    load_down = pltpu.make_async_copy(down_ref, down, sems.at[CHUNKS])
    move = pltpu.make_async_copy(qkv_ref, out_ref.at[:, :width], sems.at[CHUNKS + 1])
    load_down.start()
    for load in loads:
        load.start()
    move.start()
    low = jnp.zeros((inputs.shape[0], down.shape[0]), F32)
    slab[...] = jnp.zeros_like(slab)
    load_down.wait()
    for load, part in zip(loads, parts):
        load.wait()
        low += lax.dot_general(
            inputs[:, part], down[:, part], (((1,), (1,)), ((), ())), preferred_element_type=F32
        )
    slab[:, : low.shape[1]] = low.astype(BF16)
    add = pltpu.make_async_copy(slab, out_ref.at[:, width:], sems.at[CHUNKS + 2])
    add.start()
    move.wait()
    add.wait()


def prepare_kernel(qkv_ref, up_ref, cos_ref, sin_ref, grad_ref, valid_ref, out_ref):
    cosine = cos_ref[...]
    sine = sin_ref[...]
    kept = valid_ref[...] > 0
    rank, queries = up_ref.shape
    kv_width = (qkv_ref.shape[1] - HEAD_DIM - queries) // 2
    low_at = queries + 2 * kv_width
    low = qkv_ref[:, low_at : low_at + rank]
    pieces = out_ref.shape[0]
    for piece in range(pieces):
        columns = slice(piece * PAIR, (piece + 1) * PAIR)
        full = qkv_ref[:, columns].astype(F32) + jnp.dot(
            low, up_ref[:, columns], preferred_element_type=F32
        )
        for head in range(2):
            at = slice(head * HEAD_DIM, (head + 1) * HEAD_DIM)
            out_ref[piece, :, at] = rotated(full[:, at], cosine, sine).astype(BF16)
        grad = grad_ref[:, columns]
        out_ref[piece, :, PAIR : 2 * PAIR] = jnp.where(kept, grad, jnp.zeros_like(grad))
    for key_head in range(kv_width // HEAD_DIM):
        at = queries + key_head * HEAD_DIM
        keys = rotated(qkv_ref[:, at : at + HEAD_DIM].astype(F32), cosine, sine).astype(BF16)
        values = qkv_ref[:, at + kv_width : at + kv_width + HEAD_DIM]
        for piece in (2 * key_head, 2 * key_head + 1):
            out_ref[piece, :, 2 * PAIR : 2 * PAIR + HEAD_DIM] = keys
            out_ref[piece, :, 2 * PAIR + HEAD_DIM :] = values


def attention_kernel(
    start_ref, end_ref, q_ref, g_ref, kv_ref, out_ref, kt, vt, dkt, dvt, store0, store1, held, tail, sems
):
    store = (store0, store1)
    step = pl.program_id(0)
    blocks = held.shape[0]
    factor = 1.0 / math.sqrt(HEAD_DIM)
    exponent = factor * math.log2(math.e)
    parts = BLOCK // PART

    @pl.when(step == 0)
    def _():
        for tile in range(blocks):
            rows = slice(tile * BLOCK, (tile + 1) * BLOCK)
            kt[tile] = kv_ref[rows, :HEAD_DIM].T
            vt[tile] = kv_ref[rows, HEAD_DIM:].T
        dkt[...] = jnp.zeros_like(dkt)
        dvt[...] = jnp.zeros_like(dvt)

    first = start_ref[step * parts] // BLOCK
    end_row = end_ref[step * parts]
    own = pl.multiple_of(step * BLOCK, BLOCK)
    column = lax.broadcasted_iota(jnp.int32, (1, BLOCK), 1)
    queries = [q_ref[:, h * HEAD_DIM : (h + 1) * HEAD_DIM] for h in range(2)]
    grads = [g_ref[:, h * HEAD_DIM : (h + 1) * HEAD_DIM] for h in range(2)]
    corners = [(slice(p * PART, (p + 1) * PART), (p + 1) * PART) for p in range(parts)]

    def folded(op, table):
        pieces = [table[:, c : c + HEAD_DIM] for c in range(0, table.shape[1], HEAD_DIM)]
        while len(pieces) > 1:
            pieces = [op(a, b) for a, b in zip(pieces[::2], pieces[1::2])]
        return pieces[0]

    def spread(table, width):
        return jnp.concatenate([table] * (width // HEAD_DIM), axis=1)

    def key_rows(tile):
        return pl.ds(pl.multiple_of(tile * BLOCK, BLOCK), BLOCK)

    def corner_allowed(p, width):
        low = start_ref[step * parts + p] - own
        high = end_ref[step * parts + p] - own
        row = lax.broadcasted_iota(jnp.int32, (PART, 1), 0) + p * PART
        at = column[:, :width]
        return (at == row) | ((at < row) & (at >= low) & (at < high))

    allowed = [corner_allowed(p, width) for p, (_, width) in enumerate(corners)]
    carry = []
    for h in range(2):
        highs, sums = [], []
        for p, (rows, width) in enumerate(corners):
            scores = jnp.dot(queries[h][rows], kt[step, :, :width], preferred_element_type=F32)
            scores = jnp.where(allowed[p], scores * exponent, HIDDEN)
            store[h][step, rows, :width] = scores
            highs.append(folded(jnp.maximum, scores))
            sums.append(folded(jnp.add, jnp.exp2(scores - spread(highs[-1], width))))
        carry += [jnp.concatenate(highs, axis=0), jnp.concatenate(sums, axis=0)]

    def score_pass(tile, carry):
        bias = jnp.where(tile * BLOCK + column < end_row, F32(0.0), F32(HIDDEN))
        result = []
        for h in range(2):
            top, total = carry[2 * h], carry[2 * h + 1]
            scores = jnp.dot(queries[h], kt[tile], preferred_element_type=F32) * exponent + bias
            store[h][tile] = scores
            higher = jnp.maximum(top, folded(jnp.maximum, scores))
            total = total * jnp.exp2(top - higher) + folded(
                jnp.add, jnp.exp2(scores - spread(higher, BLOCK))
            )
            result += [higher, total]
        return tuple(result)

    carry = lax.fori_loop(first, step, score_pass, tuple(carry))
    tops, inverse = [], []
    for h in range(2):
        lane_top, lane_total = carry[2 * h], carry[2 * h + 1]
        top = jnp.max(lane_top, axis=1, keepdims=True)
        total = jnp.sum(lane_total * jnp.exp2(lane_top - top), axis=1, keepdims=True)
        tops.append(top)
        inverse.append(1.0 / total)

    def corner_probs(h, rows, width):
        return jnp.exp2(store[h][step, rows, :width] - tops[h][rows]) * inverse[h][rows]

    def probs_of(h, tile):
        return jnp.exp2(store[h][tile] - tops[h]) * inverse[h]

    own_rows = key_rows(step)
    keys, values = kv_ref[own_rows, :HEAD_DIM], kv_ref[own_rows, HEAD_DIM:]
    sums = []
    for h in range(2):
        sums.append(
            jnp.concatenate(
                [
                    jnp.dot(
                        corner_probs(h, rows, width).astype(BF16),
                        values[:width],
                        preferred_element_type=F32,
                    )
                    for rows, width in corners
                ],
                axis=0,
            )
        )

    def out_pass(tile, carry):
        values = kv_ref[key_rows(tile), HEAD_DIM:]
        return tuple(
            carry[h]
            + jnp.dot(probs_of(h, tile).astype(BF16), values, preferred_element_type=F32)
            for h in range(2)
        )

    sums = lax.fori_loop(first, step, out_pass, tuple(sums))
    outs = [total.astype(BF16) for total in sums]
    deltas = [
        jnp.sum(grads[h].astype(F32) * outs[h].astype(F32), axis=1, keepdims=True) for h in range(2)
    ]
    queries_t = [table.T for table in queries]
    grads_t = [table.T for table in grads]

    query_sums = []
    for h in range(2):
        found = []
        for rows, width in corners:
            grad_probs = jnp.dot(grads[h][rows], vt[step, :, :width], preferred_element_type=F32)
            probs = corner_probs(h, rows, width)
            grad_scores = (probs * (grad_probs - deltas[h][rows])).astype(BF16)
            found.append(jnp.dot(grad_scores, keys[:width], preferred_element_type=F32))
            dkt[step, :, :width] += jnp.dot(
                queries_t[h][:, rows], grad_scores, preferred_element_type=F32
            )
            dvt[step, :, :width] += jnp.dot(
                grads_t[h][:, rows], probs.astype(BF16), preferred_element_type=F32
            )
        query_sums.append(jnp.concatenate(found, axis=0))

    def gradient_pass(tile, carry):
        keys = kv_ref[key_rows(tile), :HEAD_DIM]
        result = []
        for h in range(2):
            grad_probs = jnp.dot(grads[h], vt[tile], preferred_element_type=F32)
            probs = probs_of(h, tile)
            grad_scores = (probs * (grad_probs - deltas[h])).astype(BF16)
            result.append(carry[h] + jnp.dot(grad_scores, keys, preferred_element_type=F32))
            dkt[tile] += jnp.dot(queries_t[h], grad_scores, preferred_element_type=F32)
            dvt[tile] += jnp.dot(grads_t[h], probs.astype(BF16), preferred_element_type=F32)
        return tuple(result)

    query_sums = lax.fori_loop(first, step, gradient_pass, tuple(query_sums))
    for h in range(2):
        at = h * HEAD_DIM
        held[step, :, at : at + HEAD_DIM] = outs[h]
        held[step, :, PAIR + at : PAIR + at + HEAD_DIM] = (query_sums[h] * factor).astype(BF16)

    def block_copy(block):
        rows = pl.ds(pl.multiple_of(block * BLOCK, BLOCK), BLOCK)
        return pltpu.make_async_copy(held.at[block], out_ref.at[rows, : 2 * PAIR], sems.at[block])

    block_copy(step).start()

    @pl.when(step == blocks - 1)
    def _():
        for tile in range(blocks):
            rows = slice(tile * BLOCK, (tile + 1) * BLOCK)
            tail[rows, :HEAD_DIM] = (dkt[tile] * factor).T.astype(BF16)
            tail[rows, HEAD_DIM:] = dvt[tile].T.astype(BF16)
        last = pltpu.make_async_copy(tail, out_ref.at[:, 2 * PAIR :], sems.at[blocks])
        last.start()
        for block in range(blocks):
            block_copy(block).wait()
        last.wait()


def attention(table, starts, ends):
    rows, width = table.shape
    blocks = rows // BLOCK
    tiles = blocks * (blocks + 1) // 2
    return pl.pallas_call(
        attention_kernel,
        out_shape=jax.ShapeDtypeStruct((rows, width), BF16),
        grid_spec=pltpu.PrefetchScalarGridSpec(
            num_scalar_prefetch=2,
            grid=(blocks,),
            in_specs=[
                pl.BlockSpec((BLOCK, PAIR), lambda i, *_: (i, 0)),
                pl.BlockSpec((BLOCK, PAIR), lambda i, *_: (i, 1)),
                pl.BlockSpec((rows, PAIR), lambda i, *_: (0, 2)),
            ],
            out_specs=pl.BlockSpec(memory_space=pl.ANY),
            scratch_shapes=[
                pltpu.VMEM((blocks, HEAD_DIM, BLOCK), BF16),
                pltpu.VMEM((blocks, HEAD_DIM, BLOCK), BF16),
                pltpu.VMEM((blocks, HEAD_DIM, BLOCK), F32),
                pltpu.VMEM((blocks, HEAD_DIM, BLOCK), F32),
                pltpu.VMEM((blocks, BLOCK, BLOCK), F32),
                pltpu.VMEM((blocks, BLOCK, BLOCK), F32),
                pltpu.VMEM((blocks, BLOCK, 2 * PAIR), BF16),
                pltpu.VMEM((rows, PAIR), BF16),
                pltpu.SemaphoreType.DMA((blocks + 1,)),
            ],
        ),
        compiler_params=pltpu.CompilerParams(vmem_limit_bytes=ATTENTION_VMEM_BYTES),
        cost_estimate=pl.CostEstimate(
            flops=tiles * 2 * 6 * 2 * BLOCK * BLOCK * HEAD_DIM,
            bytes_accessed=4 * rows * width,
            transcendentals=tiles * 2 * BLOCK * BLOCK,
        ),
    )(starts, ends, table, table, table)


def query_kernel(
    came_ref, low_ref, up_ref, inputs_ref, cos_ref, sin_ref, grad_ref, term_ref, inputs, sem
):
    load = pltpu.make_async_copy(inputs_ref, inputs, sem)
    load.start()
    cosine = cos_ref[...]
    sine = -sin_ref[...]
    rank = up_ref.shape[0]
    low_t = low_ref[...].astype(F32).T.astype(BF16)
    dlow = jnp.zeros(low_ref.shape, F32)
    for piece in range(came_ref.shape[0]):
        columns = slice(piece * PAIR, (piece + 1) * PAIR)
        for head in range(2):
            at = PAIR + head * HEAD_DIM
            to = piece * PAIR + head * HEAD_DIM
            grad_ref[:, to : to + HEAD_DIM] = rotated(
                came_ref[piece, :, at : at + HEAD_DIM].astype(F32), cosine, sine
            ).astype(BF16)
        part = grad_ref[:, columns]
        dlow += lax.dot_general(
            part, up_ref[:, columns], (((1,), (1,)), ((), ())), preferred_element_type=F32
        )
        term_ref[piece, rank:] = jnp.dot(low_t, part, preferred_element_type=F32).astype(BF16)
    dlow_t = dlow.astype(BF16).astype(F32).T.astype(BF16)
    load.wait()
    for piece in range(came_ref.shape[0]):
        columns = slice(piece * PAIR, (piece + 1) * PAIR)
        term_ref[piece, :rank] = jnp.dot(
            dlow_t, inputs[:, columns], preferred_element_type=F32
        ).astype(BF16)


def finish_kernel(came_ref, query_ref, cos_ref, sin_ref, out_ref, grad_ref):
    cosine = cos_ref[...]
    sine = -sin_ref[...]
    queries = query_ref.shape[1]
    kv_width = (grad_ref.shape[1] - queries) // 2
    grad_ref[:, :queries] = query_ref[...]
    for piece in range(came_ref.shape[0]):
        out_ref[:, piece * PAIR : (piece + 1) * PAIR] = came_ref[piece, :, :PAIR]
    for key_head in range(kv_width // HEAD_DIM):
        pair = (2 * key_head, 2 * key_head + 1)
        keys, values = (
            sum(came_ref[piece, :, at : at + HEAD_DIM].astype(F32) for piece in pair)
            for at in (2 * PAIR, 2 * PAIR + HEAD_DIM)
        )
        at = queries + key_head * HEAD_DIM
        grad_ref[:, at : at + HEAD_DIM] = rotated(keys, cosine, sine).astype(BF16)
        grad_ref[:, at + kv_width : at + kv_width + HEAD_DIM] = values.astype(BF16)


def unfold_kernel(whole_ref, first_ref, second_ref):
    rank = first_ref.shape[0]
    for piece in range(whole_ref.shape[0]):
        columns = slice(piece * PAIR, (piece + 1) * PAIR)
        first_ref[:, columns] = whole_ref[piece, :rank].astype(F32)
        second_ref[:, columns] = whole_ref[piece, rank:].astype(F32)


def exchange(table, axis):
    return lax.all_to_all(table, axis, split_axis=0, concat_axis=0, tiled=True)


def local(
    projection_rows, normed_input_rows, adapter_down, adapter_up, lengths, groups, output_gradient
):
    qkv_local = projection_rows[0]
    x_local = normed_input_rows[0]
    grad_raw = output_gradient[0]
    length_row = lengths[0]
    width_row = groups[0]
    token_count, model_width = x_local.shape
    qkv_width = qkv_local.shape[1]
    rank, query_columns = adapter_up.shape
    members = lax.axis_size("sub")
    half_index = lax.axis_index("half")
    group_index = half_index * members + lax.axis_index("sub")
    in_vmem = pl.BlockSpec(memory_space=pltpu.VMEM)
    in_place = pl.BlockSpec(memory_space=pl.ANY)
    wide = pl.pallas_call(
        widen_kernel,
        out_shape=jax.ShapeDtypeStruct((token_count, qkv_width + HEAD_DIM), BF16),
        in_specs=[in_place, in_place, in_place],
        out_specs=in_place,
        scratch_shapes=[
            pltpu.VMEM((token_count, model_width), BF16),
            pltpu.VMEM((rank, model_width), BF16),
            pltpu.VMEM((token_count, HEAD_DIM), BF16),
            pltpu.SemaphoreType.DMA((CHUNKS + 3,)),
        ],
        compiler_params=pltpu.CompilerParams(vmem_limit_bytes=VMEM_BYTES),
    )(x_local, adapter_down.T, qkv_local)
    packed_qkv = exchange(wide, "dp")
    packed_low = packed_qkv[:, qkv_width : qkv_width + rank]

    ends_dev = jnp.cumsum(width_row)
    starts_dev = ends_dev - width_row

    def owner_of(device):
        picked = (device[:, None] >= starts_dev[None, :]) & (device[:, None] < ends_dev[None, :])
        start = jnp.sum(jnp.where(picked, starts_dev[None, :], 0), axis=1)
        length = jnp.sum(jnp.where(picked, length_row[None, :], 0), axis=1)
        return start, length

    start_me, length_me = owner_of(group_index[None])
    row_at = jnp.arange(token_count, dtype=jnp.int32)
    local_offsets = (group_index - start_me) * token_count + row_at
    row_valid = (local_offsets < length_me).astype(jnp.int32)[:, None]
    cosine, sine = rope_tables(local_offsets)
    per_block = PART // token_count
    block_device = half_index * members + per_block * jnp.arange(
        members // per_block, dtype=jnp.int32
    )
    block_start, block_length = owner_of(block_device)
    first_rows = (block_start - half_index * members) * token_count
    starts = first_rows
    ends = first_rows + block_length

    params = pltpu.CompilerParams(vmem_limit_bytes=VMEM_BYTES)
    pieces = pl.pallas_call(
        prepare_kernel,
        out_shape=jax.ShapeDtypeStruct((members, token_count, PIECE), BF16),
        compiler_params=params,
    )(packed_qkv, adapter_up, cosine, sine, grad_raw, row_valid)
    table = exchange(pieces, "sub").reshape(members * token_count, PIECE)
    table, x_held = lax.optimization_barrier((table, x_local))
    packed_inputs = exchange(x_held, "dp")
    results = attention(table, starts, ends)
    came = exchange(results.reshape(members, token_count, PIECE), "sub")
    query_gradient, terms = pl.pallas_call(
        query_kernel,
        out_shape=(
            jax.ShapeDtypeStruct((token_count, query_columns), BF16),
            jax.ShapeDtypeStruct((members, 2 * rank, PAIR), BF16),
        ),
        in_specs=[in_vmem, in_vmem, in_vmem, in_place, in_vmem, in_vmem],
        scratch_shapes=[
            pltpu.VMEM((token_count, model_width), BF16),
            pltpu.SemaphoreType.DMA(()),
        ],
        compiler_params=params,
    )(came, packed_low, adapter_up, packed_inputs, cosine, sine)
    attn_rows, grad_rows = pl.pallas_call(
        finish_kernel,
        out_shape=(
            jax.ShapeDtypeStruct((token_count, query_columns), BF16),
            jax.ShapeDtypeStruct((token_count, qkv_width), BF16),
        ),
        compiler_params=params,
        cost_estimate=pl.CostEstimate(
            flops=token_count * qkv_width,
            bytes_accessed=8 * token_count * qkv_width,
            transcendentals=0,
        ),
    )(came, query_gradient, cosine, sine)
    total = jnp.sum(exchange(terms, "sub").astype(F32), axis=0)
    for axis, apart in (("half", 1), ("dp", 1), ("dp", 2), ("dp", 4)):
        size = lax.axis_size(axis)
        total = total + lax.ppermute(total, axis, [(i, i ^ apart) for i in range(size)])
    whole = exchange(jnp.broadcast_to(total.astype(BF16)[None], terms.shape), "sub")
    grad_a, grad_b = pl.pallas_call(
        unfold_kernel,
        out_shape=(
            jax.ShapeDtypeStruct((rank, model_width), F32),
            jax.ShapeDtypeStruct((rank, query_columns), F32),
        ),
        compiler_params=params,
    )(whole)
    return (attn_rows[None], grad_rows[None], grad_a.T, grad_b)


def solution(mesh):
    members, replicas = mesh.devices.shape
    split = Mesh(mesh.devices.reshape(2, members // 2, replicas), ("half", "sub", "dp"))
    rows = P("dp", ("half", "sub"), None)
    placed = (rows, rows, P(), P(), P("dp", None), P("dp", None), rows)
    return jax.shard_map(
        local,
        mesh=split,
        in_specs=placed,
        out_specs=(rows, rows, P(), P()),
        check_vma=False,
    )
```

```python
import math

import jax
import jax.numpy as jnp
from jax import lax
from jax.experimental import pallas as pl
from jax.experimental.pallas import tpu as pltpu
from jax.sharding import Mesh
from jax.sharding import PartitionSpec as P

HEAD_DIM = 128
HALF_DIM = HEAD_DIM // 2
PART = 256
BLOCK = 512
PAIR = 2 * HEAD_DIM
PIECE = 2 * PAIR + 2 * HEAD_DIM
rope_base = 500000.0
VMEM_BYTES = 48 * 1024 * 1024
ATTENTION_VMEM_BYTES = 60 * 1024 * 1024
HIDDEN = -1e30
CHUNKS = 4
F32 = jnp.float32
BF16 = jnp.bfloat16


def rope_tables(offsets):
    index_float = jnp.arange(HALF_DIM, dtype=F32)
    inverse = jnp.power(F32(rope_base), -index_float / HALF_DIM)
    angles = offsets.astype(F32)[:, None] * inverse[None, :]
    cosine, sine = jnp.cos(angles), jnp.sin(angles)
    return jnp.concatenate([cosine, cosine], axis=1), jnp.concatenate([-sine, sine], axis=1)


def rotated(table, cosine, sine):
    return table * cosine + pltpu.roll(table, HALF_DIM, 1) * sine


def widen_kernel(inputs_ref, down_ref, qkv_ref, out_ref, inputs, slab, sems):
    width = qkv_ref.shape[1]
    rank = down_ref.shape[0]
    chunk = inputs.shape[1] // CHUNKS
    parts = [slice(part * chunk, (part + 1) * chunk) for part in range(CHUNKS)]
    loads = [
        pltpu.make_async_copy(inputs_ref.at[:, part], inputs.at[:, part], sems.at[index])
        for index, part in enumerate(parts)
    ]
    move = pltpu.make_async_copy(qkv_ref, out_ref.at[:, :width], sems.at[CHUNKS])
    for load in loads:
        load.start()
    move.start()
    low = jnp.zeros((inputs.shape[0], rank), F32)
    slab[...] = jnp.zeros_like(slab)
    for load, part in zip(loads, parts):
        load.wait()
        low += lax.dot_general(
            inputs[:, part], down_ref[:, part], (((1,), (1,)), ((), ())), preferred_element_type=F32
        )
    slab[:, :rank] = low.astype(BF16)
    add = pltpu.make_async_copy(slab, out_ref.at[:, width:], sems.at[CHUNKS + 1])
    add.start()
    move.wait()
    add.wait()


def prepare_kernel(qkv_ref, up_ref, cos_ref, sin_ref, grad_ref, valid_ref, out_ref):
    cosine = cos_ref[...]
    sine = sin_ref[...]
    kept = valid_ref[...] > 0
    rank, queries = up_ref.shape
    kv_width = (qkv_ref.shape[1] - HEAD_DIM - queries) // 2
    low_at = queries + 2 * kv_width
    low = qkv_ref[:, low_at : low_at + rank]
    pieces = out_ref.shape[0]
    for piece in range(pieces):
        columns = slice(piece * PAIR, (piece + 1) * PAIR)
        full = qkv_ref[:, columns].astype(F32) + jnp.dot(
            low, up_ref[:, columns], preferred_element_type=F32
        )
        for head in range(2):
            at = slice(head * HEAD_DIM, (head + 1) * HEAD_DIM)
            out_ref[piece, :, at] = rotated(full[:, at], cosine, sine).astype(BF16)
        grad = grad_ref[:, columns]
        out_ref[piece, :, PAIR : 2 * PAIR] = jnp.where(kept, grad, jnp.zeros_like(grad))
    for key_head in range(kv_width // HEAD_DIM):
        at = queries + key_head * HEAD_DIM
        keys = rotated(qkv_ref[:, at : at + HEAD_DIM].astype(F32), cosine, sine).astype(BF16)
        values = qkv_ref[:, at + kv_width : at + kv_width + HEAD_DIM]
        for piece in (2 * key_head, 2 * key_head + 1):
            out_ref[piece, :, 2 * PAIR : 2 * PAIR + HEAD_DIM] = keys
            out_ref[piece, :, 2 * PAIR + HEAD_DIM :] = values


def attention_kernel(
    start_ref, end_ref, q_ref, g_ref, kv_ref, out_ref, kt, vt, dkt, dvt, store0, store1, held, tail, sems
):
    store = (store0, store1)
    step = pl.program_id(0)
    blocks = held.shape[0]
    factor = 1.0 / math.sqrt(HEAD_DIM)
    exponent = factor * math.log2(math.e)
    parts = BLOCK // PART

    @pl.when(step == 0)
    def _():
        for tile in range(blocks):
            rows = slice(tile * BLOCK, (tile + 1) * BLOCK)
            kt[tile] = kv_ref[rows, :HEAD_DIM].T
            vt[tile] = kv_ref[rows, HEAD_DIM:].T
        dkt[...] = jnp.zeros_like(dkt)
        dvt[...] = jnp.zeros_like(dvt)

    first = start_ref[step * parts] // BLOCK
    end_row = end_ref[step * parts]
    own = pl.multiple_of(step * BLOCK, BLOCK)
    column = lax.broadcasted_iota(jnp.int32, (1, BLOCK), 1)
    queries = [q_ref[:, h * HEAD_DIM : (h + 1) * HEAD_DIM] for h in range(2)]
    grads = [g_ref[:, h * HEAD_DIM : (h + 1) * HEAD_DIM] for h in range(2)]
    corners = [(slice(p * PART, (p + 1) * PART), (p + 1) * PART) for p in range(parts)]

    def folded(op, table):
        pieces = [table[:, c : c + HEAD_DIM] for c in range(0, table.shape[1], HEAD_DIM)]
        while len(pieces) > 1:
            pieces = [op(a, b) for a, b in zip(pieces[::2], pieces[1::2])]
        return pieces[0]

    def spread(table, width):
        return jnp.concatenate([table] * (width // HEAD_DIM), axis=1)

    def key_rows(tile):
        return pl.ds(pl.multiple_of(tile * BLOCK, BLOCK), BLOCK)

    def corner_allowed(p, width):
        low = start_ref[step * parts + p] - own
        high = end_ref[step * parts + p] - own
        row = lax.broadcasted_iota(jnp.int32, (PART, 1), 0) + p * PART
        at = column[:, :width]
        return (at == row) | ((at < row) & (at >= low) & (at < high))

    allowed = [corner_allowed(p, width) for p, (_, width) in enumerate(corners)]
    carry = []
    for h in range(2):
        highs, sums = [], []
        for p, (rows, width) in enumerate(corners):
            scores = jnp.dot(queries[h][rows], kt[step, :, :width], preferred_element_type=F32)
            scores = jnp.where(allowed[p], scores * exponent, HIDDEN)
            store[h][step, rows, :width] = scores
            highs.append(folded(jnp.maximum, scores))
            sums.append(folded(jnp.add, jnp.exp2(scores - spread(highs[-1], width))))
        carry += [jnp.concatenate(highs, axis=0), jnp.concatenate(sums, axis=0)]

    def score_pass(tile, carry):
        bias = jnp.where(tile * BLOCK + column < end_row, F32(0.0), F32(HIDDEN))
        result = []
        for h in range(2):
            top, total = carry[2 * h], carry[2 * h + 1]
            scores = jnp.dot(queries[h], kt[tile], preferred_element_type=F32) * exponent + bias
            store[h][tile] = scores
            higher = jnp.maximum(top, folded(jnp.maximum, scores))
            total = total * jnp.exp2(top - higher) + folded(
                jnp.add, jnp.exp2(scores - spread(higher, BLOCK))
            )
            result += [higher, total]
        return tuple(result)

    carry = lax.fori_loop(first, step, score_pass, tuple(carry))
    tops, inverse = [], []
    for h in range(2):
        lane_top, lane_total = carry[2 * h], carry[2 * h + 1]
        top = jnp.max(lane_top, axis=1, keepdims=True)
        total = jnp.sum(lane_total * jnp.exp2(lane_top - top), axis=1, keepdims=True)
        tops.append(top)
        inverse.append(1.0 / total)

    def corner_probs(h, rows, width):
        return jnp.exp2(store[h][step, rows, :width] - tops[h][rows]) * inverse[h][rows]

    def probs_of(h, tile):
        return jnp.exp2(store[h][tile] - tops[h]) * inverse[h]

    own_rows = key_rows(step)
    keys, values = kv_ref[own_rows, :HEAD_DIM], kv_ref[own_rows, HEAD_DIM:]
    sums = []
    for h in range(2):
        sums.append(
            jnp.concatenate(
                [
                    jnp.dot(
                        corner_probs(h, rows, width).astype(BF16),
                        values[:width],
                        preferred_element_type=F32,
                    )
                    for rows, width in corners
                ],
                axis=0,
            )
        )

    def out_pass(tile, carry):
        values = kv_ref[key_rows(tile), HEAD_DIM:]
        return tuple(
            carry[h]
            + jnp.dot(probs_of(h, tile).astype(BF16), values, preferred_element_type=F32)
            for h in range(2)
        )

    sums = lax.fori_loop(first, step, out_pass, tuple(sums))
    outs = [total.astype(BF16) for total in sums]
    deltas = [
        jnp.sum(grads[h].astype(F32) * outs[h].astype(F32), axis=1, keepdims=True) for h in range(2)
    ]
    queries_t = [table.T for table in queries]
    grads_t = [table.T for table in grads]

    query_sums = []
    for h in range(2):
        found = []
        for rows, width in corners:
            grad_probs = jnp.dot(grads[h][rows], vt[step, :, :width], preferred_element_type=F32)
            probs = corner_probs(h, rows, width)
            grad_scores = (probs * (grad_probs - deltas[h][rows])).astype(BF16)
            found.append(jnp.dot(grad_scores, keys[:width], preferred_element_type=F32))
            dkt[step, :, :width] += jnp.dot(
                queries_t[h][:, rows], grad_scores, preferred_element_type=F32
            )
            dvt[step, :, :width] += jnp.dot(
                grads_t[h][:, rows], probs.astype(BF16), preferred_element_type=F32
            )
        query_sums.append(jnp.concatenate(found, axis=0))

    def gradient_pass(tile, carry):
        keys = kv_ref[key_rows(tile), :HEAD_DIM]
        result = []
        for h in range(2):
            grad_probs = jnp.dot(grads[h], vt[tile], preferred_element_type=F32)
            probs = probs_of(h, tile)
            grad_scores = (probs * (grad_probs - deltas[h])).astype(BF16)
            result.append(carry[h] + jnp.dot(grad_scores, keys, preferred_element_type=F32))
            dkt[tile] += jnp.dot(queries_t[h], grad_scores, preferred_element_type=F32)
            dvt[tile] += jnp.dot(grads_t[h], probs.astype(BF16), preferred_element_type=F32)
        return tuple(result)

    query_sums = lax.fori_loop(first, step, gradient_pass, tuple(query_sums))
    for h in range(2):
        at = h * HEAD_DIM
        held[step, :, at : at + HEAD_DIM] = outs[h]
        held[step, :, PAIR + at : PAIR + at + HEAD_DIM] = (query_sums[h] * factor).astype(BF16)

    def block_copy(block):
        rows = pl.ds(pl.multiple_of(block * BLOCK, BLOCK), BLOCK)
        return pltpu.make_async_copy(held.at[block], out_ref.at[rows, : 2 * PAIR], sems.at[block])

    block_copy(step).start()

    @pl.when(step == blocks - 1)
    def _():
        for tile in range(blocks):
            rows = slice(tile * BLOCK, (tile + 1) * BLOCK)
            tail[rows, :HEAD_DIM] = (dkt[tile] * factor).T.astype(BF16)
            tail[rows, HEAD_DIM:] = dvt[tile].T.astype(BF16)
        last = pltpu.make_async_copy(tail, out_ref.at[:, 2 * PAIR :], sems.at[blocks])
        last.start()
        for block in range(blocks):
            block_copy(block).wait()
        last.wait()


def attention(table, starts, ends):
    rows, width = table.shape
    blocks = rows // BLOCK
    tiles = blocks * (blocks + 1) // 2
    return pl.pallas_call(
        attention_kernel,
        out_shape=pltpu.HBM((rows, width), BF16),
        grid_spec=pltpu.PrefetchScalarGridSpec(
            num_scalar_prefetch=2,
            grid=(blocks,),
            in_specs=[
                pl.BlockSpec((BLOCK, PAIR), lambda i, *_: (i, 0)),
                pl.BlockSpec((BLOCK, PAIR), lambda i, *_: (i, 1)),
                pl.BlockSpec((rows, PAIR), lambda i, *_: (0, 2)),
            ],
            out_specs=pl.BlockSpec(memory_space=pl.ANY),
            scratch_shapes=[
                pltpu.VMEM((blocks, HEAD_DIM, BLOCK), BF16),
                pltpu.VMEM((blocks, HEAD_DIM, BLOCK), BF16),
                pltpu.VMEM((blocks, HEAD_DIM, BLOCK), F32),
                pltpu.VMEM((blocks, HEAD_DIM, BLOCK), F32),
                pltpu.VMEM((blocks, BLOCK, BLOCK), F32),
                pltpu.VMEM((blocks, BLOCK, BLOCK), F32),
                pltpu.VMEM((blocks, BLOCK, 2 * PAIR), BF16),
                pltpu.VMEM((rows, PAIR), BF16),
                pltpu.SemaphoreType.DMA((blocks + 1,)),
            ],
        ),
        compiler_params=pltpu.CompilerParams(vmem_limit_bytes=ATTENTION_VMEM_BYTES),
        cost_estimate=pl.CostEstimate(
            flops=tiles * 2 * 6 * 2 * BLOCK * BLOCK * HEAD_DIM,
            bytes_accessed=4 * rows * width,
            transcendentals=tiles * 2 * BLOCK * BLOCK,
        ),
    )(starts, ends, table, table, table)


def query_kernel(
    came_ref, low_ref, up_ref, inputs_ref, cos_ref, sin_ref, grad_ref, term_ref, inputs, sem
):
    load = pltpu.make_async_copy(inputs_ref, inputs, sem)
    load.start()
    cosine = cos_ref[...]
    sine = -sin_ref[...]
    rank = up_ref.shape[0]
    low_t = low_ref[...].astype(F32).T.astype(BF16)
    dlow = jnp.zeros(low_ref.shape, F32)
    for piece in range(came_ref.shape[0]):
        columns = slice(piece * PAIR, (piece + 1) * PAIR)
        for head in range(2):
            at = PAIR + head * HEAD_DIM
            to = piece * PAIR + head * HEAD_DIM
            grad_ref[:, to : to + HEAD_DIM] = rotated(
                came_ref[piece, :, at : at + HEAD_DIM].astype(F32), cosine, sine
            ).astype(BF16)
        part = grad_ref[:, columns]
        dlow += lax.dot_general(
            part, up_ref[:, columns], (((1,), (1,)), ((), ())), preferred_element_type=F32
        )
        term_ref[piece, rank:] = jnp.dot(low_t, part, preferred_element_type=F32).astype(BF16)
    dlow_t = dlow.astype(BF16).astype(F32).T.astype(BF16)
    load.wait()
    for piece in range(came_ref.shape[0]):
        columns = slice(piece * PAIR, (piece + 1) * PAIR)
        term_ref[piece, :rank] = jnp.dot(
            dlow_t, inputs[:, columns], preferred_element_type=F32
        ).astype(BF16)


def finish_kernel(came_ref, query_ref, cos_ref, sin_ref, out_ref, grad_ref):
    cosine = cos_ref[...]
    sine = -sin_ref[...]
    queries = query_ref.shape[1]
    kv_width = (grad_ref.shape[1] - queries) // 2
    grad_ref[:, :queries] = query_ref[...]
    for piece in range(came_ref.shape[0]):
        out_ref[:, piece * PAIR : (piece + 1) * PAIR] = came_ref[piece, :, :PAIR]
    for key_head in range(kv_width // HEAD_DIM):
        pair = (2 * key_head, 2 * key_head + 1)
        keys, values = (
            sum(came_ref[piece, :, at : at + HEAD_DIM].astype(F32) for piece in pair)
            for at in (2 * PAIR, 2 * PAIR + HEAD_DIM)
        )
        at = queries + key_head * HEAD_DIM
        grad_ref[:, at : at + HEAD_DIM] = rotated(keys, cosine, sine).astype(BF16)
        grad_ref[:, at + kv_width : at + kv_width + HEAD_DIM] = values.astype(BF16)


def unfold_kernel(whole_ref, first_ref, second_ref):
    rank = first_ref.shape[0]
    for piece in range(whole_ref.shape[0]):
        columns = slice(piece * PAIR, (piece + 1) * PAIR)
        first_ref[:, columns] = whole_ref[piece, :rank].astype(F32)
        second_ref[:, columns] = whole_ref[piece, rank:].astype(F32)


def in_hbm(table):
    return pltpu.with_memory_space_constraint(table, pltpu.HBM)


def exchange(table, axis):
    return lax.all_to_all(table, axis, split_axis=0, concat_axis=0, tiled=True)


def local(
    projection_rows, normed_input_rows, adapter_down, adapter_up, lengths, groups, output_gradient
):
    qkv_local = projection_rows[0]
    x_local = normed_input_rows[0]
    grad_raw = output_gradient[0]
    length_row = lengths[0]
    width_row = groups[0]
    token_count, model_width = x_local.shape
    qkv_width = qkv_local.shape[1]
    rank, query_columns = adapter_up.shape
    members = lax.axis_size("sub")
    half_index = lax.axis_index("half")
    group_index = half_index * members + lax.axis_index("sub")
    in_vmem = pl.BlockSpec(memory_space=pltpu.VMEM)
    in_place = pl.BlockSpec(memory_space=pl.ANY)
    wide = pl.pallas_call(
        widen_kernel,
        out_shape=pltpu.HBM((token_count, qkv_width + HEAD_DIM), BF16),
        in_specs=[in_place, in_vmem, in_place],
        out_specs=in_place,
        scratch_shapes=[
            pltpu.VMEM((token_count, model_width), BF16),
            pltpu.VMEM((token_count, HEAD_DIM), BF16),
            pltpu.SemaphoreType.DMA((CHUNKS + 2,)),
        ],
        compiler_params=pltpu.CompilerParams(vmem_limit_bytes=VMEM_BYTES),
    )(in_hbm(x_local), adapter_down.T, in_hbm(qkv_local))
    packed_qkv = exchange(wide, "dp")
    packed_low = packed_qkv[:, qkv_width : qkv_width + rank]

    ends_dev = jnp.cumsum(width_row)
    starts_dev = ends_dev - width_row

    def owner_of(device):
        picked = (device[:, None] >= starts_dev[None, :]) & (device[:, None] < ends_dev[None, :])
        start = jnp.sum(jnp.where(picked, starts_dev[None, :], 0), axis=1)
        length = jnp.sum(jnp.where(picked, length_row[None, :], 0), axis=1)
        return start, length

    start_me, length_me = owner_of(group_index[None])
    row_at = jnp.arange(token_count, dtype=jnp.int32)
    local_offsets = (group_index - start_me) * token_count + row_at
    row_valid = (local_offsets < length_me).astype(jnp.int32)[:, None]
    cosine, sine = rope_tables(local_offsets)
    per_block = PART // token_count
    block_device = half_index * members + per_block * jnp.arange(
        members // per_block, dtype=jnp.int32
    )
    block_start, block_length = owner_of(block_device)
    first_rows = (block_start - half_index * members) * token_count
    starts = first_rows
    ends = first_rows + block_length

    params = pltpu.CompilerParams(vmem_limit_bytes=VMEM_BYTES)
    pieces = pl.pallas_call(
        prepare_kernel,
        out_shape=jax.ShapeDtypeStruct((members, token_count, PIECE), BF16),
        compiler_params=params,
    )(packed_qkv, adapter_up, cosine, sine, grad_raw, row_valid)
    table = in_hbm(exchange(pieces, "sub").reshape(members * token_count, PIECE))
    table, x_held = lax.optimization_barrier((table, x_local))
    packed_inputs = in_hbm(exchange(x_held, "dp"))
    results = attention(table, starts, ends)
    came = exchange(results.reshape(members, token_count, PIECE), "sub")
    query_gradient, terms = pl.pallas_call(
        query_kernel,
        out_shape=(
            jax.ShapeDtypeStruct((token_count, query_columns), BF16),
            jax.ShapeDtypeStruct((members, 2 * rank, PAIR), BF16),
        ),
        in_specs=[in_vmem, in_vmem, in_vmem, in_place, in_vmem, in_vmem],
        scratch_shapes=[
            pltpu.VMEM((token_count, model_width), BF16),
            pltpu.SemaphoreType.DMA(()),
        ],
        compiler_params=params,
    )(came, packed_low, adapter_up, packed_inputs, cosine, sine)
    attn_rows, grad_rows = pl.pallas_call(
        finish_kernel,
        out_shape=(
            jax.ShapeDtypeStruct((token_count, query_columns), BF16),
            jax.ShapeDtypeStruct((token_count, qkv_width), BF16),
        ),
        compiler_params=params,
        cost_estimate=pl.CostEstimate(
            flops=token_count * qkv_width,
            bytes_accessed=8 * token_count * qkv_width,
            transcendentals=0,
        ),
    )(came, query_gradient, cosine, sine)
    total = jnp.sum(exchange(terms, "sub").astype(F32), axis=0)
    for axis, apart in (("half", 1), ("dp", 1), ("dp", 2), ("dp", 4)):
        size = lax.axis_size(axis)
        total = total + lax.ppermute(total, axis, [(i, i ^ apart) for i in range(size)])
    whole = exchange(jnp.broadcast_to(total.astype(BF16)[None], terms.shape), "sub")
    grad_a, grad_b = pl.pallas_call(
        unfold_kernel,
        out_shape=(
            jax.ShapeDtypeStruct((rank, model_width), F32),
            jax.ShapeDtypeStruct((rank, query_columns), F32),
        ),
        compiler_params=params,
    )(whole)
    return (attn_rows[None], grad_rows[None], grad_a.T, grad_b)


def solution(mesh):
    members, replicas = mesh.devices.shape
    split = Mesh(mesh.devices.reshape(2, members // 2, replicas), ("half", "sub", "dp"))
    rows = P("dp", ("half", "sub"), None)
    placed = (rows, rows, P(), P(), P("dp", None), P("dp", None), rows)
    return jax.shard_map(
        local,
        mesh=split,
        in_specs=placed,
        out_specs=(rows, rows, P(), P()),
        check_vma=False,
    )
```

```python
import math

import jax
import jax.numpy as jnp
from jax import lax
from jax.experimental import pallas as pl
from jax.experimental.pallas import tpu as pltpu
from jax.sharding import Mesh
from jax.sharding import PartitionSpec as P

HEAD_DIM = 128
HALF_DIM = HEAD_DIM // 2
PART = 256
BLOCK = 512
PAIR = 2 * HEAD_DIM
PIECE = 2 * PAIR + 2 * HEAD_DIM
rope_base = 500000.0
VMEM_BYTES = 48 * 1024 * 1024
ATTENTION_VMEM_BYTES = 60 * 1024 * 1024
HIDDEN = -1e30
CHUNKS = 4
F32 = jnp.float32
BF16 = jnp.bfloat16


def rope_tables(offsets):
    index_float = jnp.arange(HALF_DIM, dtype=F32)
    inverse = jnp.power(F32(rope_base), -index_float / HALF_DIM)
    angles = offsets.astype(F32)[:, None] * inverse[None, :]
    cosine, sine = jnp.cos(angles), jnp.sin(angles)
    return jnp.concatenate([cosine, cosine], axis=1), jnp.concatenate([-sine, sine], axis=1)


def rotated(table, cosine, sine):
    return table * cosine + pltpu.roll(table, HALF_DIM, 1) * sine


def widen_kernel(inputs_ref, down_ref, qkv_ref, out_ref, inputs, down, held, sems, moves):
    width = qkv_ref.shape[1]
    rank = down_ref.shape[0]

    def copies(source, target, span, use, first):
        size = span // CHUNKS
        return [
            pltpu.make_async_copy(
                source.at[:, part * size : (part + 1) * size],
                target.at[:, part * size : (part + 1) * size],
                use.at[first + part],
            )
            for part in range(CHUNKS)
        ]

    load_down = pltpu.make_async_copy(down_ref, down, sems.at[2 * CHUNKS])
    load_down.start()
    loads = copies(inputs_ref, inputs, inputs.shape[1], sems, 0)
    reads = copies(qkv_ref, held, width, sems, CHUNKS)
    writes = copies(held, out_ref, width, moves, 0)
    for load in loads + reads:
        load.start()
    low = jnp.zeros((inputs.shape[0], rank), F32)
    held[:, width:] = jnp.zeros((inputs.shape[0], HEAD_DIM), BF16)
    chunk = inputs.shape[1] // CHUNKS
    load_down.wait()
    for index, load in enumerate(loads):
        part = slice(index * chunk, (index + 1) * chunk)
        load.wait()
        low += lax.dot_general(
            inputs[:, part], down[:, part], (((1,), (1,)), ((), ())), preferred_element_type=F32
        )
        reads[index].wait()
        writes[index].start()
    held[:, width : width + rank] = low.astype(BF16)
    last = pltpu.make_async_copy(held.at[:, width:], out_ref.at[:, width:], moves.at[CHUNKS])
    last.start()
    for write in writes:
        write.wait()
    last.wait()


def prepare_kernel(qkv_ref, up_ref, cos_ref, sin_ref, grad_ref, valid_ref, out_ref):
    cosine = cos_ref[...]
    sine = sin_ref[...]
    kept = valid_ref[...] > 0
    rank, queries = up_ref.shape
    kv_width = (qkv_ref.shape[1] - HEAD_DIM - queries) // 2
    low_at = queries + 2 * kv_width
    low = qkv_ref[:, low_at : low_at + rank]
    pieces = out_ref.shape[0]
    for piece in range(pieces):
        columns = slice(piece * PAIR, (piece + 1) * PAIR)
        full = qkv_ref[:, columns].astype(F32) + jnp.dot(
            low, up_ref[:, columns], preferred_element_type=F32
        )
        for head in range(2):
            at = slice(head * HEAD_DIM, (head + 1) * HEAD_DIM)
            out_ref[piece, :, at] = rotated(full[:, at], cosine, sine).astype(BF16)
        grad = grad_ref[:, columns]
        out_ref[piece, :, PAIR : 2 * PAIR] = jnp.where(kept, grad, jnp.zeros_like(grad))
    for key_head in range(kv_width // HEAD_DIM):
        at = queries + key_head * HEAD_DIM
        keys = rotated(qkv_ref[:, at : at + HEAD_DIM].astype(F32), cosine, sine).astype(BF16)
        values = qkv_ref[:, at + kv_width : at + kv_width + HEAD_DIM]
        for piece in (2 * key_head, 2 * key_head + 1):
            out_ref[piece, :, 2 * PAIR : 2 * PAIR + HEAD_DIM] = keys
            out_ref[piece, :, 2 * PAIR + HEAD_DIM :] = values


def attention_kernel(
    start_ref, end_ref, q_ref, g_ref, kv_ref, out_ref, kt, vt, dkt, dvt, store0, store1, held, tail, sems
):
    store = (store0, store1)
    step = pl.program_id(0)
    blocks = held.shape[0]
    factor = 1.0 / math.sqrt(HEAD_DIM)
    exponent = factor * math.log2(math.e)
    parts = BLOCK // PART

    @pl.when(step == 0)
    def _():
        for tile in range(blocks):
            rows = slice(tile * BLOCK, (tile + 1) * BLOCK)
            kt[tile] = kv_ref[rows, :HEAD_DIM].T
            vt[tile] = kv_ref[rows, HEAD_DIM:].T
        dkt[...] = jnp.zeros_like(dkt)
        dvt[...] = jnp.zeros_like(dvt)

    first = start_ref[step * parts] // BLOCK
    end_row = end_ref[step * parts]
    own = pl.multiple_of(step * BLOCK, BLOCK)
    column = lax.broadcasted_iota(jnp.int32, (1, BLOCK), 1)
    queries = [q_ref[:, h * HEAD_DIM : (h + 1) * HEAD_DIM] for h in range(2)]
    grads = [g_ref[:, h * HEAD_DIM : (h + 1) * HEAD_DIM] for h in range(2)]
    corners = [(slice(p * PART, (p + 1) * PART), (p + 1) * PART) for p in range(parts)]

    def folded(op, table):
        pieces = [table[:, c : c + HEAD_DIM] for c in range(0, table.shape[1], HEAD_DIM)]
        while len(pieces) > 1:
            pieces = [op(a, b) for a, b in zip(pieces[::2], pieces[1::2])]
        return pieces[0]

    def spread(table, width):
        return jnp.concatenate([table] * (width // HEAD_DIM), axis=1)

    def key_rows(tile):
        return pl.ds(pl.multiple_of(tile * BLOCK, BLOCK), BLOCK)

    def corner_allowed(p, width):
        low = start_ref[step * parts + p] - own
        high = end_ref[step * parts + p] - own
        row = lax.broadcasted_iota(jnp.int32, (PART, 1), 0) + p * PART
        at = column[:, :width]
        return (at == row) | ((at < row) & (at >= low) & (at < high))

    allowed = [corner_allowed(p, width) for p, (_, width) in enumerate(corners)]
    carry = []
    for h in range(2):
        highs, sums = [], []
        for p, (rows, width) in enumerate(corners):
            scores = jnp.dot(queries[h][rows], kt[step, :, :width], preferred_element_type=F32)
            scores = jnp.where(allowed[p], scores * exponent, HIDDEN)
            store[h][step, rows, :width] = scores
            highs.append(folded(jnp.maximum, scores))
            sums.append(folded(jnp.add, jnp.exp2(scores - spread(highs[-1], width))))
        carry += [jnp.concatenate(highs, axis=0), jnp.concatenate(sums, axis=0)]

    def score_pass(tile, carry):
        bias = jnp.where(tile * BLOCK + column < end_row, F32(0.0), F32(HIDDEN))
        result = []
        for h in range(2):
            top, total = carry[2 * h], carry[2 * h + 1]
            scores = jnp.dot(queries[h], kt[tile], preferred_element_type=F32) * exponent + bias
            store[h][tile] = scores
            higher = jnp.maximum(top, folded(jnp.maximum, scores))
            total = total * jnp.exp2(top - higher) + folded(
                jnp.add, jnp.exp2(scores - spread(higher, BLOCK))
            )
            result += [higher, total]
        return tuple(result)

    carry = lax.fori_loop(first, step, score_pass, tuple(carry))
    tops, inverse = [], []
    for h in range(2):
        lane_top, lane_total = carry[2 * h], carry[2 * h + 1]
        top = jnp.max(lane_top, axis=1, keepdims=True)
        total = jnp.sum(lane_total * jnp.exp2(lane_top - top), axis=1, keepdims=True)
        tops.append(top)
        inverse.append(1.0 / total)

    def corner_probs(h, rows, width):
        return jnp.exp2(store[h][step, rows, :width] - tops[h][rows]) * inverse[h][rows]

    def probs_of(h, tile):
        return jnp.exp2(store[h][tile] - tops[h]) * inverse[h]

    own_rows = key_rows(step)
    keys, values = kv_ref[own_rows, :HEAD_DIM], kv_ref[own_rows, HEAD_DIM:]
    sums = []
    for h in range(2):
        sums.append(
            jnp.concatenate(
                [
                    jnp.dot(
                        corner_probs(h, rows, width).astype(BF16),
                        values[:width],
                        preferred_element_type=F32,
                    )
                    for rows, width in corners
                ],
                axis=0,
            )
        )

    def out_pass(tile, carry):
        values = kv_ref[key_rows(tile), HEAD_DIM:]
        return tuple(
            carry[h]
            + jnp.dot(probs_of(h, tile).astype(BF16), values, preferred_element_type=F32)
            for h in range(2)
        )

    sums = lax.fori_loop(first, step, out_pass, tuple(sums))
    outs = [total.astype(BF16) for total in sums]
    deltas = [
        jnp.sum(grads[h].astype(F32) * outs[h].astype(F32), axis=1, keepdims=True) for h in range(2)
    ]
    queries_t = [table.T for table in queries]
    grads_t = [table.T for table in grads]

    query_sums = []
    for h in range(2):
        found = []
        for rows, width in corners:
            grad_probs = jnp.dot(grads[h][rows], vt[step, :, :width], preferred_element_type=F32)
            probs = corner_probs(h, rows, width)
            grad_scores = (probs * (grad_probs - deltas[h][rows])).astype(BF16)
            found.append(jnp.dot(grad_scores, keys[:width], preferred_element_type=F32))
            dkt[step, :, :width] += jnp.dot(
                queries_t[h][:, rows], grad_scores, preferred_element_type=F32
            )
            dvt[step, :, :width] += jnp.dot(
                grads_t[h][:, rows], probs.astype(BF16), preferred_element_type=F32
            )
        query_sums.append(jnp.concatenate(found, axis=0))

    def gradient_pass(tile, carry):
        keys = kv_ref[key_rows(tile), :HEAD_DIM]
        result = []
        for h in range(2):
            grad_probs = jnp.dot(grads[h], vt[tile], preferred_element_type=F32)
            probs = probs_of(h, tile)
            grad_scores = (probs * (grad_probs - deltas[h])).astype(BF16)
            result.append(carry[h] + jnp.dot(grad_scores, keys, preferred_element_type=F32))
            dkt[tile] += jnp.dot(queries_t[h], grad_scores, preferred_element_type=F32)
            dvt[tile] += jnp.dot(grads_t[h], probs.astype(BF16), preferred_element_type=F32)
        return tuple(result)

    query_sums = lax.fori_loop(first, step, gradient_pass, tuple(query_sums))
    for h in range(2):
        at = h * HEAD_DIM
        held[step, :, at : at + HEAD_DIM] = outs[h]
        held[step, :, PAIR + at : PAIR + at + HEAD_DIM] = (query_sums[h] * factor).astype(BF16)

    def block_copy(block):
        rows = pl.ds(pl.multiple_of(block * BLOCK, BLOCK), BLOCK)
        return pltpu.make_async_copy(held.at[block], out_ref.at[rows, : 2 * PAIR], sems.at[block])

    block_copy(step).start()

    @pl.when(step == blocks - 1)
    def _():
        for tile in range(blocks):
            rows = slice(tile * BLOCK, (tile + 1) * BLOCK)
            tail[rows, :HEAD_DIM] = (dkt[tile] * factor).T.astype(BF16)
            tail[rows, HEAD_DIM:] = dvt[tile].T.astype(BF16)
        last = pltpu.make_async_copy(tail, out_ref.at[:, 2 * PAIR :], sems.at[blocks])
        last.start()
        for block in range(blocks):
            block_copy(block).wait()
        last.wait()


def attention(table, starts, ends):
    rows, width = table.shape
    blocks = rows // BLOCK
    tiles = blocks * (blocks + 1) // 2
    return pl.pallas_call(
        attention_kernel,
        out_shape=pltpu.HBM((rows, width), BF16),
        grid_spec=pltpu.PrefetchScalarGridSpec(
            num_scalar_prefetch=2,
            grid=(blocks,),
            in_specs=[
                pl.BlockSpec((BLOCK, PAIR), lambda i, *_: (i, 0)),
                pl.BlockSpec((BLOCK, PAIR), lambda i, *_: (i, 1)),
                pl.BlockSpec((rows, PAIR), lambda i, *_: (0, 2)),
            ],
            out_specs=pl.BlockSpec(memory_space=pl.ANY),
            scratch_shapes=[
                pltpu.VMEM((blocks, HEAD_DIM, BLOCK), BF16),
                pltpu.VMEM((blocks, HEAD_DIM, BLOCK), BF16),
                pltpu.VMEM((blocks, HEAD_DIM, BLOCK), F32),
                pltpu.VMEM((blocks, HEAD_DIM, BLOCK), F32),
                pltpu.VMEM((blocks, BLOCK, BLOCK), F32),
                pltpu.VMEM((blocks, BLOCK, BLOCK), F32),
                pltpu.VMEM((blocks, BLOCK, 2 * PAIR), BF16),
                pltpu.VMEM((rows, PAIR), BF16),
                pltpu.SemaphoreType.DMA((blocks + 1,)),
            ],
        ),
        compiler_params=pltpu.CompilerParams(vmem_limit_bytes=ATTENTION_VMEM_BYTES),
        cost_estimate=pl.CostEstimate(
            flops=tiles * 2 * 6 * 2 * BLOCK * BLOCK * HEAD_DIM,
            bytes_accessed=4 * rows * width,
            transcendentals=tiles * 2 * BLOCK * BLOCK,
        ),
    )(starts, ends, table, table, table)


def query_kernel(
    came_ref, low_ref, up_ref, inputs_ref, cos_ref, sin_ref, grad_ref, term_ref, inputs, sem
):
    load = pltpu.make_async_copy(inputs_ref, inputs, sem)
    load.start()
    cosine = cos_ref[...]
    sine = -sin_ref[...]
    rank = up_ref.shape[0]
    low_t = low_ref[...].astype(F32).T.astype(BF16)
    dlow = jnp.zeros(low_ref.shape, F32)
    for piece in range(came_ref.shape[0]):
        columns = slice(piece * PAIR, (piece + 1) * PAIR)
        for head in range(2):
            at = PAIR + head * HEAD_DIM
            to = piece * PAIR + head * HEAD_DIM
            grad_ref[:, to : to + HEAD_DIM] = rotated(
                came_ref[piece, :, at : at + HEAD_DIM].astype(F32), cosine, sine
            ).astype(BF16)
        part = grad_ref[:, columns]
        dlow += lax.dot_general(
            part, up_ref[:, columns], (((1,), (1,)), ((), ())), preferred_element_type=F32
        )
        term_ref[piece, rank:] = jnp.dot(low_t, part, preferred_element_type=F32).astype(BF16)
    dlow_t = dlow.astype(BF16).astype(F32).T.astype(BF16)
    load.wait()
    for piece in range(came_ref.shape[0]):
        columns = slice(piece * PAIR, (piece + 1) * PAIR)
        term_ref[piece, :rank] = jnp.dot(
            dlow_t, inputs[:, columns], preferred_element_type=F32
        ).astype(BF16)


def finish_kernel(came_ref, query_ref, cos_ref, sin_ref, out_ref, grad_ref):
    cosine = cos_ref[...]
    sine = -sin_ref[...]
    queries = query_ref.shape[1]
    kv_width = (grad_ref.shape[1] - queries) // 2
    grad_ref[:, :queries] = query_ref[...]
    for piece in range(came_ref.shape[0]):
        out_ref[:, piece * PAIR : (piece + 1) * PAIR] = came_ref[piece, :, :PAIR]
    for key_head in range(kv_width // HEAD_DIM):
        pair = (2 * key_head, 2 * key_head + 1)
        keys, values = (
            sum(came_ref[piece, :, at : at + HEAD_DIM].astype(F32) for piece in pair)
            for at in (2 * PAIR, 2 * PAIR + HEAD_DIM)
        )
        at = queries + key_head * HEAD_DIM
        grad_ref[:, at : at + HEAD_DIM] = rotated(keys, cosine, sine).astype(BF16)
        grad_ref[:, at + kv_width : at + kv_width + HEAD_DIM] = values.astype(BF16)


def unfold_kernel(whole_ref, first_ref, second_ref):
    rank = first_ref.shape[0]
    for piece in range(whole_ref.shape[0]):
        columns = slice(piece * PAIR, (piece + 1) * PAIR)
        first_ref[:, columns] = whole_ref[piece, :rank].astype(F32)
        second_ref[:, columns] = whole_ref[piece, rank:].astype(F32)


def in_hbm(table):
    return pltpu.with_memory_space_constraint(table, pltpu.HBM)


def exchange(table, axis):
    return lax.all_to_all(table, axis, split_axis=0, concat_axis=0, tiled=True)


def local(
    projection_rows, normed_input_rows, adapter_down, adapter_up, lengths, groups, output_gradient
):
    qkv_local = projection_rows[0]
    x_local = normed_input_rows[0]
    grad_raw = output_gradient[0]
    length_row = lengths[0]
    width_row = groups[0]
    token_count, model_width = x_local.shape
    qkv_width = qkv_local.shape[1]
    rank, query_columns = adapter_up.shape
    members = lax.axis_size("sub")
    half_index = lax.axis_index("half")
    group_index = half_index * members + lax.axis_index("sub")
    in_vmem = pl.BlockSpec(memory_space=pltpu.VMEM)
    in_place = pl.BlockSpec(memory_space=pl.ANY)
    wide = pl.pallas_call(
        widen_kernel,
        out_shape=pltpu.HBM((token_count, qkv_width + HEAD_DIM), BF16),
        in_specs=[in_place, in_place, in_place],
        out_specs=in_place,
        scratch_shapes=[
            pltpu.VMEM((token_count, model_width), BF16),
            pltpu.VMEM((rank, model_width), BF16),
            pltpu.VMEM((token_count, qkv_width + HEAD_DIM), BF16),
            pltpu.SemaphoreType.DMA((2 * CHUNKS + 1,)),
            pltpu.SemaphoreType.DMA((CHUNKS + 1,)),
        ],
        compiler_params=pltpu.CompilerParams(vmem_limit_bytes=VMEM_BYTES),
    )(in_hbm(x_local), in_hbm(adapter_down.T), in_hbm(qkv_local))
    packed_qkv = exchange(wide, "dp")
    packed_low = packed_qkv[:, qkv_width : qkv_width + rank]

    ends_dev = jnp.cumsum(width_row)
    starts_dev = ends_dev - width_row

    def owner_of(device):
        picked = (device[:, None] >= starts_dev[None, :]) & (device[:, None] < ends_dev[None, :])
        start = jnp.sum(jnp.where(picked, starts_dev[None, :], 0), axis=1)
        length = jnp.sum(jnp.where(picked, length_row[None, :], 0), axis=1)
        return start, length

    start_me, length_me = owner_of(group_index[None])
    row_at = jnp.arange(token_count, dtype=jnp.int32)
    local_offsets = (group_index - start_me) * token_count + row_at
    row_valid = (local_offsets < length_me).astype(jnp.int32)[:, None]
    cosine, sine = rope_tables(local_offsets)
    per_block = PART // token_count
    block_device = half_index * members + per_block * jnp.arange(
        members // per_block, dtype=jnp.int32
    )
    block_start, block_length = owner_of(block_device)
    first_rows = (block_start - half_index * members) * token_count
    starts = first_rows
    ends = first_rows + block_length

    params = pltpu.CompilerParams(vmem_limit_bytes=VMEM_BYTES)
    pieces = pl.pallas_call(
        prepare_kernel,
        out_shape=jax.ShapeDtypeStruct((members, token_count, PIECE), BF16),
        compiler_params=params,
    )(packed_qkv, adapter_up, cosine, sine, grad_raw, row_valid)
    table = in_hbm(exchange(pieces, "sub").reshape(members * token_count, PIECE))
    table, x_held = lax.optimization_barrier((table, x_local))
    packed_inputs = in_hbm(exchange(x_held, "dp"))
    results = attention(table, starts, ends)
    came = exchange(results.reshape(members, token_count, PIECE), "sub")
    query_gradient, terms = pl.pallas_call(
        query_kernel,
        out_shape=(
            jax.ShapeDtypeStruct((token_count, query_columns), BF16),
            pltpu.HBM((members, 2 * rank, PAIR), BF16),
        ),
        in_specs=[in_vmem, in_vmem, in_vmem, in_place, in_vmem, in_vmem],
        scratch_shapes=[
            pltpu.VMEM((token_count, model_width), BF16),
            pltpu.SemaphoreType.DMA(()),
        ],
        compiler_params=params,
    )(came, packed_low, adapter_up, packed_inputs, cosine, sine)
    attn_rows, grad_rows = pl.pallas_call(
        finish_kernel,
        out_shape=(
            jax.ShapeDtypeStruct((token_count, query_columns), BF16),
            jax.ShapeDtypeStruct((token_count, qkv_width), BF16),
        ),
        compiler_params=params,
        cost_estimate=pl.CostEstimate(
            flops=token_count * qkv_width,
            bytes_accessed=8 * token_count * qkv_width,
            transcendentals=0,
        ),
    )(came, query_gradient, cosine, sine)
    total = jnp.sum(exchange(terms, "sub").astype(F32), axis=0)
    for axis, apart in (("half", 1), ("dp", 1), ("dp", 2), ("dp", 4)):
        size = lax.axis_size(axis)
        total = total + lax.ppermute(total, axis, [(i, i ^ apart) for i in range(size)])
    whole = exchange(jnp.broadcast_to(total.astype(BF16)[None], terms.shape), "sub")
    grad_a, grad_b = pl.pallas_call(
        unfold_kernel,
        out_shape=(
            jax.ShapeDtypeStruct((rank, model_width), F32),
            jax.ShapeDtypeStruct((rank, query_columns), F32),
        ),
        compiler_params=params,
    )(whole)
    return (attn_rows[None], grad_rows[None], grad_a.T, grad_b)


def solution(mesh):
    members, replicas = mesh.devices.shape
    split = Mesh(mesh.devices.reshape(2, members // 2, replicas), ("half", "sub", "dp"))
    rows = P("dp", ("half", "sub"), None)
    placed = (rows, rows, P(), P(), P("dp", None), P("dp", None), rows)
    return jax.shard_map(
        local,
        mesh=split,
        in_specs=placed,
        out_specs=(rows, rows, P(), P()),
        check_vma=False,
    )
```

```python
import math

import jax
import jax.numpy as jnp
from jax import lax
from jax.experimental import pallas as pl
from jax.experimental.pallas import tpu as pltpu
from jax.sharding import Mesh
from jax.sharding import PartitionSpec as P

HEAD_DIM = 128
HALF_DIM = HEAD_DIM // 2
PART = 256
BLOCK = 512
PAIR = 2 * HEAD_DIM
PIECE = 2 * PAIR + 2 * HEAD_DIM
rope_base = 500000.0
VMEM_BYTES = 48 * 1024 * 1024
ATTENTION_VMEM_BYTES = 65024 * 1024
HIDDEN = -1e30
CHUNKS = 4
F32 = jnp.float32
BF16 = jnp.bfloat16


def rope_tables(offsets):
    index_float = jnp.arange(HALF_DIM, dtype=F32)
    inverse = jnp.power(F32(rope_base), -index_float / HALF_DIM)
    angles = offsets.astype(F32)[:, None] * inverse[None, :]
    cosine, sine = jnp.cos(angles), jnp.sin(angles)
    return jnp.concatenate([cosine, cosine], axis=1), jnp.concatenate([-sine, sine], axis=1)


def rotated(table, cosine, sine):
    return table * cosine + pltpu.roll(table, HALF_DIM, 1) * sine


def widen_kernel(inputs_ref, down_ref, qkv_ref, out_ref, inputs, down, held, sems, moves):
    width = qkv_ref.shape[1]
    rank = down_ref.shape[0]

    def copies(source, target, span, use, first):
        size = span // CHUNKS
        return [
            pltpu.make_async_copy(
                source.at[:, part * size : (part + 1) * size],
                target.at[:, part * size : (part + 1) * size],
                use.at[first + part],
            )
            for part in range(CHUNKS)
        ]

    load_down = pltpu.make_async_copy(down_ref, down, sems.at[2 * CHUNKS])
    load_down.start()
    loads = copies(inputs_ref, inputs, inputs.shape[1], sems, 0)
    reads = copies(qkv_ref, held, width, sems, CHUNKS)
    writes = copies(held, out_ref, width, moves, 0)
    for load in loads + reads:
        load.start()
    low = jnp.zeros((inputs.shape[0], rank), F32)
    held[:, width:] = jnp.zeros((inputs.shape[0], HEAD_DIM), BF16)
    chunk = inputs.shape[1] // CHUNKS
    load_down.wait()
    for index, load in enumerate(loads):
        part = slice(index * chunk, (index + 1) * chunk)
        load.wait()
        low += lax.dot_general(
            inputs[:, part], down[:, part], (((1,), (1,)), ((), ())), preferred_element_type=F32
        )
        reads[index].wait()
        writes[index].start()
    held[:, width : width + rank] = low.astype(BF16)
    last = pltpu.make_async_copy(held.at[:, width:], out_ref.at[:, width:], moves.at[CHUNKS])
    last.start()
    for write in writes:
        write.wait()
    last.wait()


def prepare_kernel(qkv_ref, up_ref, cos_ref, sin_ref, grad_ref, valid_ref, out_ref):
    cosine = cos_ref[...]
    sine = sin_ref[...]
    kept = valid_ref[...] > 0
    rank, queries = up_ref.shape
    kv_width = (qkv_ref.shape[1] - HEAD_DIM - queries) // 2
    low_at = queries + 2 * kv_width
    low = qkv_ref[:, low_at : low_at + rank]
    pieces = out_ref.shape[0]
    for piece in range(pieces):
        columns = slice(piece * PAIR, (piece + 1) * PAIR)
        full = qkv_ref[:, columns].astype(F32) + jnp.dot(
            low, up_ref[:, columns], preferred_element_type=F32
        )
        for head in range(2):
            at = slice(head * HEAD_DIM, (head + 1) * HEAD_DIM)
            out_ref[piece, :, at] = rotated(full[:, at], cosine, sine).astype(BF16)
        grad = grad_ref[:, columns]
        out_ref[piece, :, PAIR : 2 * PAIR] = jnp.where(kept, grad, jnp.zeros_like(grad))
    for key_head in range(kv_width // HEAD_DIM):
        at = queries + key_head * HEAD_DIM
        keys = rotated(qkv_ref[:, at : at + HEAD_DIM].astype(F32), cosine, sine).astype(BF16)
        values = qkv_ref[:, at + kv_width : at + kv_width + HEAD_DIM]
        for piece in (2 * key_head, 2 * key_head + 1):
            out_ref[piece, :, 2 * PAIR : 2 * PAIR + HEAD_DIM] = keys
            out_ref[piece, :, 2 * PAIR + HEAD_DIM :] = values


def attention_kernel(
    start_ref, end_ref, q_ref, g_ref, kv_ref, out_ref, kt, vt, dkt, dvt, store0, store1, held, tail, sems
):
    store = (store0, store1)
    step = pl.program_id(0)
    blocks = held.shape[0]
    factor = 1.0 / math.sqrt(HEAD_DIM)
    exponent = factor * math.log2(math.e)
    parts = BLOCK // PART

    @pl.when(step == 0)
    def _():
        for tile in range(blocks):
            rows = slice(tile * BLOCK, (tile + 1) * BLOCK)
            kt[tile] = kv_ref[rows, :HEAD_DIM].T
            vt[tile] = kv_ref[rows, HEAD_DIM:].T
        dkt[...] = jnp.zeros_like(dkt)
        dvt[...] = jnp.zeros_like(dvt)

    first = start_ref[step * parts] // BLOCK
    end_row = end_ref[step * parts]
    own = pl.multiple_of(step * BLOCK, BLOCK)
    column = lax.broadcasted_iota(jnp.int32, (1, BLOCK), 1)
    queries = [q_ref[:, h * HEAD_DIM : (h + 1) * HEAD_DIM] for h in range(2)]
    grads = [g_ref[:, h * HEAD_DIM : (h + 1) * HEAD_DIM] for h in range(2)]
    corners = [(slice(p * PART, (p + 1) * PART), (p + 1) * PART) for p in range(parts)]

    def folded(op, table):
        pieces = [table[:, c : c + HEAD_DIM] for c in range(0, table.shape[1], HEAD_DIM)]
        while len(pieces) > 1:
            pieces = [op(a, b) for a, b in zip(pieces[::2], pieces[1::2])]
        return pieces[0]

    def spread(table, width):
        return jnp.concatenate([table] * (width // HEAD_DIM), axis=1)

    def key_rows(tile):
        return pl.ds(pl.multiple_of(tile * BLOCK, BLOCK), BLOCK)

    def corner_allowed(p, width):
        low = start_ref[step * parts + p] - own
        high = end_ref[step * parts + p] - own
        row = lax.broadcasted_iota(jnp.int32, (PART, 1), 0) + p * PART
        at = column[:, :width]
        return (at == row) | ((at < row) & (at >= low) & (at < high))

    allowed = [corner_allowed(p, width) for p, (_, width) in enumerate(corners)]
    carry = []
    for h in range(2):
        highs, sums = [], []
        for p, (rows, width) in enumerate(corners):
            scores = jnp.dot(queries[h][rows], kt[step, :, :width], preferred_element_type=F32)
            scores = jnp.where(allowed[p], scores * exponent, HIDDEN)
            store[h][step, rows, :width] = scores
            highs.append(folded(jnp.maximum, scores))
            sums.append(folded(jnp.add, jnp.exp2(scores - spread(highs[-1], width))))
        carry += [jnp.concatenate(highs, axis=0), jnp.concatenate(sums, axis=0)]

    def score_pass(tile, carry):
        bias = jnp.where(tile * BLOCK + column < end_row, F32(0.0), F32(HIDDEN))
        result = []
        for h in range(2):
            top, total = carry[2 * h], carry[2 * h + 1]
            scores = jnp.dot(queries[h], kt[tile], preferred_element_type=F32) * exponent + bias
            store[h][tile] = scores
            higher = jnp.maximum(top, folded(jnp.maximum, scores))
            total = total * jnp.exp2(top - higher) + folded(
                jnp.add, jnp.exp2(scores - spread(higher, BLOCK))
            )
            result += [higher, total]
        return tuple(result)

    carry = lax.fori_loop(first, step, score_pass, tuple(carry))
    tops, inverse = [], []
    for h in range(2):
        lane_top, lane_total = carry[2 * h], carry[2 * h + 1]
        top = jnp.max(lane_top, axis=1, keepdims=True)
        total = jnp.sum(lane_total * jnp.exp2(lane_top - top), axis=1, keepdims=True)
        tops.append(top)
        inverse.append(1.0 / total)

    def corner_probs(h, rows, width):
        return jnp.exp2(store[h][step, rows, :width] - tops[h][rows]) * inverse[h][rows]

    def probs_of(h, tile):
        return jnp.exp2(store[h][tile] - tops[h]) * inverse[h]

    own_rows = key_rows(step)
    keys, values = kv_ref[own_rows, :HEAD_DIM], kv_ref[own_rows, HEAD_DIM:]
    sums = []
    for h in range(2):
        sums.append(
            jnp.concatenate(
                [
                    jnp.dot(
                        corner_probs(h, rows, width).astype(BF16),
                        values[:width],
                        preferred_element_type=F32,
                    )
                    for rows, width in corners
                ],
                axis=0,
            )
        )

    def out_pass(tile, carry):
        values = kv_ref[key_rows(tile), HEAD_DIM:]
        return tuple(
            carry[h]
            + jnp.dot(probs_of(h, tile).astype(BF16), values, preferred_element_type=F32)
            for h in range(2)
        )

    sums = lax.fori_loop(first, step, out_pass, tuple(sums))
    outs = [total.astype(BF16) for total in sums]
    deltas = [
        jnp.sum(grads[h].astype(F32) * outs[h].astype(F32), axis=1, keepdims=True) for h in range(2)
    ]
    queries_t = [table.T for table in queries]
    grads_t = [table.T for table in grads]

    query_sums = []
    for h in range(2):
        found = []
        for rows, width in corners:
            grad_probs = jnp.dot(grads[h][rows], vt[step, :, :width], preferred_element_type=F32)
            probs = corner_probs(h, rows, width)
            grad_scores = (probs * (grad_probs - deltas[h][rows])).astype(BF16)
            found.append(jnp.dot(grad_scores, keys[:width], preferred_element_type=F32))
            dkt[step, :, :width] += jnp.dot(
                queries_t[h][:, rows], grad_scores, preferred_element_type=F32
            )
            dvt[step, :, :width] += jnp.dot(
                grads_t[h][:, rows], probs.astype(BF16), preferred_element_type=F32
            )
        query_sums.append(jnp.concatenate(found, axis=0))

    def gradient_pass(tile, carry):
        keys = kv_ref[key_rows(tile), :HEAD_DIM]
        result = []
        for h in range(2):
            grad_probs = jnp.dot(grads[h], vt[tile], preferred_element_type=F32)
            probs = probs_of(h, tile)
            grad_scores = (probs * (grad_probs - deltas[h])).astype(BF16)
            result.append(carry[h] + jnp.dot(grad_scores, keys, preferred_element_type=F32))
            dkt[tile] += jnp.dot(queries_t[h], grad_scores, preferred_element_type=F32)
            dvt[tile] += jnp.dot(grads_t[h], probs.astype(BF16), preferred_element_type=F32)
        return tuple(result)

    query_sums = lax.fori_loop(first, step, gradient_pass, tuple(query_sums))
    for h in range(2):
        at = h * HEAD_DIM
        held[step, :, at : at + HEAD_DIM] = outs[h]
        held[step, :, PAIR + at : PAIR + at + HEAD_DIM] = (query_sums[h] * factor).astype(BF16)

    def block_copy(block):
        rows = pl.ds(pl.multiple_of(block * BLOCK, BLOCK), BLOCK)
        return pltpu.make_async_copy(held.at[block], out_ref.at[rows, : 2 * PAIR], sems.at[block])

    block_copy(step).start()

    @pl.when(step == blocks - 1)
    def _():
        for tile in range(blocks):
            rows = slice(tile * BLOCK, (tile + 1) * BLOCK)
            tail[rows, :HEAD_DIM] = (dkt[tile] * factor).T.astype(BF16)
            tail[rows, HEAD_DIM:] = dvt[tile].T.astype(BF16)
        last = pltpu.make_async_copy(tail, out_ref.at[:, 2 * PAIR :], sems.at[blocks])
        last.start()
        for block in range(blocks):
            block_copy(block).wait()
        last.wait()


def attention(table, starts, ends):
    rows, width = table.shape
    blocks = rows // BLOCK
    tiles = blocks * (blocks + 1) // 2
    return pl.pallas_call(
        attention_kernel,
        out_shape=pltpu.HBM((rows, width), BF16),
        grid_spec=pltpu.PrefetchScalarGridSpec(
            num_scalar_prefetch=2,
            grid=(blocks,),
            in_specs=[
                pl.BlockSpec((BLOCK, PAIR), lambda i, *_: (i, 0)),
                pl.BlockSpec((BLOCK, PAIR), lambda i, *_: (i, 1)),
                pl.BlockSpec((rows, PAIR), lambda i, *_: (0, 2)),
            ],
            out_specs=pl.BlockSpec(memory_space=pl.ANY),
            scratch_shapes=[
                pltpu.VMEM((blocks, HEAD_DIM, BLOCK), BF16),
                pltpu.VMEM((blocks, HEAD_DIM, BLOCK), BF16),
                pltpu.VMEM((blocks, HEAD_DIM, BLOCK), F32),
                pltpu.VMEM((blocks, HEAD_DIM, BLOCK), F32),
                pltpu.VMEM((blocks, BLOCK, BLOCK), F32),
                pltpu.VMEM((blocks, BLOCK, BLOCK), F32),
                pltpu.VMEM((blocks, BLOCK, 2 * PAIR), BF16),
                pltpu.VMEM((rows, PAIR), BF16),
                pltpu.SemaphoreType.DMA((blocks + 1,)),
            ],
        ),
        compiler_params=pltpu.CompilerParams(vmem_limit_bytes=ATTENTION_VMEM_BYTES),
        cost_estimate=pl.CostEstimate(
            flops=tiles * 2 * 6 * 2 * BLOCK * BLOCK * HEAD_DIM,
            bytes_accessed=4 * rows * width,
            transcendentals=tiles * 2 * BLOCK * BLOCK,
        ),
    )(starts, ends, table, table, table)


def unrotated_pair(came_ref, piece, cosine, sine):
    heads = [
        rotated(came_ref[piece, :, at : at + HEAD_DIM].astype(F32), cosine, sine).astype(BF16)
        for at in (PAIR, PAIR + HEAD_DIM)
    ]
    return jnp.concatenate(heads, axis=1)


def query_kernel(
    came_ref, low_ref, up_ref, inputs_ref, cos_ref, sin_ref, term_ref, inputs, sem
):
    load = pltpu.make_async_copy(inputs_ref, inputs, sem)
    load.start()
    cosine = cos_ref[...]
    sine = -sin_ref[...]
    rank = up_ref.shape[0]
    low_t = low_ref[...].astype(F32).T.astype(BF16)
    dlow = jnp.zeros(low_ref.shape, F32)
    for piece in range(came_ref.shape[0]):
        columns = slice(piece * PAIR, (piece + 1) * PAIR)
        part = unrotated_pair(came_ref, piece, cosine, sine)
        dlow += lax.dot_general(
            part, up_ref[:, columns], (((1,), (1,)), ((), ())), preferred_element_type=F32
        )
        term_ref[piece, rank:] = jnp.dot(low_t, part, preferred_element_type=F32).astype(BF16)
    dlow_t = dlow.astype(BF16).astype(F32).T.astype(BF16)
    load.wait()
    for piece in range(came_ref.shape[0]):
        columns = slice(piece * PAIR, (piece + 1) * PAIR)
        term_ref[piece, :rank] = jnp.dot(
            dlow_t, inputs[:, columns], preferred_element_type=F32
        ).astype(BF16)


def finish_kernel(came_ref, cos_ref, sin_ref, out_ref, grad_ref):
    cosine = cos_ref[...]
    sine = -sin_ref[...]
    queries = out_ref.shape[1]
    kv_width = (grad_ref.shape[1] - queries) // 2
    for piece in range(came_ref.shape[0]):
        columns = slice(piece * PAIR, (piece + 1) * PAIR)
        out_ref[:, columns] = came_ref[piece, :, :PAIR]
        grad_ref[:, columns] = unrotated_pair(came_ref, piece, cosine, sine)
    for key_head in range(kv_width // HEAD_DIM):
        pair = (2 * key_head, 2 * key_head + 1)
        keys, values = (
            sum(came_ref[piece, :, at : at + HEAD_DIM].astype(F32) for piece in pair)
            for at in (2 * PAIR, 2 * PAIR + HEAD_DIM)
        )
        at = queries + key_head * HEAD_DIM
        grad_ref[:, at : at + HEAD_DIM] = rotated(keys, cosine, sine).astype(BF16)
        grad_ref[:, at + kv_width : at + kv_width + HEAD_DIM] = values.astype(BF16)


def unfold_kernel(whole_ref, first_ref, second_ref):
    rank = first_ref.shape[0]
    for piece in range(whole_ref.shape[0]):
        columns = slice(piece * PAIR, (piece + 1) * PAIR)
        first_ref[:, columns] = whole_ref[piece, :rank].astype(F32)
        second_ref[:, columns] = whole_ref[piece, rank:].astype(F32)


def in_hbm(table):
    return pltpu.with_memory_space_constraint(table, pltpu.HBM)


def exchange(table, axis):
    return lax.all_to_all(table, axis, split_axis=0, concat_axis=0, tiled=True)


def local(
    projection_rows, normed_input_rows, adapter_down, adapter_up, lengths, groups, output_gradient
):
    qkv_local = projection_rows[0]
    x_local = normed_input_rows[0]
    grad_raw = output_gradient[0]
    length_row = lengths[0]
    width_row = groups[0]
    token_count, model_width = x_local.shape
    qkv_width = qkv_local.shape[1]
    rank, query_columns = adapter_up.shape
    members = lax.axis_size("sub")
    half_index = lax.axis_index("half")
    group_index = half_index * members + lax.axis_index("sub")
    in_vmem = pl.BlockSpec(memory_space=pltpu.VMEM)
    in_place = pl.BlockSpec(memory_space=pl.ANY)
    wide = pl.pallas_call(
        widen_kernel,
        out_shape=pltpu.HBM((token_count, qkv_width + HEAD_DIM), BF16),
        in_specs=[in_place, in_place, in_place],
        out_specs=in_place,
        scratch_shapes=[
            pltpu.VMEM((token_count, model_width), BF16),
            pltpu.VMEM((rank, model_width), BF16),
            pltpu.VMEM((token_count, qkv_width + HEAD_DIM), BF16),
            pltpu.SemaphoreType.DMA((2 * CHUNKS + 1,)),
            pltpu.SemaphoreType.DMA((CHUNKS + 1,)),
        ],
        compiler_params=pltpu.CompilerParams(vmem_limit_bytes=VMEM_BYTES),
    )(in_hbm(x_local), in_hbm(adapter_down.T), in_hbm(qkv_local))
    packed_qkv = exchange(wide, "dp")
    packed_low = packed_qkv[:, qkv_width : qkv_width + rank]

    ends_dev = jnp.cumsum(width_row)
    starts_dev = ends_dev - width_row

    def owner_of(device):
        picked = (device[:, None] >= starts_dev[None, :]) & (device[:, None] < ends_dev[None, :])
        start = jnp.sum(jnp.where(picked, starts_dev[None, :], 0), axis=1)
        length = jnp.sum(jnp.where(picked, length_row[None, :], 0), axis=1)
        return start, length

    start_me, length_me = owner_of(group_index[None])
    row_at = jnp.arange(token_count, dtype=jnp.int32)
    local_offsets = (group_index - start_me) * token_count + row_at
    row_valid = (local_offsets < length_me).astype(jnp.int32)[:, None]
    cosine, sine = rope_tables(local_offsets)
    per_block = PART // token_count
    block_device = half_index * members + per_block * jnp.arange(
        members // per_block, dtype=jnp.int32
    )
    block_start, block_length = owner_of(block_device)
    first_rows = (block_start - half_index * members) * token_count
    starts = first_rows
    ends = first_rows + block_length

    params = pltpu.CompilerParams(vmem_limit_bytes=VMEM_BYTES)
    pieces = pl.pallas_call(
        prepare_kernel,
        out_shape=jax.ShapeDtypeStruct((members, token_count, PIECE), BF16),
        compiler_params=params,
    )(packed_qkv, adapter_up, cosine, sine, grad_raw, row_valid)
    table = in_hbm(exchange(pieces, "sub").reshape(members * token_count, PIECE))
    table, x_held = lax.optimization_barrier((table, x_local))
    packed_inputs = in_hbm(exchange(x_held, "dp"))
    results = attention(table, starts, ends)
    came = exchange(results.reshape(members, token_count, PIECE), "sub")
    terms = pl.pallas_call(
        query_kernel,
        out_shape=jax.ShapeDtypeStruct((members, 2 * rank, PAIR), BF16),
        in_specs=[in_vmem, in_vmem, in_vmem, in_place, in_vmem, in_vmem],
        scratch_shapes=[
            pltpu.VMEM((token_count, model_width), BF16),
            pltpu.SemaphoreType.DMA(()),
        ],
        compiler_params=params,
    )(came, packed_low, adapter_up, packed_inputs, cosine, sine)
    attn_rows, grad_rows = pl.pallas_call(
        finish_kernel,
        out_shape=(
            jax.ShapeDtypeStruct((token_count, query_columns), BF16),
            jax.ShapeDtypeStruct((token_count, qkv_width), BF16),
        ),
        compiler_params=params,
        cost_estimate=pl.CostEstimate(
            flops=token_count * qkv_width,
            bytes_accessed=8 * token_count * qkv_width,
            transcendentals=0,
        ),
    )(came, cosine, sine)
    total = jnp.sum(exchange(terms, "sub").astype(F32), axis=0)
    for axis, apart in (("half", 1), ("dp", 1), ("dp", 2), ("dp", 4)):
        size = lax.axis_size(axis)
        total = total + lax.ppermute(total, axis, [(i, i ^ apart) for i in range(size)])
    whole = exchange(jnp.broadcast_to(total.astype(BF16)[None], terms.shape), "sub")
    grad_a, grad_b = pl.pallas_call(
        unfold_kernel,
        out_shape=(
            jax.ShapeDtypeStruct((rank, model_width), F32),
            jax.ShapeDtypeStruct((rank, query_columns), F32),
        ),
        compiler_params=params,
    )(whole)
    return (attn_rows[None], grad_rows[None], grad_a.T, grad_b)


def solution(mesh):
    members, replicas = mesh.devices.shape
    split = Mesh(mesh.devices.reshape(2, members // 2, replicas), ("half", "sub", "dp"))
    rows = P("dp", ("half", "sub"), None)
    placed = (rows, rows, P(), P(), P("dp", None), P("dp", None), rows)
    return jax.shard_map(
        local,
        mesh=split,
        in_specs=placed,
        out_specs=(rows, rows, P(), P()),
        check_vma=False,
    )
```

```python
import math

import jax
import jax.numpy as jnp
from jax import lax
from jax.experimental import pallas as pl
from jax.experimental.pallas import tpu as pltpu
from jax.sharding import Mesh
from jax.sharding import PartitionSpec as P

HEAD_DIM = 128
HALF_DIM = HEAD_DIM // 2
PART = 256
BLOCK = 512
PAIR = 2 * HEAD_DIM
PIECE_IN = 2 * PAIR + HEAD_DIM
PIECE = 2 * PAIR + 2 * HEAD_DIM
rope_base = 500000.0
VMEM_BYTES = 48 * 1024 * 1024
ATTENTION_VMEM_BYTES = 65024 * 1024
HIDDEN = -1e30
CHUNKS = 4
F32 = jnp.float32
BF16 = jnp.bfloat16


def rope_tables(offsets):
    index_float = jnp.arange(HALF_DIM, dtype=F32)
    inverse = jnp.power(F32(rope_base), -index_float / HALF_DIM)
    angles = offsets.astype(F32)[:, None] * inverse[None, :]
    cosine, sine = jnp.cos(angles), jnp.sin(angles)
    return jnp.concatenate([cosine, cosine], axis=1), jnp.concatenate([-sine, sine], axis=1)


def rotated(table, cosine, sine):
    return table * cosine + pltpu.roll(table, HALF_DIM, 1) * sine


def widen_kernel(inputs_ref, down_ref, qkv_ref, out_ref, inputs, down, held, sems, moves):
    width = qkv_ref.shape[1]
    rank = down_ref.shape[0]

    def copies(source, target, span, use, first):
        size = span // CHUNKS
        return [
            pltpu.make_async_copy(
                source.at[:, part * size : (part + 1) * size],
                target.at[:, part * size : (part + 1) * size],
                use.at[first + part],
            )
            for part in range(CHUNKS)
        ]

    load_down = pltpu.make_async_copy(down_ref, down, sems.at[2 * CHUNKS])
    load_down.start()
    loads = copies(inputs_ref, inputs, inputs.shape[1], sems, 0)
    reads = copies(qkv_ref, held, width, sems, CHUNKS)
    writes = copies(held, out_ref, width, moves, 0)
    for load in loads + reads:
        load.start()
    low = jnp.zeros((inputs.shape[0], rank), F32)
    held[:, width:] = jnp.zeros((inputs.shape[0], HEAD_DIM), BF16)
    chunk = inputs.shape[1] // CHUNKS
    load_down.wait()
    for index, load in enumerate(loads):
        part = slice(index * chunk, (index + 1) * chunk)
        load.wait()
        low += lax.dot_general(
            inputs[:, part], down[:, part], (((1,), (1,)), ((), ())), preferred_element_type=F32
        )
        reads[index].wait()
        writes[index].start()
    held[:, width : width + rank] = low.astype(BF16)
    last = pltpu.make_async_copy(held.at[:, width:], out_ref.at[:, width:], moves.at[CHUNKS])
    last.start()
    for write in writes:
        write.wait()
    last.wait()


def prepare_kernel(qkv_ref, up_ref, cos_ref, sin_ref, grad_ref, valid_ref, out_ref):
    cosine = cos_ref[...]
    sine = sin_ref[...]
    kept = valid_ref[...] > 0
    rank, queries = up_ref.shape
    kv_width = (qkv_ref.shape[1] - HEAD_DIM - queries) // 2
    low_at = queries + 2 * kv_width
    low = qkv_ref[:, low_at : low_at + rank]
    pieces = out_ref.shape[0]
    for piece in range(pieces):
        columns = slice(piece * PAIR, (piece + 1) * PAIR)
        full = qkv_ref[:, columns].astype(F32) + jnp.dot(
            low, up_ref[:, columns], preferred_element_type=F32
        )
        for head in range(2):
            at = slice(head * HEAD_DIM, (head + 1) * HEAD_DIM)
            out_ref[piece, :, at] = rotated(full[:, at], cosine, sine).astype(BF16)
        grad = grad_ref[:, columns]
        out_ref[piece, :, PAIR : 2 * PAIR] = jnp.where(kept, grad, jnp.zeros_like(grad))
    for key_head in range(kv_width // HEAD_DIM):
        at = queries + key_head * HEAD_DIM
        keys = rotated(qkv_ref[:, at : at + HEAD_DIM].astype(F32), cosine, sine).astype(BF16)
        values = qkv_ref[:, at + kv_width : at + kv_width + HEAD_DIM]
        out_ref[2 * key_head, :, 2 * PAIR :] = keys
        out_ref[2 * key_head + 1, :, 2 * PAIR :] = values


def attention_kernel(
    start_ref,
    end_ref,
    side_ref,
    q_ref,
    g_ref,
    mine_ref,
    other_ref,
    out_ref,
    kv_ref,
    kt,
    vt,
    dkt,
    dvt,
    store0,
    store1,
    held,
    tail,
    sems,
):
    store = (store0, store1)
    step = pl.program_id(0)
    blocks = held.shape[0]
    factor = 1.0 / math.sqrt(HEAD_DIM)
    exponent = factor * math.log2(math.e)
    parts = BLOCK // PART

    def place(keys_ref, values_ref):
        for tile in range(blocks):
            rows = slice(tile * BLOCK, (tile + 1) * BLOCK)
            keys, values = keys_ref[rows], values_ref[rows]
            kv_ref[rows, :HEAD_DIM] = keys
            kv_ref[rows, HEAD_DIM:] = values
            kt[tile] = keys.T
            vt[tile] = values.T

    @pl.when((step == 0) & (side_ref[0] == 0))
    def _():
        place(mine_ref, other_ref)

    @pl.when((step == 0) & (side_ref[0] == 1))
    def _():
        place(other_ref, mine_ref)

    @pl.when(step == 0)
    def _():
        dkt[...] = jnp.zeros_like(dkt)
        dvt[...] = jnp.zeros_like(dvt)

    first = start_ref[step * parts] // BLOCK
    end_row = end_ref[step * parts]
    own = pl.multiple_of(step * BLOCK, BLOCK)
    column = lax.broadcasted_iota(jnp.int32, (1, BLOCK), 1)
    queries = [q_ref[:, h * HEAD_DIM : (h + 1) * HEAD_DIM] for h in range(2)]
    grads = [g_ref[:, h * HEAD_DIM : (h + 1) * HEAD_DIM] for h in range(2)]
    corners = [(slice(p * PART, (p + 1) * PART), (p + 1) * PART) for p in range(parts)]

    def folded(op, table):
        pieces = [table[:, c : c + HEAD_DIM] for c in range(0, table.shape[1], HEAD_DIM)]
        while len(pieces) > 1:
            pieces = [op(a, b) for a, b in zip(pieces[::2], pieces[1::2])]
        return pieces[0]

    def spread(table, width):
        return jnp.concatenate([table] * (width // HEAD_DIM), axis=1)

    def key_rows(tile):
        return pl.ds(pl.multiple_of(tile * BLOCK, BLOCK), BLOCK)

    def corner_allowed(p, width):
        low = start_ref[step * parts + p] - own
        high = end_ref[step * parts + p] - own
        row = lax.broadcasted_iota(jnp.int32, (PART, 1), 0) + p * PART
        at = column[:, :width]
        return (at == row) | ((at < row) & (at >= low) & (at < high))

    allowed = [corner_allowed(p, width) for p, (_, width) in enumerate(corners)]
    carry = []
    for h in range(2):
        highs, sums = [], []
        for p, (rows, width) in enumerate(corners):
            scores = jnp.dot(queries[h][rows], kt[step, :, :width], preferred_element_type=F32)
            scores = jnp.where(allowed[p], scores * exponent, HIDDEN)
            store[h][step, rows, :width] = scores
            highs.append(folded(jnp.maximum, scores))
            sums.append(folded(jnp.add, jnp.exp2(scores - spread(highs[-1], width))))
        carry += [jnp.concatenate(highs, axis=0), jnp.concatenate(sums, axis=0)]

    def score_pass(tile, carry):
        bias = jnp.where(tile * BLOCK + column < end_row, F32(0.0), F32(HIDDEN))
        result = []
        for h in range(2):
            top, total = carry[2 * h], carry[2 * h + 1]
            scores = jnp.dot(queries[h], kt[tile], preferred_element_type=F32) * exponent + bias
            store[h][tile] = scores
            higher = jnp.maximum(top, folded(jnp.maximum, scores))
            total = total * jnp.exp2(top - higher) + folded(
                jnp.add, jnp.exp2(scores - spread(higher, BLOCK))
            )
            result += [higher, total]
        return tuple(result)

    carry = lax.fori_loop(first, step, score_pass, tuple(carry))
    tops, inverse = [], []
    for h in range(2):
        lane_top, lane_total = carry[2 * h], carry[2 * h + 1]
        top = jnp.max(lane_top, axis=1, keepdims=True)
        total = jnp.sum(lane_total * jnp.exp2(lane_top - top), axis=1, keepdims=True)
        tops.append(top)
        inverse.append(1.0 / total)

    def corner_probs(h, rows, width):
        return jnp.exp2(store[h][step, rows, :width] - tops[h][rows]) * inverse[h][rows]

    def probs_of(h, tile):
        return jnp.exp2(store[h][tile] - tops[h]) * inverse[h]

    own_rows = key_rows(step)
    keys, values = kv_ref[own_rows, :HEAD_DIM], kv_ref[own_rows, HEAD_DIM:]
    sums = []
    for h in range(2):
        sums.append(
            jnp.concatenate(
                [
                    jnp.dot(
                        corner_probs(h, rows, width).astype(BF16),
                        values[:width],
                        preferred_element_type=F32,
                    )
                    for rows, width in corners
                ],
                axis=0,
            )
        )

    def out_pass(tile, carry):
        values = kv_ref[key_rows(tile), HEAD_DIM:]
        return tuple(
            carry[h]
            + jnp.dot(probs_of(h, tile).astype(BF16), values, preferred_element_type=F32)
            for h in range(2)
        )

    sums = lax.fori_loop(first, step, out_pass, tuple(sums))
    outs = [total.astype(BF16) for total in sums]
    deltas = [
        jnp.sum(grads[h].astype(F32) * outs[h].astype(F32), axis=1, keepdims=True) for h in range(2)
    ]
    queries_t = [table.T for table in queries]
    grads_t = [table.T for table in grads]

    query_sums = []
    for h in range(2):
        found = []
        for rows, width in corners:
            grad_probs = jnp.dot(grads[h][rows], vt[step, :, :width], preferred_element_type=F32)
            probs = corner_probs(h, rows, width)
            grad_scores = (probs * (grad_probs - deltas[h][rows])).astype(BF16)
            found.append(jnp.dot(grad_scores, keys[:width], preferred_element_type=F32))
            dkt[step, :, :width] += jnp.dot(
                queries_t[h][:, rows], grad_scores, preferred_element_type=F32
            )
            dvt[step, :, :width] += jnp.dot(
                grads_t[h][:, rows], probs.astype(BF16), preferred_element_type=F32
            )
        query_sums.append(jnp.concatenate(found, axis=0))

    def gradient_pass(tile, carry):
        keys = kv_ref[key_rows(tile), :HEAD_DIM]
        result = []
        for h in range(2):
            grad_probs = jnp.dot(grads[h], vt[tile], preferred_element_type=F32)
            probs = probs_of(h, tile)
            grad_scores = (probs * (grad_probs - deltas[h])).astype(BF16)
            result.append(carry[h] + jnp.dot(grad_scores, keys, preferred_element_type=F32))
            dkt[tile] += jnp.dot(queries_t[h], grad_scores, preferred_element_type=F32)
            dvt[tile] += jnp.dot(grads_t[h], probs.astype(BF16), preferred_element_type=F32)
        return tuple(result)

    query_sums = lax.fori_loop(first, step, gradient_pass, tuple(query_sums))
    for h in range(2):
        at = h * HEAD_DIM
        held[step, :, at : at + HEAD_DIM] = outs[h]
        held[step, :, PAIR + at : PAIR + at + HEAD_DIM] = (query_sums[h] * factor).astype(BF16)

    def block_copy(block):
        rows = pl.ds(pl.multiple_of(block * BLOCK, BLOCK), BLOCK)
        return pltpu.make_async_copy(held.at[block], out_ref.at[rows, : 2 * PAIR], sems.at[block])

    block_copy(step).start()

    @pl.when(step == blocks - 1)
    def _():
        for tile in range(blocks):
            rows = slice(tile * BLOCK, (tile + 1) * BLOCK)
            tail[rows, :HEAD_DIM] = (dkt[tile] * factor).T.astype(BF16)
            tail[rows, HEAD_DIM:] = dvt[tile].T.astype(BF16)
        last = pltpu.make_async_copy(tail, out_ref.at[:, 2 * PAIR :], sems.at[blocks])
        last.start()
        for block in range(blocks):
            block_copy(block).wait()
        last.wait()


def attention(table, other, starts, ends, side):
    rows, width = table.shape[0], PIECE
    blocks = rows // BLOCK
    tiles = blocks * (blocks + 1) // 2
    return pl.pallas_call(
        attention_kernel,
        out_shape=pltpu.HBM((rows, width), BF16),
        grid_spec=pltpu.PrefetchScalarGridSpec(
            num_scalar_prefetch=3,
            grid=(blocks,),
            in_specs=[
                pl.BlockSpec((BLOCK, PAIR), lambda i, *_: (i, 0)),
                pl.BlockSpec((BLOCK, PAIR), lambda i, *_: (i, 1)),
                pl.BlockSpec((rows, HEAD_DIM), lambda i, *_: (0, 2 * PAIR // HEAD_DIM)),
                pl.BlockSpec((rows, HEAD_DIM), lambda i, *_: (0, 0)),
            ],
            out_specs=pl.BlockSpec(memory_space=pl.ANY),
            scratch_shapes=[
                pltpu.VMEM((rows, PAIR), BF16),
                pltpu.VMEM((blocks, HEAD_DIM, BLOCK), BF16),
                pltpu.VMEM((blocks, HEAD_DIM, BLOCK), BF16),
                pltpu.VMEM((blocks, HEAD_DIM, BLOCK), F32),
                pltpu.VMEM((blocks, HEAD_DIM, BLOCK), F32),
                pltpu.VMEM((blocks, BLOCK, BLOCK), F32),
                pltpu.VMEM((blocks, BLOCK, BLOCK), F32),
                pltpu.VMEM((blocks, BLOCK, 2 * PAIR), BF16),
                pltpu.VMEM((rows, PAIR), BF16),
                pltpu.SemaphoreType.DMA((blocks + 1,)),
            ],
        ),
        compiler_params=pltpu.CompilerParams(vmem_limit_bytes=ATTENTION_VMEM_BYTES),
        cost_estimate=pl.CostEstimate(
            flops=tiles * 2 * 6 * 2 * BLOCK * BLOCK * HEAD_DIM,
            bytes_accessed=4 * rows * width,
            transcendentals=tiles * 2 * BLOCK * BLOCK,
        ),
    )(starts, ends, side, table, table, table, other)


def unrotated_pair(came_ref, piece, cosine, sine):
    heads = [
        rotated(came_ref[piece, :, at : at + HEAD_DIM].astype(F32), cosine, sine).astype(BF16)
        for at in (PAIR, PAIR + HEAD_DIM)
    ]
    return jnp.concatenate(heads, axis=1)


def query_kernel(
    came_ref, low_ref, up_ref, inputs_ref, cos_ref, sin_ref, term_ref, inputs, sem
):
    load = pltpu.make_async_copy(inputs_ref, inputs, sem)
    load.start()
    cosine = cos_ref[...]
    sine = -sin_ref[...]
    rank = up_ref.shape[0]
    low_t = low_ref[...].astype(F32).T.astype(BF16)
    dlow = jnp.zeros(low_ref.shape, F32)
    for piece in range(came_ref.shape[0]):
        columns = slice(piece * PAIR, (piece + 1) * PAIR)
        part = unrotated_pair(came_ref, piece, cosine, sine)
        dlow += lax.dot_general(
            part, up_ref[:, columns], (((1,), (1,)), ((), ())), preferred_element_type=F32
        )
        term_ref[piece, rank:] = jnp.dot(low_t, part, preferred_element_type=F32).astype(BF16)
    dlow_t = dlow.astype(BF16).astype(F32).T.astype(BF16)
    load.wait()
    for piece in range(came_ref.shape[0]):
        columns = slice(piece * PAIR, (piece + 1) * PAIR)
        term_ref[piece, :rank] = jnp.dot(
            dlow_t, inputs[:, columns], preferred_element_type=F32
        ).astype(BF16)


def finish_kernel(came_ref, cos_ref, sin_ref, out_ref, grad_ref):
    cosine = cos_ref[...]
    sine = -sin_ref[...]
    queries = out_ref.shape[1]
    kv_width = (grad_ref.shape[1] - queries) // 2
    for piece in range(came_ref.shape[0]):
        columns = slice(piece * PAIR, (piece + 1) * PAIR)
        out_ref[:, columns] = came_ref[piece, :, :PAIR]
        grad_ref[:, columns] = unrotated_pair(came_ref, piece, cosine, sine)
    for key_head in range(kv_width // HEAD_DIM):
        pair = (2 * key_head, 2 * key_head + 1)
        keys, values = (
            sum(came_ref[piece, :, at : at + HEAD_DIM].astype(F32) for piece in pair)
            for at in (2 * PAIR, 2 * PAIR + HEAD_DIM)
        )
        at = queries + key_head * HEAD_DIM
        grad_ref[:, at : at + HEAD_DIM] = rotated(keys, cosine, sine).astype(BF16)
        grad_ref[:, at + kv_width : at + kv_width + HEAD_DIM] = values.astype(BF16)


def unfold_kernel(whole_ref, first_ref, second_ref):
    rank = first_ref.shape[0]
    for piece in range(whole_ref.shape[0]):
        columns = slice(piece * PAIR, (piece + 1) * PAIR)
        first_ref[:, columns] = whole_ref[piece, :rank].astype(F32)
        second_ref[:, columns] = whole_ref[piece, rank:].astype(F32)


def in_hbm(table):
    return pltpu.with_memory_space_constraint(table, pltpu.HBM)


def exchange(table, axis):
    return lax.all_to_all(table, axis, split_axis=0, concat_axis=0, tiled=True)


def local(
    projection_rows, normed_input_rows, adapter_down, adapter_up, lengths, groups, output_gradient
):
    qkv_local = projection_rows[0]
    x_local = normed_input_rows[0]
    grad_raw = output_gradient[0]
    length_row = lengths[0]
    width_row = groups[0]
    token_count, model_width = x_local.shape
    qkv_width = qkv_local.shape[1]
    rank, query_columns = adapter_up.shape
    members = lax.axis_size("sub")
    half_index = lax.axis_index("half")
    group_index = half_index * members + lax.axis_index("sub")
    in_vmem = pl.BlockSpec(memory_space=pltpu.VMEM)
    in_place = pl.BlockSpec(memory_space=pl.ANY)
    wide = pl.pallas_call(
        widen_kernel,
        out_shape=pltpu.HBM((token_count, qkv_width + HEAD_DIM), BF16),
        in_specs=[in_place, in_place, in_place],
        out_specs=in_place,
        scratch_shapes=[
            pltpu.VMEM((token_count, model_width), BF16),
            pltpu.VMEM((rank, model_width), BF16),
            pltpu.VMEM((token_count, qkv_width + HEAD_DIM), BF16),
            pltpu.SemaphoreType.DMA((2 * CHUNKS + 1,)),
            pltpu.SemaphoreType.DMA((CHUNKS + 1,)),
        ],
        compiler_params=pltpu.CompilerParams(vmem_limit_bytes=VMEM_BYTES),
    )(in_hbm(x_local), in_hbm(adapter_down.T), in_hbm(qkv_local))
    packed_qkv = exchange(wide, "dp")
    packed_low = packed_qkv[:, qkv_width : qkv_width + rank]

    ends_dev = jnp.cumsum(width_row)
    starts_dev = ends_dev - width_row

    def owner_of(device):
        picked = (device[:, None] >= starts_dev[None, :]) & (device[:, None] < ends_dev[None, :])
        start = jnp.sum(jnp.where(picked, starts_dev[None, :], 0), axis=1)
        length = jnp.sum(jnp.where(picked, length_row[None, :], 0), axis=1)
        return start, length

    start_me, length_me = owner_of(group_index[None])
    row_at = jnp.arange(token_count, dtype=jnp.int32)
    local_offsets = (group_index - start_me) * token_count + row_at
    row_valid = (local_offsets < length_me).astype(jnp.int32)[:, None]
    cosine, sine = rope_tables(local_offsets)
    per_block = PART // token_count
    block_device = half_index * members + per_block * jnp.arange(
        members // per_block, dtype=jnp.int32
    )
    block_start, block_length = owner_of(block_device)
    first_rows = (block_start - half_index * members) * token_count
    starts = first_rows
    ends = first_rows + block_length

    params = pltpu.CompilerParams(vmem_limit_bytes=VMEM_BYTES)
    pieces = pl.pallas_call(
        prepare_kernel,
        out_shape=jax.ShapeDtypeStruct((members, token_count, PIECE_IN), BF16),
        compiler_params=params,
    )(packed_qkv, adapter_up, cosine, sine, grad_raw, row_valid)
    table = exchange(pieces, "sub").reshape(members * token_count, PIECE_IN)
    table, x_held = lax.optimization_barrier((table, x_local))
    packed_inputs = in_hbm(exchange(x_held, "dp"))
    other = lax.ppermute(table[:, 2 * PAIR :], "sub", [(i, i ^ 1) for i in range(members)])
    side = lax.axis_index("sub").astype(jnp.int32).reshape(1) % 2
    results = attention(in_hbm(table), other, starts, ends, side)
    came = exchange(results.reshape(members, token_count, PIECE), "sub")
    terms = pl.pallas_call(
        query_kernel,
        out_shape=jax.ShapeDtypeStruct((members, 2 * rank, PAIR), BF16),
        in_specs=[in_vmem, in_vmem, in_vmem, in_place, in_vmem, in_vmem],
        scratch_shapes=[
            pltpu.VMEM((token_count, model_width), BF16),
            pltpu.SemaphoreType.DMA(()),
        ],
        compiler_params=params,
    )(came, packed_low, adapter_up, packed_inputs, cosine, sine)
    attn_rows, grad_rows = pl.pallas_call(
        finish_kernel,
        out_shape=(
            jax.ShapeDtypeStruct((token_count, query_columns), BF16),
            jax.ShapeDtypeStruct((token_count, qkv_width), BF16),
        ),
        compiler_params=params,
        cost_estimate=pl.CostEstimate(
            flops=token_count * qkv_width,
            bytes_accessed=8 * token_count * qkv_width,
            transcendentals=0,
        ),
    )(came, cosine, sine)
    total = jnp.sum(exchange(terms, "sub").astype(F32), axis=0)
    for axis, apart in (("half", 1), ("dp", 1), ("dp", 2), ("dp", 4)):
        size = lax.axis_size(axis)
        total = total + lax.ppermute(total, axis, [(i, i ^ apart) for i in range(size)])
    whole = exchange(jnp.broadcast_to(total.astype(BF16)[None], terms.shape), "sub")
    grad_a, grad_b = pl.pallas_call(
        unfold_kernel,
        out_shape=(
            jax.ShapeDtypeStruct((rank, model_width), F32),
            jax.ShapeDtypeStruct((rank, query_columns), F32),
        ),
        compiler_params=params,
    )(whole)
    return (attn_rows[None], grad_rows[None], grad_a.T, grad_b)


def solution(mesh):
    members, replicas = mesh.devices.shape
    split = Mesh(mesh.devices.reshape(2, members // 2, replicas), ("half", "sub", "dp"))
    rows = P("dp", ("half", "sub"), None)
    placed = (rows, rows, P(), P(), P("dp", None), P("dp", None), rows)
    return jax.shard_map(
        local,
        mesh=split,
        in_specs=placed,
        out_specs=(rows, rows, P(), P()),
        check_vma=False,
    )
```

```python
import math

import jax
import jax.numpy as jnp
from jax import lax
from jax.experimental import pallas as pl
from jax.experimental.pallas import tpu as pltpu
from jax.sharding import Mesh
from jax.sharding import PartitionSpec as P

HEAD_DIM = 128
HALF_DIM = HEAD_DIM // 2
PART = 256
BLOCK = 512
PAIR = 2 * HEAD_DIM
PIECE_IN = 2 * PAIR + HEAD_DIM
PIECE = 2 * PAIR + 2 * HEAD_DIM
rope_base = 500000.0
VMEM_BYTES = 48 * 1024 * 1024
ATTENTION_VMEM_BYTES = 64768 * 1024
HIDDEN = -1e30
CHUNKS = 4
F32 = jnp.float32
BF16 = jnp.bfloat16


def rope_tables(offsets):
    index_float = jnp.arange(HALF_DIM, dtype=F32)
    inverse = jnp.power(F32(rope_base), -index_float / HALF_DIM)
    angles = offsets.astype(F32)[:, None] * inverse[None, :]
    cosine, sine = jnp.cos(angles), jnp.sin(angles)
    return jnp.concatenate([cosine, cosine], axis=1), jnp.concatenate([-sine, sine], axis=1)


def rotated(table, cosine, sine):
    return table * cosine + pltpu.roll(table, HALF_DIM, 1) * sine


def widen_kernel(inputs_ref, down_ref, qkv_ref, out_ref, inputs, down, held, sems, moves):
    width = qkv_ref.shape[1]
    rank = down_ref.shape[0]

    def copies(source, target, span, use, first):
        size = span // CHUNKS
        return [
            pltpu.make_async_copy(
                source.at[:, part * size : (part + 1) * size],
                target.at[:, part * size : (part + 1) * size],
                use.at[first + part],
            )
            for part in range(CHUNKS)
        ]

    load_down = pltpu.make_async_copy(down_ref, down, sems.at[2 * CHUNKS])
    load_down.start()
    loads = copies(inputs_ref, inputs, inputs.shape[1], sems, 0)
    reads = copies(qkv_ref, held, width, sems, CHUNKS)
    writes = copies(held, out_ref, width, moves, 0)
    for load in loads + reads:
        load.start()
    low = jnp.zeros((inputs.shape[0], rank), F32)
    held[:, width:] = jnp.zeros((inputs.shape[0], HEAD_DIM), BF16)
    chunk = inputs.shape[1] // CHUNKS
    load_down.wait()
    for index, load in enumerate(loads):
        part = slice(index * chunk, (index + 1) * chunk)
        load.wait()
        low += lax.dot_general(
            inputs[:, part], down[:, part], (((1,), (1,)), ((), ())), preferred_element_type=F32
        )
        reads[index].wait()
        writes[index].start()
    held[:, width : width + rank] = low.astype(BF16)
    last = pltpu.make_async_copy(held.at[:, width:], out_ref.at[:, width:], moves.at[CHUNKS])
    last.start()
    for write in writes:
        write.wait()
    last.wait()


def prepare_kernel(qkv_ref, up_ref, cos_ref, sin_ref, grad_ref, valid_ref, out_ref):
    cosine = cos_ref[...]
    sine = sin_ref[...]
    kept = valid_ref[...] > 0
    rank, queries = up_ref.shape
    kv_width = (qkv_ref.shape[1] - HEAD_DIM - queries) // 2
    low_at = queries + 2 * kv_width
    low = qkv_ref[:, low_at : low_at + rank]
    pieces = out_ref.shape[0]
    for piece in range(pieces):
        columns = slice(piece * PAIR, (piece + 1) * PAIR)
        full = qkv_ref[:, columns].astype(F32) + jnp.dot(
            low, up_ref[:, columns], preferred_element_type=F32
        )
        for head in range(2):
            at = slice(head * HEAD_DIM, (head + 1) * HEAD_DIM)
            out_ref[piece, :, at] = rotated(full[:, at], cosine, sine).astype(BF16)
        grad = grad_ref[:, columns]
        out_ref[piece, :, PAIR : 2 * PAIR] = jnp.where(kept, grad, jnp.zeros_like(grad))
    for key_head in range(kv_width // HEAD_DIM):
        at = queries + key_head * HEAD_DIM
        keys = rotated(qkv_ref[:, at : at + HEAD_DIM].astype(F32), cosine, sine).astype(BF16)
        values = qkv_ref[:, at + kv_width : at + kv_width + HEAD_DIM]
        out_ref[2 * key_head, :, 2 * PAIR :] = keys
        out_ref[2 * key_head + 1, :, 2 * PAIR :] = values


def attention_kernel(
    start_ref,
    end_ref,
    side_ref,
    q_ref,
    g_ref,
    mine_ref,
    other_ref,
    out_ref,
    kv_ref,
    kt,
    vt,
    dkt,
    dvt,
    store0,
    store1,
    held,
    tail,
    sems,
):
    store = (store0, store1)
    step = pl.program_id(0)
    blocks = held.shape[0]
    factor = 1.0 / math.sqrt(HEAD_DIM)
    exponent = factor * math.log2(math.e)
    parts = BLOCK // PART

    def place(keys_ref, values_ref):
        for tile in range(blocks):
            rows = slice(tile * BLOCK, (tile + 1) * BLOCK)
            keys, values = keys_ref[rows], values_ref[rows]
            kv_ref[rows, :HEAD_DIM] = keys
            kv_ref[rows, HEAD_DIM:] = values
            kt[tile] = keys.T
            vt[tile] = values.T

    @pl.when((step == 0) & (side_ref[0] == 0))
    def _():
        place(mine_ref, other_ref)

    @pl.when((step == 0) & (side_ref[0] == 1))
    def _():
        place(other_ref, mine_ref)

    @pl.when(step == 0)
    def _():
        dkt[...] = jnp.zeros_like(dkt)
        dvt[...] = jnp.zeros_like(dvt)

    first = start_ref[step * parts] // BLOCK
    end_row = end_ref[step * parts]
    own = pl.multiple_of(step * BLOCK, BLOCK)
    column = lax.broadcasted_iota(jnp.int32, (1, BLOCK), 1)
    queries = [q_ref[:, h * HEAD_DIM : (h + 1) * HEAD_DIM] for h in range(2)]
    grads = [g_ref[:, h * HEAD_DIM : (h + 1) * HEAD_DIM] for h in range(2)]
    corners = [(slice(p * PART, (p + 1) * PART), (p + 1) * PART) for p in range(parts)]

    def folded(op, table):
        pieces = [table[:, c : c + HEAD_DIM] for c in range(0, table.shape[1], HEAD_DIM)]
        while len(pieces) > 1:
            pieces = [op(a, b) for a, b in zip(pieces[::2], pieces[1::2])]
        return pieces[0]

    def spread(table, width):
        return jnp.concatenate([table] * (width // HEAD_DIM), axis=1)

    def key_rows(tile):
        return pl.ds(pl.multiple_of(tile * BLOCK, BLOCK), BLOCK)

    def corner_allowed(p, width):
        low = start_ref[step * parts + p] - own
        high = end_ref[step * parts + p] - own
        row = lax.broadcasted_iota(jnp.int32, (PART, 1), 0) + p * PART
        at = column[:, :width]
        return (at == row) | ((at < row) & (at >= low) & (at < high))

    allowed = [corner_allowed(p, width) for p, (_, width) in enumerate(corners)]
    carry = []
    for h in range(2):
        highs, sums = [], []
        for p, (rows, width) in enumerate(corners):
            scores = jnp.dot(queries[h][rows], kt[step, :, :width], preferred_element_type=F32)
            scores = jnp.where(allowed[p], scores * exponent, HIDDEN)
            store[h][step, rows, :width] = scores
            highs.append(folded(jnp.maximum, scores))
            sums.append(folded(jnp.add, jnp.exp2(scores - spread(highs[-1], width))))
        carry += [jnp.concatenate(highs, axis=0), jnp.concatenate(sums, axis=0)]

    def score_pass(tile, carry):
        bias = jnp.where(tile * BLOCK + column < end_row, F32(0.0), F32(HIDDEN))
        result = []
        for h in range(2):
            top, total = carry[2 * h], carry[2 * h + 1]
            scores = jnp.dot(queries[h], kt[tile], preferred_element_type=F32) * exponent + bias
            store[h][tile] = scores
            higher = jnp.maximum(top, folded(jnp.maximum, scores))
            total = total * jnp.exp2(top - higher) + folded(
                jnp.add, jnp.exp2(scores - spread(higher, BLOCK))
            )
            result += [higher, total]
        return tuple(result)

    carry = lax.fori_loop(first, step, score_pass, tuple(carry))
    tops, inverse = [], []
    for h in range(2):
        lane_top, lane_total = carry[2 * h], carry[2 * h + 1]
        top = jnp.max(lane_top, axis=1, keepdims=True)
        total = jnp.sum(lane_total * jnp.exp2(lane_top - top), axis=1, keepdims=True)
        tops.append(top)
        inverse.append(1.0 / total)

    def corner_probs(h, rows, width):
        return jnp.exp2(store[h][step, rows, :width] - tops[h][rows]) * inverse[h][rows]

    def probs_of(h, tile):
        return jnp.exp2(store[h][tile] - tops[h]) * inverse[h]

    own_rows = key_rows(step)
    keys, values = kv_ref[own_rows, :HEAD_DIM], kv_ref[own_rows, HEAD_DIM:]
    sums = []
    for h in range(2):
        sums.append(
            jnp.concatenate(
                [
                    jnp.dot(
                        corner_probs(h, rows, width).astype(BF16),
                        values[:width],
                        preferred_element_type=F32,
                    )
                    for rows, width in corners
                ],
                axis=0,
            )
        )

    def out_pass(tile, carry):
        values = kv_ref[key_rows(tile), HEAD_DIM:]
        return tuple(
            carry[h]
            + jnp.dot(probs_of(h, tile).astype(BF16), values, preferred_element_type=F32)
            for h in range(2)
        )

    sums = lax.fori_loop(first, step, out_pass, tuple(sums))
    outs = [total.astype(BF16) for total in sums]
    deltas = [
        jnp.sum(grads[h].astype(F32) * outs[h].astype(F32), axis=1, keepdims=True) for h in range(2)
    ]
    queries_t = [table.T for table in queries]
    grads_t = [table.T for table in grads]

    query_sums = []
    for h in range(2):
        found = []
        for rows, width in corners:
            grad_probs = jnp.dot(grads[h][rows], vt[step, :, :width], preferred_element_type=F32)
            probs = corner_probs(h, rows, width)
            grad_scores = (probs * (grad_probs - deltas[h][rows])).astype(BF16)
            found.append(jnp.dot(grad_scores, keys[:width], preferred_element_type=F32))
            dkt[step, :, :width] += jnp.dot(
                queries_t[h][:, rows], grad_scores, preferred_element_type=F32
            )
            dvt[step, :, :width] += jnp.dot(
                grads_t[h][:, rows], probs.astype(BF16), preferred_element_type=F32
            )
        query_sums.append(jnp.concatenate(found, axis=0))

    def gradient_pass(tile, carry):
        keys = kv_ref[key_rows(tile), :HEAD_DIM]
        result = []
        for h in range(2):
            grad_probs = jnp.dot(grads[h], vt[tile], preferred_element_type=F32)
            probs = probs_of(h, tile)
            grad_scores = (probs * (grad_probs - deltas[h])).astype(BF16)
            result.append(carry[h] + jnp.dot(grad_scores, keys, preferred_element_type=F32))
            dkt[tile] += jnp.dot(queries_t[h], grad_scores, preferred_element_type=F32)
            dvt[tile] += jnp.dot(grads_t[h], probs.astype(BF16), preferred_element_type=F32)
        return tuple(result)

    query_sums = lax.fori_loop(first, step, gradient_pass, tuple(query_sums))
    for h in range(2):
        at = h * HEAD_DIM
        held[step, :, at : at + HEAD_DIM] = outs[h]
        held[step, :, PAIR + at : PAIR + at + HEAD_DIM] = (query_sums[h] * factor).astype(BF16)

    def block_copy(block):
        rows = pl.ds(pl.multiple_of(block * BLOCK, BLOCK), BLOCK)
        return pltpu.make_async_copy(held.at[block], out_ref.at[rows, : 2 * PAIR], sems.at[block])

    block_copy(step).start()

    @pl.when(step == blocks - 1)
    def _():
        for tile in range(blocks):
            rows = slice(tile * BLOCK, (tile + 1) * BLOCK)
            tail[rows, :HEAD_DIM] = (dkt[tile] * factor).T.astype(BF16)
            tail[rows, HEAD_DIM:] = dvt[tile].T.astype(BF16)
        last = pltpu.make_async_copy(tail, out_ref.at[:, 2 * PAIR :], sems.at[blocks])
        last.start()
        for block in range(blocks):
            block_copy(block).wait()
        last.wait()


def attention(table, other, starts, ends, side):
    rows, width = table.shape[0], PIECE
    blocks = rows // BLOCK
    tiles = blocks * (blocks + 1) // 2
    return pl.pallas_call(
        attention_kernel,
        out_shape=pltpu.HBM((rows, width), BF16),
        grid_spec=pltpu.PrefetchScalarGridSpec(
            num_scalar_prefetch=3,
            grid=(blocks,),
            in_specs=[
                pl.BlockSpec((BLOCK, PAIR), lambda i, *_: (i, 0)),
                pl.BlockSpec((BLOCK, PAIR), lambda i, *_: (i, 1)),
                pl.BlockSpec((rows, HEAD_DIM), lambda i, *_: (0, 2 * PAIR // HEAD_DIM)),
                pl.BlockSpec((rows, HEAD_DIM), lambda i, *_: (0, 0)),
            ],
            out_specs=pl.BlockSpec(memory_space=pl.ANY),
            scratch_shapes=[
                pltpu.VMEM((rows, PAIR), BF16),
                pltpu.VMEM((blocks, HEAD_DIM, BLOCK), BF16),
                pltpu.VMEM((blocks, HEAD_DIM, BLOCK), BF16),
                pltpu.VMEM((blocks, HEAD_DIM, BLOCK), F32),
                pltpu.VMEM((blocks, HEAD_DIM, BLOCK), F32),
                pltpu.VMEM((blocks, BLOCK, BLOCK), F32),
                pltpu.VMEM((blocks, BLOCK, BLOCK), F32),
                pltpu.VMEM((blocks, BLOCK, 2 * PAIR), BF16),
                pltpu.VMEM((rows, PAIR), BF16),
                pltpu.SemaphoreType.DMA((blocks + 1,)),
            ],
        ),
        compiler_params=pltpu.CompilerParams(vmem_limit_bytes=ATTENTION_VMEM_BYTES),
        cost_estimate=pl.CostEstimate(
            flops=tiles * 2 * 6 * 2 * BLOCK * BLOCK * HEAD_DIM,
            bytes_accessed=4 * rows * width,
            transcendentals=tiles * 2 * BLOCK * BLOCK,
        ),
    )(starts, ends, side, table, table, table, other)


def unrotated_pair(came_ref, piece, cosine, sine):
    heads = [
        rotated(came_ref[piece, :, at : at + HEAD_DIM].astype(F32), cosine, sine).astype(BF16)
        for at in (PAIR, PAIR + HEAD_DIM)
    ]
    return jnp.concatenate(heads, axis=1)


def query_kernel(
    came_ref, low_ref, up_ref, inputs_ref, cos_ref, sin_ref, term_ref, inputs, sem
):
    load = pltpu.make_async_copy(inputs_ref, inputs, sem)
    load.start()
    cosine = cos_ref[...]
    sine = -sin_ref[...]
    rank = up_ref.shape[0]
    low_t = low_ref[...].astype(F32).T.astype(BF16)
    dlow = jnp.zeros(low_ref.shape, F32)
    for piece in range(came_ref.shape[0]):
        columns = slice(piece * PAIR, (piece + 1) * PAIR)
        part = unrotated_pair(came_ref, piece, cosine, sine)
        dlow += lax.dot_general(
            part, up_ref[:, columns], (((1,), (1,)), ((), ())), preferred_element_type=F32
        )
        term_ref[piece, rank:] = jnp.dot(low_t, part, preferred_element_type=F32).astype(BF16)
    dlow_t = dlow.astype(BF16).astype(F32).T.astype(BF16)
    load.wait()
    for piece in range(came_ref.shape[0]):
        columns = slice(piece * PAIR, (piece + 1) * PAIR)
        term_ref[piece, :rank] = jnp.dot(
            dlow_t, inputs[:, columns], preferred_element_type=F32
        ).astype(BF16)


def finish_kernel(came_ref, cos_ref, sin_ref, out_ref, grad_ref):
    cosine = cos_ref[...]
    sine = -sin_ref[...]
    queries = out_ref.shape[1]
    kv_width = (grad_ref.shape[1] - queries) // 2
    for piece in range(came_ref.shape[0]):
        columns = slice(piece * PAIR, (piece + 1) * PAIR)
        out_ref[:, columns] = came_ref[piece, :, :PAIR]
        grad_ref[:, columns] = unrotated_pair(came_ref, piece, cosine, sine)
    for key_head in range(kv_width // HEAD_DIM):
        pair = (2 * key_head, 2 * key_head + 1)
        keys, values = (
            sum(came_ref[piece, :, at : at + HEAD_DIM].astype(F32) for piece in pair)
            for at in (2 * PAIR, 2 * PAIR + HEAD_DIM)
        )
        at = queries + key_head * HEAD_DIM
        grad_ref[:, at : at + HEAD_DIM] = rotated(keys, cosine, sine).astype(BF16)
        grad_ref[:, at + kv_width : at + kv_width + HEAD_DIM] = values.astype(BF16)


def unfold_kernel(whole_ref, first_ref, second_ref):
    rank = first_ref.shape[0]
    for piece in range(whole_ref.shape[0]):
        columns = slice(piece * PAIR, (piece + 1) * PAIR)
        first_ref[:, columns] = whole_ref[piece, :rank].astype(F32)
        second_ref[:, columns] = whole_ref[piece, rank:].astype(F32)


def in_hbm(table):
    return pltpu.with_memory_space_constraint(table, pltpu.HBM)


def exchange(table, axis):
    return lax.all_to_all(table, axis, split_axis=0, concat_axis=0, tiled=True)


def local(
    projection_rows, normed_input_rows, adapter_down, adapter_up, lengths, groups, output_gradient
):
    qkv_local = projection_rows[0]
    x_local = normed_input_rows[0]
    grad_raw = output_gradient[0]
    length_row = lengths[0]
    width_row = groups[0]
    token_count, model_width = x_local.shape
    qkv_width = qkv_local.shape[1]
    rank, query_columns = adapter_up.shape
    members = lax.axis_size("sub")
    half_index = lax.axis_index("half")
    group_index = half_index * members + lax.axis_index("sub")
    in_vmem = pl.BlockSpec(memory_space=pltpu.VMEM)
    in_place = pl.BlockSpec(memory_space=pl.ANY)
    wide = pl.pallas_call(
        widen_kernel,
        out_shape=pltpu.HBM((token_count, qkv_width + HEAD_DIM), BF16),
        in_specs=[in_place, in_place, in_place],
        out_specs=in_place,
        scratch_shapes=[
            pltpu.VMEM((token_count, model_width), BF16),
            pltpu.VMEM((rank, model_width), BF16),
            pltpu.VMEM((token_count, qkv_width + HEAD_DIM), BF16),
            pltpu.SemaphoreType.DMA((2 * CHUNKS + 1,)),
            pltpu.SemaphoreType.DMA((CHUNKS + 1,)),
        ],
        compiler_params=pltpu.CompilerParams(vmem_limit_bytes=VMEM_BYTES),
    )(in_hbm(x_local), in_hbm(adapter_down.T), in_hbm(qkv_local))
    packed_qkv = exchange(wide, "dp")
    packed_low = packed_qkv[:, qkv_width : qkv_width + rank]

    ends_dev = jnp.cumsum(width_row)
    starts_dev = ends_dev - width_row

    def owner_of(device):
        picked = (device[:, None] >= starts_dev[None, :]) & (device[:, None] < ends_dev[None, :])
        start = jnp.sum(jnp.where(picked, starts_dev[None, :], 0), axis=1)
        length = jnp.sum(jnp.where(picked, length_row[None, :], 0), axis=1)
        return start, length

    start_me, length_me = owner_of(group_index[None])
    row_at = jnp.arange(token_count, dtype=jnp.int32)
    local_offsets = (group_index - start_me) * token_count + row_at
    row_valid = (local_offsets < length_me).astype(jnp.int32)[:, None]
    cosine, sine = rope_tables(local_offsets)
    per_block = PART // token_count
    block_device = half_index * members + per_block * jnp.arange(
        members // per_block, dtype=jnp.int32
    )
    block_start, block_length = owner_of(block_device)
    first_rows = (block_start - half_index * members) * token_count
    starts = first_rows
    ends = first_rows + block_length

    params = pltpu.CompilerParams(vmem_limit_bytes=VMEM_BYTES)
    pieces = pl.pallas_call(
        prepare_kernel,
        out_shape=jax.ShapeDtypeStruct((members, token_count, PIECE_IN), BF16),
        compiler_params=params,
    )(packed_qkv, adapter_up, cosine, sine, grad_raw, row_valid)
    table = exchange(pieces, "sub").reshape(members * token_count, PIECE_IN)
    mine, x_held = lax.optimization_barrier((table[:, 2 * PAIR :], x_local))
    packed_inputs = in_hbm(exchange(x_held, "dp"))
    other = lax.ppermute(mine, "sub", [(i, i ^ 1) for i in range(members)])
    side = lax.axis_index("sub").astype(jnp.int32).reshape(1) % 2
    results = attention(in_hbm(table), other, starts, ends, side)
    came = exchange(results.reshape(members, token_count, PIECE), "sub")
    terms = pl.pallas_call(
        query_kernel,
        out_shape=jax.ShapeDtypeStruct((members, 2 * rank, PAIR), BF16),
        in_specs=[in_vmem, in_vmem, in_vmem, in_place, in_vmem, in_vmem],
        scratch_shapes=[
            pltpu.VMEM((token_count, model_width), BF16),
            pltpu.SemaphoreType.DMA(()),
        ],
        compiler_params=params,
    )(came, packed_low, adapter_up, packed_inputs, cosine, sine)
    attn_rows, grad_rows = pl.pallas_call(
        finish_kernel,
        out_shape=(
            jax.ShapeDtypeStruct((token_count, query_columns), BF16),
            jax.ShapeDtypeStruct((token_count, qkv_width), BF16),
        ),
        compiler_params=params,
        cost_estimate=pl.CostEstimate(
            flops=token_count * qkv_width,
            bytes_accessed=8 * token_count * qkv_width,
            transcendentals=0,
        ),
    )(came, cosine, sine)
    total = jnp.sum(exchange(terms, "sub").astype(F32), axis=0)
    for axis, apart in (("half", 1), ("dp", 1), ("dp", 2), ("dp", 4)):
        size = lax.axis_size(axis)
        total = total + lax.ppermute(total, axis, [(i, i ^ apart) for i in range(size)])
    whole = exchange(jnp.broadcast_to(total.astype(BF16)[None], terms.shape), "sub")
    grad_a, grad_b = pl.pallas_call(
        unfold_kernel,
        out_shape=(
            jax.ShapeDtypeStruct((rank, model_width), F32),
            jax.ShapeDtypeStruct((rank, query_columns), F32),
        ),
        compiler_params=params,
    )(whole)
    return (attn_rows[None], grad_rows[None], grad_a.T, grad_b)


def solution(mesh):
    members, replicas = mesh.devices.shape
    split = Mesh(mesh.devices.reshape(2, members // 2, replicas), ("half", "sub", "dp"))
    rows = P("dp", ("half", "sub"), None)
    placed = (rows, rows, P(), P(), P("dp", None), P("dp", None), rows)
    return jax.shard_map(
        local,
        mesh=split,
        in_specs=placed,
        out_specs=(rows, rows, P(), P()),
        check_vma=False,
    )
```

```python
import math

import jax
import jax.numpy as jnp
from jax import lax
from jax.experimental import pallas as pl
from jax.experimental.pallas import tpu as pltpu
from jax.sharding import Mesh
from jax.sharding import PartitionSpec as P

HEAD_DIM = 128
HALF_DIM = HEAD_DIM // 2
PART = 256
BLOCK = 512
PAIR = 2 * HEAD_DIM
PIECE_IN = 2 * PAIR + HEAD_DIM
PIECE = 2 * PAIR + 2 * HEAD_DIM
rope_base = 500000.0
VMEM_BYTES = 48 * 1024 * 1024
ATTENTION_VMEM_BYTES = 64768 * 1024
HIDDEN = -1e30
CHUNKS = 4
F32 = jnp.float32
BF16 = jnp.bfloat16


def rope_tables(offsets):
    index_float = jnp.arange(HALF_DIM, dtype=F32)
    inverse = jnp.power(F32(rope_base), -index_float / HALF_DIM)
    angles = offsets.astype(F32)[:, None] * inverse[None, :]
    cosine, sine = jnp.cos(angles), jnp.sin(angles)
    return jnp.concatenate([cosine, cosine], axis=1), jnp.concatenate([-sine, sine], axis=1)


def rotated(table, cosine, sine):
    return table * cosine + pltpu.roll(table, HALF_DIM, 1) * sine


def widen_kernel(inputs_ref, down_ref, qkv_ref, out_ref, inputs, down, held, sems, moves):
    width = qkv_ref.shape[1]
    rank = down_ref.shape[0]

    def copies(source, target, span, use, first):
        size = span // CHUNKS
        return [
            pltpu.make_async_copy(
                source.at[:, part * size : (part + 1) * size],
                target.at[:, part * size : (part + 1) * size],
                use.at[first + part],
            )
            for part in range(CHUNKS)
        ]

    load_down = pltpu.make_async_copy(down_ref, down, sems.at[2 * CHUNKS])
    load_down.start()
    loads = copies(inputs_ref, inputs, inputs.shape[1], sems, 0)
    reads = copies(qkv_ref, held, width, sems, CHUNKS)
    writes = copies(held, out_ref, width, moves, 0)
    for load in loads + reads:
        load.start()
    low = jnp.zeros((inputs.shape[0], rank), F32)
    held[:, width:] = jnp.zeros((inputs.shape[0], HEAD_DIM), BF16)
    chunk = inputs.shape[1] // CHUNKS
    load_down.wait()
    for index, load in enumerate(loads):
        part = slice(index * chunk, (index + 1) * chunk)
        load.wait()
        low += lax.dot_general(
            inputs[:, part], down[:, part], (((1,), (1,)), ((), ())), preferred_element_type=F32
        )
        reads[index].wait()
        writes[index].start()
    held[:, width : width + rank] = low.astype(BF16)
    last = pltpu.make_async_copy(held.at[:, width:], out_ref.at[:, width:], moves.at[CHUNKS])
    last.start()
    for write in writes:
        write.wait()
    last.wait()


def prepare_kernel(qkv_ref, up_ref, cos_ref, sin_ref, grad_ref, valid_ref, out_ref):
    cosine = cos_ref[...]
    sine = sin_ref[...]
    kept = valid_ref[...] > 0
    rank, queries = up_ref.shape
    kv_width = (qkv_ref.shape[1] - HEAD_DIM - queries) // 2
    low_at = queries + 2 * kv_width
    low = qkv_ref[:, low_at : low_at + rank]
    pieces = out_ref.shape[0]
    for piece in range(pieces):
        columns = slice(piece * PAIR, (piece + 1) * PAIR)
        full = qkv_ref[:, columns].astype(F32) + jnp.dot(
            low, up_ref[:, columns], preferred_element_type=F32
        )
        for head in range(2):
            at = slice(head * HEAD_DIM, (head + 1) * HEAD_DIM)
            out_ref[piece, :, at] = rotated(full[:, at], cosine, sine).astype(BF16)
        grad = grad_ref[:, columns]
        out_ref[piece, :, PAIR : 2 * PAIR] = jnp.where(kept, grad, jnp.zeros_like(grad))
    for key_head in range(kv_width // HEAD_DIM):
        at = queries + key_head * HEAD_DIM
        keys = rotated(qkv_ref[:, at : at + HEAD_DIM].astype(F32), cosine, sine).astype(BF16)
        values = qkv_ref[:, at + kv_width : at + kv_width + HEAD_DIM]
        out_ref[2 * key_head, :, 2 * PAIR :] = keys
        out_ref[2 * key_head + 1, :, 2 * PAIR :] = values


def attention_kernel(
    start_ref,
    end_ref,
    side_ref,
    q_ref,
    g_ref,
    mine_ref,
    other_ref,
    out_ref,
    kv_ref,
    kt,
    vt,
    dkt,
    dvt,
    store0,
    store1,
    held,
    tail,
    sems,
):
    store = (store0, store1)
    step = pl.program_id(0)
    blocks = held.shape[0]
    factor = 1.0 / math.sqrt(HEAD_DIM)
    exponent = factor * math.log2(math.e)
    parts = BLOCK // PART

    def place(keys_ref, values_ref):
        for tile in range(blocks):
            rows = slice(tile * BLOCK, (tile + 1) * BLOCK)
            keys, values = keys_ref[rows], values_ref[rows]
            kv_ref[rows, :HEAD_DIM] = keys
            kv_ref[rows, HEAD_DIM:] = values
            kt[tile] = keys.T
            vt[tile] = values.T

    @pl.when((step == 0) & (side_ref[0] == 0))
    def _():
        place(mine_ref, other_ref)

    @pl.when((step == 0) & (side_ref[0] == 1))
    def _():
        place(other_ref, mine_ref)

    @pl.when(step == 0)
    def _():
        dkt[...] = jnp.zeros_like(dkt)
        dvt[...] = jnp.zeros_like(dvt)

    first = start_ref[step * parts] // BLOCK
    end_row = end_ref[step * parts]
    own = pl.multiple_of(step * BLOCK, BLOCK)
    column = lax.broadcasted_iota(jnp.int32, (1, BLOCK), 1)
    queries = [q_ref[:, h * HEAD_DIM : (h + 1) * HEAD_DIM] for h in range(2)]
    grads = [g_ref[:, h * HEAD_DIM : (h + 1) * HEAD_DIM] for h in range(2)]
    corners = [(slice(p * PART, (p + 1) * PART), (p + 1) * PART) for p in range(parts)]

    def folded(op, table):
        pieces = [table[:, c : c + HEAD_DIM] for c in range(0, table.shape[1], HEAD_DIM)]
        while len(pieces) > 1:
            pieces = [op(a, b) for a, b in zip(pieces[::2], pieces[1::2])]
        return pieces[0]

    def spread(table, width):
        return jnp.concatenate([table] * (width // HEAD_DIM), axis=1)

    def key_rows(tile):
        return pl.ds(pl.multiple_of(tile * BLOCK, BLOCK), BLOCK)

    def corner_allowed(p, width):
        low = start_ref[step * parts + p] - own
        high = end_ref[step * parts + p] - own
        row = lax.broadcasted_iota(jnp.int32, (PART, 1), 0) + p * PART
        at = column[:, :width]
        return (at == row) | ((at < row) & (at >= low) & (at < high))

    allowed = [corner_allowed(p, width) for p, (_, width) in enumerate(corners)]
    carry = []
    for h in range(2):
        highs, sums = [], []
        for p, (rows, width) in enumerate(corners):
            scores = jnp.dot(queries[h][rows], kt[step, :, :width], preferred_element_type=F32)
            scores = jnp.where(allowed[p], scores * exponent, HIDDEN)
            store[h][step, rows, :width] = scores
            highs.append(folded(jnp.maximum, scores))
            sums.append(folded(jnp.add, jnp.exp2(scores - spread(highs[-1], width))))
        carry += [jnp.concatenate(highs, axis=0), jnp.concatenate(sums, axis=0)]

    def score_pass(tile, carry):
        bias = jnp.where(tile * BLOCK + column < end_row, F32(0.0), F32(HIDDEN))
        result = []
        for h in range(2):
            top, total = carry[2 * h], carry[2 * h + 1]
            scores = jnp.dot(queries[h], kt[tile], preferred_element_type=F32) * exponent + bias
            store[h][tile] = scores
            higher = jnp.maximum(top, folded(jnp.maximum, scores))
            total = total * jnp.exp2(top - higher) + folded(
                jnp.add, jnp.exp2(scores - spread(higher, BLOCK))
            )
            result += [higher, total]
        return tuple(result)

    carry = lax.fori_loop(first, step, score_pass, tuple(carry))
    tops, inverse = [], []
    for h in range(2):
        lane_top, lane_total = carry[2 * h], carry[2 * h + 1]
        top = jnp.max(lane_top, axis=1, keepdims=True)
        total = jnp.sum(lane_total * jnp.exp2(lane_top - top), axis=1, keepdims=True)
        tops.append(top)
        inverse.append(1.0 / total)

    def corner_probs(h, rows, width):
        return jnp.exp2(store[h][step, rows, :width] - tops[h][rows]) * inverse[h][rows]

    def probs_of(h, tile):
        return jnp.exp2(store[h][tile] - tops[h]) * inverse[h]

    own_rows = key_rows(step)
    keys, values = kv_ref[own_rows, :HEAD_DIM], kv_ref[own_rows, HEAD_DIM:]
    sums = []
    for h in range(2):
        sums.append(
            jnp.concatenate(
                [
                    jnp.dot(
                        corner_probs(h, rows, width).astype(BF16),
                        values[:width],
                        preferred_element_type=F32,
                    )
                    for rows, width in corners
                ],
                axis=0,
            )
        )

    def out_pass(tile, carry):
        values = kv_ref[key_rows(tile), HEAD_DIM:]
        return tuple(
            carry[h]
            + jnp.dot(probs_of(h, tile).astype(BF16), values, preferred_element_type=F32)
            for h in range(2)
        )

    sums = lax.fori_loop(first, step, out_pass, tuple(sums))
    outs = [total.astype(BF16) for total in sums]
    deltas = [
        jnp.sum(grads[h].astype(F32) * outs[h].astype(F32), axis=1, keepdims=True) for h in range(2)
    ]
    queries_t = [table.T for table in queries]
    grads_t = [table.T for table in grads]

    query_sums = []
    for h in range(2):
        found = []
        for rows, width in corners:
            grad_probs = jnp.dot(grads[h][rows], vt[step, :, :width], preferred_element_type=F32)
            probs = corner_probs(h, rows, width)
            grad_scores = (probs * (grad_probs - deltas[h][rows])).astype(BF16)
            found.append(jnp.dot(grad_scores, keys[:width], preferred_element_type=F32))
            dkt[step, :, :width] += jnp.dot(
                queries_t[h][:, rows], grad_scores, preferred_element_type=F32
            )
            dvt[step, :, :width] += jnp.dot(
                grads_t[h][:, rows], probs.astype(BF16), preferred_element_type=F32
            )
        query_sums.append(jnp.concatenate(found, axis=0))

    def gradient_pass(tile, carry):
        keys = kv_ref[key_rows(tile), :HEAD_DIM]
        result = []
        for h in range(2):
            grad_probs = jnp.dot(grads[h], vt[tile], preferred_element_type=F32)
            probs = probs_of(h, tile)
            grad_scores = (probs * (grad_probs - deltas[h])).astype(BF16)
            result.append(carry[h] + jnp.dot(grad_scores, keys, preferred_element_type=F32))
            dkt[tile] += jnp.dot(queries_t[h], grad_scores, preferred_element_type=F32)
            dvt[tile] += jnp.dot(grads_t[h], probs.astype(BF16), preferred_element_type=F32)
        return tuple(result)

    query_sums = lax.fori_loop(first, step, gradient_pass, tuple(query_sums))
    for h in range(2):
        at = h * HEAD_DIM
        held[step, :, at : at + HEAD_DIM] = outs[h]
        held[step, :, PAIR + at : PAIR + at + HEAD_DIM] = (query_sums[h] * factor).astype(BF16)

    def block_copy(block):
        rows = pl.ds(pl.multiple_of(block * BLOCK, BLOCK), BLOCK)
        return pltpu.make_async_copy(held.at[block], out_ref.at[rows, : 2 * PAIR], sems.at[block])

    block_copy(step).start()

    @pl.when(step == blocks - 1)
    def _():
        for tile in range(blocks):
            rows = slice(tile * BLOCK, (tile + 1) * BLOCK)
            tail[rows, :HEAD_DIM] = (dkt[tile] * factor).astype(BF16).T
            tail[rows, HEAD_DIM:] = dvt[tile].astype(BF16).T
        last = pltpu.make_async_copy(tail, out_ref.at[:, 2 * PAIR :], sems.at[blocks])
        last.start()
        for block in range(blocks):
            block_copy(block).wait()
        last.wait()


def attention(table, other, starts, ends, side):
    rows, width = table.shape[0], PIECE
    blocks = rows // BLOCK
    tiles = blocks * (blocks + 1) // 2
    return pl.pallas_call(
        attention_kernel,
        out_shape=pltpu.HBM((rows, width), BF16),
        grid_spec=pltpu.PrefetchScalarGridSpec(
            num_scalar_prefetch=3,
            grid=(blocks,),
            in_specs=[
                pl.BlockSpec((BLOCK, PAIR), lambda i, *_: (i, 0)),
                pl.BlockSpec((BLOCK, PAIR), lambda i, *_: (i, 1)),
                pl.BlockSpec((rows, HEAD_DIM), lambda i, *_: (0, 2 * PAIR // HEAD_DIM)),
                pl.BlockSpec((rows, HEAD_DIM), lambda i, *_: (0, 0)),
            ],
            out_specs=pl.BlockSpec(memory_space=pl.ANY),
            scratch_shapes=[
                pltpu.VMEM((rows, PAIR), BF16),
                pltpu.VMEM((blocks, HEAD_DIM, BLOCK), BF16),
                pltpu.VMEM((blocks, HEAD_DIM, BLOCK), BF16),
                pltpu.VMEM((blocks, HEAD_DIM, BLOCK), F32),
                pltpu.VMEM((blocks, HEAD_DIM, BLOCK), F32),
                pltpu.VMEM((blocks, BLOCK, BLOCK), F32),
                pltpu.VMEM((blocks, BLOCK, BLOCK), F32),
                pltpu.VMEM((blocks, BLOCK, 2 * PAIR), BF16),
                pltpu.VMEM((rows, PAIR), BF16),
                pltpu.SemaphoreType.DMA((blocks + 1,)),
            ],
        ),
        compiler_params=pltpu.CompilerParams(vmem_limit_bytes=ATTENTION_VMEM_BYTES),
        cost_estimate=pl.CostEstimate(
            flops=tiles * 2 * 6 * 2 * BLOCK * BLOCK * HEAD_DIM,
            bytes_accessed=4 * rows * width,
            transcendentals=tiles * 2 * BLOCK * BLOCK,
        ),
    )(starts, ends, side, table, table, table, other)


def unrotated_pair(came_ref, piece, cosine, sine):
    heads = [
        rotated(came_ref[piece, :, at : at + HEAD_DIM].astype(F32), cosine, sine).astype(BF16)
        for at in (PAIR, PAIR + HEAD_DIM)
    ]
    return jnp.concatenate(heads, axis=1)


def query_kernel(
    came_ref, low_ref, up_ref, inputs_ref, cos_ref, sin_ref, term_ref, inputs, sem
):
    load = pltpu.make_async_copy(inputs_ref, inputs, sem)
    load.start()
    cosine = cos_ref[...]
    sine = -sin_ref[...]
    rank = up_ref.shape[0]
    low_t = low_ref[...].astype(F32).T.astype(BF16)
    dlow = jnp.zeros(low_ref.shape, F32)
    for piece in range(came_ref.shape[0]):
        columns = slice(piece * PAIR, (piece + 1) * PAIR)
        part = unrotated_pair(came_ref, piece, cosine, sine)
        dlow += lax.dot_general(
            part, up_ref[:, columns], (((1,), (1,)), ((), ())), preferred_element_type=F32
        )
        term_ref[piece, rank:] = jnp.dot(low_t, part, preferred_element_type=F32).astype(BF16)
    dlow_t = dlow.astype(BF16).astype(F32).T.astype(BF16)
    load.wait()
    for piece in range(came_ref.shape[0]):
        columns = slice(piece * PAIR, (piece + 1) * PAIR)
        term_ref[piece, :rank] = jnp.dot(
            dlow_t, inputs[:, columns], preferred_element_type=F32
        ).astype(BF16)


def finish_kernel(came_ref, cos_ref, sin_ref, out_ref, grad_ref):
    cosine = cos_ref[...]
    sine = -sin_ref[...]
    queries = out_ref.shape[1]
    kv_width = (grad_ref.shape[1] - queries) // 2
    for piece in range(came_ref.shape[0]):
        columns = slice(piece * PAIR, (piece + 1) * PAIR)
        out_ref[:, columns] = came_ref[piece, :, :PAIR]
        grad_ref[:, columns] = unrotated_pair(came_ref, piece, cosine, sine)
    for key_head in range(kv_width // HEAD_DIM):
        pair = (2 * key_head, 2 * key_head + 1)
        keys, values = (
            sum(came_ref[piece, :, at : at + HEAD_DIM].astype(F32) for piece in pair)
            for at in (2 * PAIR, 2 * PAIR + HEAD_DIM)
        )
        at = queries + key_head * HEAD_DIM
        grad_ref[:, at : at + HEAD_DIM] = rotated(keys, cosine, sine).astype(BF16)
        grad_ref[:, at + kv_width : at + kv_width + HEAD_DIM] = values.astype(BF16)


def repeat_kernel(total_ref, came_ref, out_ref):
    total = (total_ref[...] + came_ref[...]).astype(BF16)
    for piece in range(out_ref.shape[0]):
        out_ref[piece] = total


def unfold_kernel(whole_ref, first_ref, second_ref):
    rank = first_ref.shape[0]
    for piece in range(whole_ref.shape[0]):
        columns = slice(piece * PAIR, (piece + 1) * PAIR)
        first_ref[:, columns] = whole_ref[piece, :rank].astype(F32)
        second_ref[:, columns] = whole_ref[piece, rank:].astype(F32)


def in_hbm(table):
    return pltpu.with_memory_space_constraint(table, pltpu.HBM)


def exchange(table, axis):
    return lax.all_to_all(table, axis, split_axis=0, concat_axis=0, tiled=True)


def local(
    projection_rows, normed_input_rows, adapter_down, adapter_up, lengths, groups, output_gradient
):
    qkv_local = projection_rows[0]
    x_local = normed_input_rows[0]
    grad_raw = output_gradient[0]
    length_row = lengths[0]
    width_row = groups[0]
    token_count, model_width = x_local.shape
    qkv_width = qkv_local.shape[1]
    rank, query_columns = adapter_up.shape
    members = lax.axis_size("sub")
    half_index = lax.axis_index("half")
    group_index = half_index * members + lax.axis_index("sub")
    in_vmem = pl.BlockSpec(memory_space=pltpu.VMEM)
    in_place = pl.BlockSpec(memory_space=pl.ANY)
    wide = pl.pallas_call(
        widen_kernel,
        out_shape=pltpu.HBM((token_count, qkv_width + HEAD_DIM), BF16),
        in_specs=[in_place, in_place, in_place],
        out_specs=in_place,
        scratch_shapes=[
            pltpu.VMEM((token_count, model_width), BF16),
            pltpu.VMEM((rank, model_width), BF16),
            pltpu.VMEM((token_count, qkv_width + HEAD_DIM), BF16),
            pltpu.SemaphoreType.DMA((2 * CHUNKS + 1,)),
            pltpu.SemaphoreType.DMA((CHUNKS + 1,)),
        ],
        compiler_params=pltpu.CompilerParams(vmem_limit_bytes=VMEM_BYTES),
    )(in_hbm(x_local), in_hbm(adapter_down.T), in_hbm(qkv_local))
    packed_qkv = exchange(wide, "dp")
    packed_low = packed_qkv[:, qkv_width : qkv_width + rank]

    ends_dev = jnp.cumsum(width_row)
    starts_dev = ends_dev - width_row

    def owner_of(device):
        picked = (device[:, None] >= starts_dev[None, :]) & (device[:, None] < ends_dev[None, :])
        start = jnp.sum(jnp.where(picked, starts_dev[None, :], 0), axis=1)
        length = jnp.sum(jnp.where(picked, length_row[None, :], 0), axis=1)
        return start, length

    start_me, length_me = owner_of(group_index[None])
    row_at = jnp.arange(token_count, dtype=jnp.int32)
    local_offsets = (group_index - start_me) * token_count + row_at
    row_valid = (local_offsets < length_me).astype(jnp.int32)[:, None]
    cosine, sine = rope_tables(local_offsets)
    per_block = PART // token_count
    block_device = half_index * members + per_block * jnp.arange(
        members // per_block, dtype=jnp.int32
    )
    block_start, block_length = owner_of(block_device)
    first_rows = (block_start - half_index * members) * token_count
    starts = first_rows
    ends = first_rows + block_length

    params = pltpu.CompilerParams(vmem_limit_bytes=VMEM_BYTES)
    pieces = pl.pallas_call(
        prepare_kernel,
        out_shape=jax.ShapeDtypeStruct((members, token_count, PIECE_IN), BF16),
        compiler_params=params,
    )(packed_qkv, adapter_up, cosine, sine, grad_raw, row_valid)
    table = exchange(pieces, "sub").reshape(members * token_count, PIECE_IN)
    mine, x_held = lax.optimization_barrier((table[:, 2 * PAIR :], x_local))
    packed_inputs = in_hbm(exchange(x_held, "dp"))
    other = lax.ppermute(mine, "sub", [(i, i ^ 1) for i in range(members)])
    side = lax.axis_index("sub").astype(jnp.int32).reshape(1) % 2
    results = attention(in_hbm(table), other, starts, ends, side)
    came = exchange(results.reshape(members, token_count, PIECE), "sub")
    terms = pl.pallas_call(
        query_kernel,
        out_shape=jax.ShapeDtypeStruct((members, 2 * rank, PAIR), BF16),
        in_specs=[in_vmem, in_vmem, in_vmem, in_place, in_vmem, in_vmem],
        scratch_shapes=[
            pltpu.VMEM((token_count, model_width), BF16),
            pltpu.SemaphoreType.DMA(()),
        ],
        compiler_params=params,
    )(came, packed_low, adapter_up, packed_inputs, cosine, sine)
    attn_rows, grad_rows = pl.pallas_call(
        finish_kernel,
        out_shape=(
            jax.ShapeDtypeStruct((token_count, query_columns), BF16),
            jax.ShapeDtypeStruct((token_count, qkv_width), BF16),
        ),
        compiler_params=params,
        cost_estimate=pl.CostEstimate(
            flops=token_count * qkv_width,
            bytes_accessed=8 * token_count * qkv_width,
            transcendentals=0,
        ),
    )(came, cosine, sine)
    total = jnp.sum(exchange(terms, "sub").astype(F32), axis=0)
    came_total = jnp.zeros_like(total)
    for axis, apart in (("half", 1), ("dp", 1), ("dp", 2), ("dp", 4)):
        total = total + came_total
        size = lax.axis_size(axis)
        came_total = lax.ppermute(total, axis, [(i, i ^ apart) for i in range(size)])
    copies = pl.pallas_call(
        repeat_kernel,
        out_shape=jax.ShapeDtypeStruct(terms.shape, BF16),
        compiler_params=params,
    )(total, came_total)
    whole = exchange(copies, "sub")
    grad_a, grad_b = pl.pallas_call(
        unfold_kernel,
        out_shape=(
            jax.ShapeDtypeStruct((rank, model_width), F32),
            jax.ShapeDtypeStruct((rank, query_columns), F32),
        ),
        compiler_params=params,
    )(whole)
    return (attn_rows[None], grad_rows[None], grad_a.T, grad_b)


def solution(mesh):
    members, replicas = mesh.devices.shape
    split = Mesh(mesh.devices.reshape(2, members // 2, replicas), ("half", "sub", "dp"))
    rows = P("dp", ("half", "sub"), None)
    placed = (rows, rows, P(), P(), P("dp", None), P("dp", None), rows)
    return jax.shard_map(
        local,
        mesh=split,
        in_specs=placed,
        out_specs=(rows, rows, P(), P()),
        check_vma=False,
    )
```
